32 devices in a mesh: gx: 8 (over z, x), gy: 4 (over y, core).
Axes of the slice: x: 2, y: 2, z: 4, core: 2. Of those that a mesh axis runs over, the one named last changes fastest.
Arguments:
- features: bfloat16 [96, 4096], P(None, ('gx', 'gy')), may hold values from -6 to 6
- kernel_map: int32 [27, 4096], P(None, ('gx', 'gy')), may hold values from 0 to 256
- send_rows: int32 [8, 512], P(None, ('gx', 'gy')), may hold values from 0 to 127
- counts: int32 [32], P(('gx', 'gy')), may hold values from 32 to 128, as said below
- weight_one: bfloat16 [27, 96, 96], replicated, may hold values from -0.15625 to 0.15625
- weight_two: bfloat16 [27, 96, 96], replicated, may hold values from -0.15625 to 0.15625
- first_norm_scale: float32 [96], replicated, may hold values from 0.5 to 1.5
- first_norm_bias: float32 [96], replicated, may hold values from -3 to 3
- second_norm_scale: float32 [96], replicated, may hold values from 0.5 to 1.5
- second_norm_bias: float32 [96], replicated, may hold values from -3 to 3
- cotangent: bfloat16 [96, 4096], P(None, ('gx', 'gy')), may hold values from -6 to 6
Outputs:
- output: bfloat16 [96, 4096], P(None, ('gx', 'gy'))
- grad_features: bfloat16 [96, 4096], P(None, ('gx', 'gy'))
- grad_weight_one: float32 [27, 96, 96], replicated
- grad_weight_two: float32 [27, 96, 96], replicated
- grad_norms: float32 [4, 96], replicated
The draws below stay inside these ranges and needn't reach their ends.
Inputs may be any that keep to these rules, and one draw needn't show every extreme that they name: `counts`: counts rise along the device order; the first device uses 128 // 4 rows and the last device of the grid uses all 128 rows.
All inputs are finite; a program needn't handle non-finite values.
Results may differ from the reference program's by a relative error of at most 0.0075.
Values may be sent and summed in bfloat16 or wider, within the bound.
No kernel may reach another device: no remote copies, remote signals or barrier semaphores. Data moves between devices by JAX's collectives and lax.ppermute only.
A program may use at most 64 MiB of HBM per device.

```python
import jax
import jax.numpy as jnp
from jax import lax

CHANNELS = 96
OFFSETS = 27
ROWS = 128
BLOCK = 16
GRID = 32
N_GX = 8
N_GY = 4


def device_parity():
    ranks = jnp.arange(ROWS * GRID, dtype=jnp.int32) // ROWS
    return ((ranks // N_GY + ranks % N_GY) % 2).astype(jnp.int32)


def draw_features(key, part):
    key = jax.random.fold_in(key, 29)
    parity = device_parity()
    shape = (CHANNELS, ROWS * GRID)
    level = jnp.where(parity == 0, 0.5, 2.0).astype(jnp.float32)
    noise = jax.random.normal(key, shape, jnp.float32)
    values = jnp.clip(noise * level[None, :], -6.0, 6.0)
    return values.astype(jnp.bfloat16)


def draw_counts(key, part):
    ranks = jnp.arange(GRID, dtype=jnp.int32)
    base = ROWS // 3 + ranks * (ROWS - ROWS // 3) // (GRID - 1)
    jitter = jax.random.randint(key, (GRID,), -(ROWS // 16), ROWS // 16 + 1, dtype=jnp.int32)
    values = jnp.clip(base + jitter, ROWS // 4, ROWS).astype(jnp.int32)
    values = values.at[0].set(ROWS // 4)
    return values.at[GRID - 1].set(ROWS)


def draw_kernel_map(key, part):
    shape = (OFFSETS, ROWS * GRID)
    keys = jax.random.split(jax.random.fold_in(key, 71), 6)
    parity = device_parity()[None, :]
    local_cut = jnp.where(parity == 0, 48, 79).astype(jnp.int32)
    edge_cut = jnp.where(parity == 0, 88, 91).astype(jnp.int32)
    kind = jax.random.randint(keys[0], shape, 0, 100, dtype=jnp.int32)
    local = jax.random.randint(keys[1], shape, 0, ROWS, dtype=jnp.int32)
    edge_block = jax.random.randint(keys[2], shape, 0, 4, dtype=jnp.int32)
    edge_row = jax.random.randint(keys[3], shape, 0, BLOCK, dtype=jnp.int32)
    edge = ROWS + edge_block * BLOCK + edge_row
    diag_rows = max(1, BLOCK // 4)
    diag_block = jax.random.randint(keys[4], shape, 4, 8, dtype=jnp.int32)
    diag_row = jax.random.randint(keys[5], shape, 0, diag_rows, dtype=jnp.int32)
    diag = ROWS + diag_block * BLOCK + diag_row
    empty = jnp.full(shape, ROWS + 8 * BLOCK, dtype=jnp.int32)
    values = jnp.where(kind < local_cut, local, jnp.where(kind < edge_cut, edge, jnp.where(kind < 94, diag, empty)))
    return values.astype(jnp.int32)


def touch_ends(values, rng, least, high):
    place = [jax.random.randint(jax.random.fold_in(rng, axis), (), 0, length) for axis, length in enumerate(values.shape)]
    main_axis = values.shape.index(max(values.shape))
    beside = place[:main_axis] + [(place[main_axis] + 1) % values.shape[main_axis]] + place[main_axis + 1:]
    return values.at[tuple(place)].set(least).at[tuple(beside)].set(high)


def levels(own_key, dims, shards, low, top_value):
    def one(dim, blocks):
        steps = jax.random.uniform(jax.random.fold_in(jax.random.fold_in(own_key, 6), dim), (blocks,), jnp.float32, low / len(shards), top_value / len(shards))
        return jnp.repeat(jnp.exp(steps), dims[dim] // blocks).reshape((-1,) + (1,) * (len(dims) - dim - 1))

    loudness = one(*shards[0])
    for cut in shards[1:]:
        loudness = loudness * one(*cut)
    return loudness


def normal_values(key, extent, width, reach, shards=(), kind=jnp.bfloat16):
    drawn = jax.random.normal(key, extent, jnp.float32) * width
    if len(shards) > 0:
        drawn = levels(key, extent, shards, -0.22, 0.18) * drawn
    return jnp.clip(drawn, min=-reach, max=reach).astype(kind)


def setup_inputs(seed: int = 0) -> dict:
    arg_keys = jax.random.split(jax.random.key(seed), 12)
    return {
        "features": draw_features(jax.random.fold_in(arg_keys[11], 71), 0),
        "kernel_map": draw_kernel_map(jax.random.fold_in(arg_keys[11], 71), 0),
        "send_rows": touch_ends(jax.random.randint(arg_keys[2], (8, BLOCK * GRID), 0, ROWS), jax.random.fold_in(arg_keys[2], 1), 0, ROWS - 1).astype(jnp.int32),
        "counts": draw_counts(jax.random.fold_in(arg_keys[11], 71), 0),
        "weight_one": normal_values(arg_keys[4], (OFFSETS, CHANNELS, CHANNELS), (OFFSETS * CHANNELS // 2) ** -0.5, 0.15625),
        "weight_two": normal_values(arg_keys[5], (OFFSETS, CHANNELS, CHANNELS), (OFFSETS * CHANNELS // 2) ** -0.5, 0.15625),
        "first_norm_scale": jnp.clip(1.0 + 0.1 * jax.random.normal(arg_keys[6], (CHANNELS,), jnp.float32), 0.5, 1.5),
        "first_norm_bias": normal_values(arg_keys[7], (CHANNELS,), 0.5, 3.0, (), jnp.float32),
        "second_norm_scale": jnp.clip(1.0 + 0.1 * jax.random.normal(arg_keys[8], (CHANNELS,), jnp.float32), 0.5, 1.5),
        "second_norm_bias": normal_values(arg_keys[9], (CHANNELS,), 0.5, 3.0, (), jnp.float32),
        "cotangent": normal_values(arg_keys[10], (CHANNELS, ROWS * GRID), 1.0, 6.0, ((1, 32),)),
    }


EPS = 1e-05
STEP_LIST = ((1, 0), (-1, 0), (0, 1), (0, -1), (1, 1), (1, -1), (-1, 1), (-1, -1))

def silu_value(values):
    return values * jax.nn.sigmoid(values)

def silu_slope(values):
    sigma = jax.nn.sigmoid(values)
    return sigma * (1.0 + values * (1.0 - sigma))

def grid_shift(array, step_x, step_y):
    result = array
    for axis_id, amount in ((1, step_x), (2, step_y)):
        if amount != 0:
            length = result.shape[axis_id]
            zero_part = jnp.zeros_like(lax.slice_in_dim(result, 0, 1, axis=axis_id))
            if amount > 0:
                result = jnp.concatenate([zero_part, lax.slice_in_dim(result, 0, length - 1, axis=axis_id)], axis=axis_id)
            else:
                result = jnp.concatenate([lax.slice_in_dim(result, 1, length, axis=axis_id), zero_part], axis=axis_id)
    return result

def send_index(send_grid):
    offsets = (jnp.arange(GRID, dtype=jnp.int32) * ROWS)[None, :, None]
    return (send_grid + offsets).astype(jnp.int32)

def extend(values, send_grid):
    channels = values.shape[0]
    flat = values.reshape(channels, GRID * ROWS)
    index = send_index(send_grid)
    parts = [values]
    for slot_id in range(8):
        block = jnp.take(flat, index[slot_id].reshape(-1), axis=1).reshape(channels, N_GX, N_GY, BLOCK)
        moved = grid_shift(block, STEP_LIST[slot_id][0], STEP_LIST[slot_id][1])
        parts.append(moved.reshape(channels, GRID, BLOCK))
    parts.append(jnp.zeros((channels, GRID, 1), values.dtype))
    return jnp.concatenate(parts, axis=2)

def map_index(map_grid):
    table_len = ROWS + 8 * BLOCK + 1
    offsets = (jnp.arange(GRID, dtype=jnp.int32) * table_len)[None, :, None]
    return (map_grid + offsets).astype(jnp.int32)

def convolve(extended, weights, map_grid):
    channels = extended.shape[0]
    flat = extended.reshape(channels, -1)
    index = map_index(map_grid).reshape(OFFSETS, -1)

    def one_offset(total, pair):
        weight_here, index_here = pair
        gathered = jnp.take(flat, index_here, axis=1).astype(jnp.float32)
        product = jnp.dot(weight_here.astype(jnp.float32).T, gathered, precision=lax.Precision.HIGHEST)
        return (total + product, None)
    total, _ = lax.scan(one_offset, jnp.zeros((channels, GRID * ROWS), jnp.float32), (weights, index))
    return total.reshape(channels, GRID, ROWS)

def weight_grad(extended, grad_rows, map_grid):
    channels = extended.shape[0]
    flat = extended.reshape(channels, -1)
    index = map_index(map_grid).reshape(OFFSETS, -1)
    grad_flat = grad_rows.reshape(channels, -1).astype(jnp.float32)

    def one_offset(index_here):
        gathered = jnp.take(flat, index_here, axis=1).astype(jnp.float32)
        return jnp.dot(gathered, grad_flat.T, precision=lax.Precision.HIGHEST)
    return lax.map(one_offset, index)

def spread_back(grad_rows, weights, map_grid, send_grid):
    channels = grad_rows.shape[0]
    table_len = ROWS + 8 * BLOCK + 1
    index = map_index(map_grid).reshape(OFFSETS, -1)
    grad_flat = grad_rows.reshape(channels, -1).astype(jnp.float32)

    def one_offset(table, pair):
        weight_here, index_here = pair
        contrib = jnp.dot(weight_here.astype(jnp.float32), grad_flat, precision=lax.Precision.HIGHEST)
        return (table.at[:, index_here].add(contrib), None)
    table, _ = lax.scan(one_offset, jnp.zeros((channels, GRID * table_len), jnp.float32), (weights, index))
    table = table.reshape(channels, GRID, table_len)
    local = table[:, :, :ROWS].reshape(channels, GRID * ROWS)
    sends = send_index(send_grid)
    for slot_id in range(8):
        block = table[:, :, ROWS + slot_id * BLOCK:ROWS + (slot_id + 1) * BLOCK].astype(jnp.bfloat16)
        block = block.reshape(channels, N_GX, N_GY, BLOCK)
        moved = grid_shift(block, -STEP_LIST[slot_id][0], -STEP_LIST[slot_id][1]).astype(jnp.float32)
        local = local.at[:, sends[slot_id].reshape(-1)].add(moved.reshape(channels, -1))
    return local.reshape(channels, GRID, ROWS)

def apply_batch_norm(pre_norm, active_mask, row_total):
    masked = pre_norm * active_mask
    mean = lax.optimization_barrier(jnp.sum(masked, axis=(1, 2))) / row_total
    var = lax.optimization_barrier(jnp.sum(masked * pre_norm, axis=(1, 2))) / row_total - mean * mean
    inverse_deviation = lax.rsqrt(var + EPS)
    return ((pre_norm - mean[:, None, None]) * inverse_deviation[:, None, None], inverse_deviation)

def norm_backward_step(linear_gradient, normalized_input, inverse_deviation, norm_scale, active_mask, row_total):
    scale_gradient = lax.optimization_barrier(jnp.sum(linear_gradient * normalized_input * active_mask, axis=(1, 2)))
    bias_gradient = lax.optimization_barrier(jnp.sum(linear_gradient, axis=(1, 2)))
    prenorm_gradient = (norm_scale * inverse_deviation)[:, None, None] * (linear_gradient - (bias_gradient[:, None, None] + normalized_input * scale_gradient[:, None, None]) / row_total) * active_mask
    return (prenorm_gradient.astype(jnp.bfloat16), scale_gradient, bias_gradient)

def reference(features, kernel_map, send_rows, counts, weight_one, weight_two, first_norm_scale, first_norm_bias, second_norm_scale, second_norm_bias, cotangent):
    channels = features.shape[0]
    map_grid = kernel_map.reshape(OFFSETS, GRID, ROWS)
    send_grid = send_rows.reshape(8, GRID, BLOCK)
    active_mask = (jnp.arange(ROWS, dtype=jnp.int32)[None, :] < counts[:, None]).astype(jnp.float32)
    row_total = jnp.sum(counts).astype(jnp.float32)
    begin_offset = (features.reshape(channels, GRID, ROWS).astype(jnp.float32) * active_mask).astype(jnp.bfloat16)
    ext_zero = extend(begin_offset, send_grid)
    first_hidden = convolve(ext_zero, weight_one, map_grid)
    first_normalized, first_inverse_deviation = apply_batch_norm(first_hidden, active_mask, row_total)
    first_linear = first_norm_scale[:, None, None] * first_normalized + first_norm_bias[:, None, None]
    act_one = (silu_value(first_linear) * active_mask).astype(jnp.bfloat16)
    ext_one = extend(act_one, send_grid)
    second_hidden = convolve(ext_one, weight_two, map_grid)
    second_normalized, second_inverse_deviation = apply_batch_norm(second_hidden, active_mask, row_total)
    accumulated_sum = second_norm_scale[:, None, None] * second_normalized + second_norm_bias[:, None, None] + begin_offset.astype(jnp.float32)
    output = (silu_value(accumulated_sum) * active_mask).astype(jnp.bfloat16)
    gradient_total = cotangent.reshape(channels, GRID, ROWS).astype(jnp.float32) * active_mask * silu_slope(accumulated_sum)
    second_gradient, second_scale_gradient, second_bias_gradient = norm_backward_step(gradient_total, second_normalized, second_inverse_deviation, second_norm_scale, active_mask, row_total)
    grad_weight_two = weight_grad(ext_one, second_gradient, map_grid)
    linear_gradient = spread_back(second_gradient, weight_two, map_grid, send_grid) * active_mask * silu_slope(first_linear)
    first_gradient, first_scale_gradient, first_bias_gradient = norm_backward_step(linear_gradient, first_normalized, first_inverse_deviation, first_norm_scale, active_mask, row_total)
    grad_weight_one = weight_grad(ext_zero, first_gradient, map_grid)
    grad_features = ((spread_back(first_gradient, weight_one, map_grid, send_grid) + gradient_total) * active_mask).astype(jnp.bfloat16)
    grad_norms = jnp.stack([first_scale_gradient, first_bias_gradient, second_scale_gradient, second_bias_gradient])
    return (output.reshape(channels, GRID * ROWS), grad_features.reshape(channels, GRID * ROWS), grad_weight_one, grad_weight_two, grad_norms)
```

```python
import functools

import jax
import jax.numpy as jnp
from jax import lax
from jax.experimental import pallas as pl
from jax.experimental.pallas import tpu as pltpu
from jax.sharding import PartitionSpec as P

EPS = 1e-05
STEP_LIST = ((1, 0), (-1, 0), (0, 1), (0, -1), (1, 1), (1, -1), (-1, 1), (-1, -1))
AXES = ("gx", "gy")
LANES = 128
F32 = jnp.float32
BF16 = jnp.bfloat16


def nn(a, b):
    return lax.dot_general(a, b, (((1,), (0,)), ((), ())), preferred_element_type=F32)


def nt(a, b):
    return lax.dot_general(a, b, (((1,), (1,)), ((), ())), preferred_element_type=F32)


def iota(shape, dim):
    return lax.broadcasted_iota(jnp.int32, shape, dim)


def eye(size):
    return jnp.where(iota((size, size), 0) == iota((size, size), 1), 1.0, 0.0).astype(BF16)


def sigmoid(v):
    return 1.0 / (1.0 + jnp.exp(-v))


def neighbour(place, grid, step):
    i, j = place[0] + step[0], place[1] + step[1]
    inside = (i >= 0) & (i < grid[0]) & (j >= 0) & (j < grid[1])
    return jnp.where(inside, i * grid[1] + j, place[0] * grid[1] + place[1]), inside


def here():
    return lax.axis_index("gx"), lax.axis_index("gy")


def put_blocks(buf_ref, rows, grid, sign, width, base=None):
    place = here()
    for n, (a, b) in enumerate(STEP_LIST):
        dest, _ = neighbour(place, grid, (sign * a, sign * b))
        block = rows[n * width : (n + 1) * width]
        if base is not None:
            block = jnp.where(iota(block.shape, 1) < 96, block, base)
        buf_ref[dest, 0:width, :] = block.astype(BF16)


def take_blocks(buf_ref, grid, sign, width):
    place = here()
    blocks = []
    for a, b in STEP_LIST:
        src, inside = neighbour(place, grid, (sign * a, sign * b))
        block = buf_ref[src, 0:width, :].astype(F32)
        blocks.append(jnp.where(inside, block, 0.0))
    return jnp.concatenate(blocks, axis=0)


def pad_to(x, rows, lanes):
    if x.shape[1] < lanes:
        x = jnp.concatenate([x, jnp.zeros((x.shape[0], lanes - x.shape[1]), x.dtype)], axis=1)
    if x.shape[0] < rows:
        x = jnp.concatenate([x, jnp.zeros((rows - x.shape[0], lanes), x.dtype)], axis=0)
    return x


def cols_to_rows(cols):
    lane = iota((cols[0].shape[0], LANES), 1)
    total = jnp.zeros((cols[0].shape[0], LANES), F32)
    for at, col in enumerate(cols):
        total = jnp.where(lane == at, col, total)
    return pad_to(total, LANES, LANES).T


def rows_to_cols(rows):
    sub = iota((LANES, LANES), 0)
    total = jnp.zeros((LANES, LANES), F32)
    for at, row in enumerate(rows):
        total = jnp.where(sub == at, row, total)
    total = total.T
    return [total[:, at : at + 1] for at in range(len(rows))]


def split3(x):
    high = x.astype(BF16).astype(F32)
    mid = (x - high).astype(BF16).astype(F32)
    low = (x - high - mid).astype(BF16).astype(F32)
    return [high, mid, low]


def pack_rows(pieces, last):
    sub = iota((16, LANES), 0)
    lane = iota((16, LANES), 1)
    total = jnp.zeros((16, LANES), F32)
    for q, piece in enumerate(pieces):
        total = jnp.where(sub // 3 == q, piece, total)
    part = sub % 3
    moved = jnp.where(
        part == 0,
        pltpu.roll(total, 96, 1),
        jnp.where(part == 1, pltpu.roll(total, 64, 1), pltpu.roll(total, 32, 1)),
    )
    moved = jnp.where(sub == 15, last, moved)
    return jnp.where(lane >= 96, moved, 0.0)


def unpack_rows(tiles, groups):
    devices = tiles.shape[0]
    flat = tiles.reshape(devices * 16, LANES)
    sub = iota(tiles.shape, 1)
    lane = iota(tiles.shape, 2)
    part = sub % 3
    moved = [pltpu.roll(flat, 32 * (p + 1), 1).reshape(tiles.shape) for p in range(3)]
    value = jnp.where(part == 0, moved[0], jnp.where(part == 1, moved[1], moved[2]))
    value = jnp.where((lane // 32 == part) & (sub < 15), value, 0.0)
    results = []
    for low, high in groups:
        mask = (sub >= 3 * low) & (sub < 3 * high)
        results.append(jnp.sum(jnp.where(mask, value, 0.0), axis=1))
    return results


def valid_lanes(counts_ref, rows=1):
    return (iota((rows, LANES), 1) < counts_ref[0]).astype(F32)


def open_kernel(grid, counts_ref, features_ref, send_ref, buf_ref, start_ref, pick_ref, place_ref):
    width = send_ref.shape[1]
    send = send_ref[...].astype(F32).astype(BF16)
    spread = jnp.where(iota((width, LANES), 1) % width == iota((width, LANES), 0), 1.0, 0.0).astype(BF16)
    wide = nn(send, spread)
    wide = jnp.where(iota(wide.shape, 1) // width == iota(wide.shape, 0), wide, 0.0)
    row = jnp.sum(wide, axis=0, keepdims=True)
    pick = jnp.where(row == iota((LANES, LANES), 0).astype(F32), 1.0, 0.0)
    pick_ref[...] = pick.astype(BF16)
    place = pick.T.astype(BF16)
    place_ref[...] = place
    valid = valid_lanes(counts_ref)
    start = features_ref[...].astype(F32) * valid
    start_ref[...] = start.astype(BF16)
    extra = jnp.where(iota((LANES - 96, LANES), 0) == 0, valid, 0.0)
    rows = nt(place, jnp.concatenate([start, extra], axis=0).astype(BF16))
    put_blocks(buf_ref, rows, grid, 1, width)


def prepare_kernel(map_ref, one_ref, two_ref, hot_ref, one_t_ref, two_t_ref):
    table = hot_ref.shape[0]
    sub = iota((table, LANES), 0)
    for k in range(map_ref.shape[0]):
        hot_ref[:, k * LANES : (k + 1) * LANES] = jnp.where(
            sub == map_ref[k : k + 1, :], 1.0, 0.0
        ).astype(BF16)
    unit = eye(one_ref.shape[1])
    one_t_ref[...] = nt(unit, one_ref[...]).astype(BF16)
    two_t_ref[...] = nt(unit, two_ref[...]).astype(BF16)


def gather_convolve(table, hot_ref, weight_t_ref, taken_ref):
    channels = table.shape[0]
    taken = nn(table, hot_ref[...]).astype(BF16)
    offsets = hot_ref.shape[1] // LANES
    for k in range(offsets):
        taken_ref[k * channels : (k + 1) * channels, :] = taken[:, k * LANES : (k + 1) * LANES]
    return nn(weight_t_ref[...], taken_ref[...])


def first_kernel(
    grid, counts_ref, buf_ref, start_ref, hot_ref, weight_ref, place_ref,
    out_buf_ref, hidden_ref, taken_ref, flag_ref,
):
    width = buf_ref.shape[1]
    channels = start_ref.shape[0]
    halo_rows = take_blocks(buf_ref, grid, -1, width).astype(BF16)
    flag_ref[...] = jnp.broadcast_to(halo_rows[:, 96:97].astype(F32), (LANES, LANES))
    halo = nt(eye(LANES), halo_rows)[:channels].astype(BF16)
    table = jnp.concatenate([start_ref[...], halo], axis=1)
    hidden = gather_convolve(table, hot_ref, weight_ref, taken_ref)
    hidden_ref[...] = hidden
    valid = valid_lanes(counts_ref)
    count = counts_ref[0].astype(F32)
    sums = jnp.sum(hidden * valid, axis=1, keepdims=True)
    centred = (hidden - sums / count) * valid
    spread = jnp.sum(centred * centred, axis=1, keepdims=True)
    stat = cols_to_rows([sums, spread])
    base = pack_rows(split3(stat[0:1]) + split3(stat[1:2])[:2], count)
    out_buf_ref[...] = jnp.broadcast_to(base.astype(BF16)[None], out_buf_ref.shape)
    rows = pad_to(nt(place_ref[...], centred.astype(BF16)), LANES, LANES)
    put_blocks(out_buf_ref, rows, grid, 1, width, base)


def second_kernel(
    grid, counts_ref, buf_ref, hidden_ref, flag_ref, scale_ref, bias_ref, hot_ref, weight_ref,
    out_buf_ref, hidden_two_ref, taken_ref, norm_ref, slope_ref, halo_slope_ref, halo_cross_ref,
    const_ref, mean_ref,
):
    width = buf_ref.shape[1]
    channels = hidden_ref.shape[0]
    tiles = buf_ref[...].astype(F32)
    sums, spreads = unpack_rows(tiles, ((0, 3), (3, 5)))
    counts = tiles[:, 15, 96:97]
    total = jnp.sum(counts, axis=0, keepdims=True)
    means = sums / counts
    mean_ref[...] = means
    mean = jnp.sum(sums, axis=0, keepdims=True) / total
    apart = means - mean
    var = jnp.sum(spreads + counts * apart * apart, axis=0, keepdims=True) / total
    rstd = lax.rsqrt(var + EPS)
    scale = pad_to(scale_ref[...], 1, LANES)
    bias = pad_to(bias_ref[...], 1, LANES)
    total_row = jnp.broadcast_to(total, (1, LANES))
    mean_c, rstd_c, scale_c, bias_c = [c[:channels] for c in rows_to_cols([mean, rstd, scale, bias])]
    sub = iota((8, LANES), 0)
    const_ref[...] = jnp.where(sub == 0, scale * rstd, jnp.where(sub == 1, total_row, 0.0))

    valid = valid_lanes(counts_ref)
    normal = (hidden_ref[...] - mean_c) * rstd_c
    norm_ref[...] = normal
    linear = scale_c * normal + bias_c
    sig = sigmoid(linear)
    slope_ref[...] = sig * (1.0 + linear * (1.0 - sig)) * valid
    act = (linear * sig * valid).astype(BF16)

    place = here()
    lifted = []
    for n, (a, b) in enumerate(STEP_LIST):
        src, inside = neighbour(place, grid, (-a, -b))
        block = buf_ref[src, 0:width, :].astype(F32) + mean_ref[pl.ds(src, 1), :]
        lifted.append(jnp.where(inside, block, 0.0))
    lane = iota((LANES, LANES), 1)
    halo = jnp.where(lane < channels, jnp.concatenate(lifted, axis=0), 0.0)
    flag = flag_ref[...]
    halo_normal = (halo - mean) * rstd
    halo_linear = scale * halo_normal + bias
    halo_sig = sigmoid(halo_linear)
    halo_slope = halo_sig * (1.0 + halo_linear * (1.0 - halo_sig)) * flag
    halo_slope_ref[...] = halo_slope
    halo_cross_ref[...] = halo_slope * halo_normal
    halo_act = nt(eye(LANES), (halo_linear * halo_sig * flag).astype(BF16))[:channels].astype(BF16)

    hidden = gather_convolve(jnp.concatenate([act, halo_act], axis=1), hot_ref, weight_ref, taken_ref)
    hidden_two_ref[...] = hidden
    count = counts_ref[0].astype(F32)
    sums_two = jnp.sum(hidden * valid, axis=1, keepdims=True)
    centred = (hidden - sums_two / count) * valid
    spread_two = jnp.sum(centred * centred, axis=1, keepdims=True)
    stat = cols_to_rows([sums_two, spread_two])[0:2]
    stat = jnp.where(iota((2, LANES), 1) < 96, stat, count)
    out_buf_ref[...] = jnp.broadcast_to(stat[None], out_buf_ref.shape)


def third_kernel(
    counts_ref, buf_ref, hidden_ref, start_ref, cotangent_ref, scale_ref, bias_ref,
    out_buf_ref, output_ref, norm_ref, grad_ref, const_ref,
):
    channels = hidden_ref.shape[0]
    sums = buf_ref[:, 0, :]
    spreads = buf_ref[:, 1, :]
    counts = sums[:, 96:97]
    total = jnp.sum(counts, axis=0, keepdims=True)
    mean = jnp.sum(sums, axis=0, keepdims=True) / total
    apart = sums / counts - mean
    var = jnp.sum(spreads + counts * apart * apart, axis=0, keepdims=True) / total
    rstd = lax.rsqrt(var + EPS)
    scale = pad_to(scale_ref[...], 1, LANES)
    bias = pad_to(bias_ref[...], 1, LANES)
    total_row = jnp.broadcast_to(total, (1, LANES))
    mean_c, rstd_c, scale_c, bias_c = [c[:channels] for c in rows_to_cols([mean, rstd, scale, bias])]
    sub = iota((8, LANES), 0)
    const_ref[...] = jnp.where(sub == 0, scale * rstd, jnp.where(sub == 1, total_row, 0.0))
    valid = valid_lanes(counts_ref)
    normal = (hidden_ref[...] - mean_c) * rstd_c
    norm_ref[...] = normal
    summed = scale_c * normal + bias_c + start_ref[...].astype(F32)
    sig = sigmoid(summed)
    output_ref[...] = (summed * sig * valid).astype(BF16)
    grad = cotangent_ref[...].astype(F32) * valid * (sig * (1.0 + summed * (1.0 - sig)))
    grad_ref[...] = grad
    dbias = jnp.sum(grad, axis=1, keepdims=True)
    dgain = jnp.sum(grad * normal * valid, axis=1, keepdims=True)
    rows = cols_to_rows([dgain, dbias])[0:2]
    out_buf_ref[...] = jnp.broadcast_to(rows[None], out_buf_ref.shape)


def scatter(grad, weight_ref, hot_ref):
    channels = grad.shape[0]
    terms = nn(weight_ref[...], grad).astype(BF16)
    offsets = hot_ref.shape[1] // LANES
    wide = jnp.concatenate([terms[k * channels : (k + 1) * channels] for k in range(offsets)], axis=1)
    return nt(wide, hot_ref[...])


def row_gradient(grad, normal, const, dgain, dbias, valid):
    channels = grad.shape[0]
    factor, part_bias, part_gain = rows_to_cols([const[0:1], dbias / const[1:2], dgain / const[1:2]])
    return (
        factor[:channels] * (grad - (part_bias[:channels] + normal * part_gain[:channels])) * valid
    ).astype(BF16)


def fourth_kernel(
    grid, counts_ref, buf_ref, norm_ref, grad_ref, const_ref, weight_ref, hot_ref,
    norm_one_ref, slope_ref, halo_slope_ref, halo_cross_ref,
    out_buf_ref, grad_two_ref, table_ref, sums_ref,
):
    channels = norm_ref.shape[0]
    width = out_buf_ref.shape[1]
    valid = valid_lanes(counts_ref)
    both = jnp.sum(buf_ref[...], axis=0)
    sums_ref[...] = both
    grad = row_gradient(grad_ref[...], norm_ref[...], const_ref[...], both[0:1], both[1:2], valid)
    grad_two_ref[...] = grad
    table = scatter(grad, weight_ref, hot_ref)
    local = table[:, :LANES]
    table_ref[...] = local
    halo = pad_to(table[:, LANES : 2 * LANES], LANES, LANES).T
    pulled = local * slope_ref[...]
    dbias = jnp.sum(pulled, axis=1, keepdims=True)
    dgain = jnp.sum(pulled * norm_one_ref[...], axis=1, keepdims=True)
    rows = cols_to_rows([dgain, dbias])
    dgain = rows[0:1] + jnp.sum(halo * halo_cross_ref[...], axis=0, keepdims=True)
    dbias = rows[1:2] + jnp.sum(halo * halo_slope_ref[...], axis=0, keepdims=True)
    base = pack_rows(split3(dgain)[:2] + split3(dbias)[:2], 0.0)
    out_buf_ref[...] = jnp.broadcast_to(base.astype(BF16)[None], out_buf_ref.shape)
    put_blocks(out_buf_ref, halo, grid, -1, width, base)


def packed_weight_grad(taken_ref, grad, put):
    channels = grad.shape[0]
    zero = jnp.zeros((channels, LANES), BF16)

    def taken(k):
        return taken_ref[k * channels : (k + 1) * channels, :]

    for part in range(3):
        upper = jnp.concatenate([grad, zero], axis=1)
        lower = jnp.concatenate([zero[:32], grad[32 * part : 32 * part + 32]], axis=1)
        right = jnp.concatenate([upper, lower], axis=0)
        left = jnp.concatenate(
            [
                jnp.concatenate([taken(3 * e + part) for e in range(6)], axis=0),
                jnp.concatenate([taken(21 + e) for e in range(6)], axis=0),
            ],
            axis=1,
        )
        result = nt(left, right)
        for e in range(6):
            put(3 * e + part, result[e * channels : (e + 1) * channels])
    last = nt(taken_ref[18 * channels : 21 * channels, :], pad_to(grad, LANES, LANES))
    for e in range(3):
        put(18 + e, last[e * channels : (e + 1) * channels])


def weight_two_kernel(taken_ref, grad_ref, out_ref):
    channels = grad_ref.shape[0]

    def put(block, value):
        out_ref[block * channels : (block + 1) * channels, :] = value.astype(BF16)

    packed_weight_grad(taken_ref, grad_ref[...], put)
    tail = out_ref.shape[0] - 21 * channels
    if tail:
        out_ref[21 * channels :, :] = jnp.zeros((tail, LANES), BF16)


def fifth_kernel(
    grid, counts_ref, buf_ref, table_ref, place_ref, norm_ref, slope_ref, const_ref, sums_two_ref, taken_ref,
    packed_two_ref, grad_one_ref, give_ref, keep_ref, sums_ref,
):
    width = buf_ref.shape[1]
    channels = norm_ref.shape[0]
    valid = valid_lanes(counts_ref)
    dgains, dbiases = unpack_rows(buf_ref[...].astype(F32), ((0, 2), (2, 4)))
    dgain = jnp.sum(dgains, axis=0, keepdims=True)
    dbias = jnp.sum(dbiases, axis=0, keepdims=True)
    two = sums_two_ref[...]
    sums_ref[...] = jnp.concatenate([dgain, dbias, two], axis=0)[:, :channels]
    arrived = nt(eye(LANES), take_blocks(buf_ref, grid, 1, width).astype(BF16))[:channels].astype(BF16)
    back = table_ref[...] + nn(arrived, place_ref[...])
    grad = row_gradient(back * slope_ref[...], norm_ref[...], const_ref[...], dgain, dbias, valid)
    grad_one_ref[...] = grad
    core = lax.axis_index("gy") % 2
    used = 21 * channels

    @pl.when(core == 0)
    def _():
        def put(block, value):
            keep_ref[block * channels : (block + 1) * channels, :] = value.astype(BF16)

        packed_weight_grad(taken_ref, grad, put)
        give_ref[...] = packed_two_ref[...]
        if keep_ref.shape[0] > used:
            keep_ref[used:, :] = jnp.zeros((keep_ref.shape[0] - used, LANES), BF16)

    @pl.when(core != 0)
    def _():
        def put(block, value):
            give_ref[block * channels : (block + 1) * channels, :] = value.astype(BF16)

        packed_weight_grad(taken_ref, grad, put)
        keep_ref[...] = packed_two_ref[...]
        if keep_ref.shape[0] > used:
            give_ref[used:, :] = jnp.zeros((keep_ref.shape[0] - used, LANES), BF16)


def back_kernel(grad_ref, weight_ref, hot_ref, table_ref, halo_ref):
    table = scatter(grad_ref[...], weight_ref, hot_ref)
    table_ref[...] = table[:, :LANES]
    halo_ref[...] = pad_to(table[:, LANES : 2 * LANES], LANES, LANES).T.astype(BF16)


def sixth_kernel(grid, width, halo_ref, keep_ref, got_ref, out_buf_ref):
    devices, rows = out_buf_ref.shape[0], out_buf_ref.shape[1] - width
    put_blocks(out_buf_ref, halo_ref[...], grid, -1, width)
    total = (keep_ref[...].astype(F32) + got_ref[...].astype(F32)).astype(BF16)
    out_buf_ref[:, width:, :] = total.reshape(devices, rows, LANES)


def seventh_kernel(grid, width, counts_ref, buf_ref, table_ref, place_ref, grad_ref, out_buf_ref, out_ref):
    channels = table_ref.shape[0]
    devices, rows = buf_ref.shape[0], buf_ref.shape[1] - width
    valid = valid_lanes(counts_ref)
    arrived = nt(eye(LANES), take_blocks(buf_ref, grid, 1, width).astype(BF16))[:channels].astype(BF16)
    back = table_ref[...] + nn(arrived, place_ref[...])
    out_ref[...] = ((back + grad_ref[...]) * valid).astype(BF16)
    pieces = []
    for core in range(2):
        total = jnp.zeros((rows, LANES), F32)
        for d in range(core, devices, 2):
            total = total + buf_ref[d, width:, :].astype(F32)
        pieces.append(total.astype(BF16))
    for d in range(devices):
        out_buf_ref[d] = pieces[d % 2]


def last_kernel(own_ref, other_ref, one_ref, two_ref):
    core = lax.axis_index("gy") % 2
    channels = one_ref.shape[1]

    def unpack(src_ref, dst_ref):
        lane = iota((channels, LANES), 1)
        for e in range(7):
            extra = jnp.zeros((channels, LANES), F32)
            for part in range(3):
                block = 3 * e + part
                value = src_ref[block * channels : (block + 1) * channels, :].astype(F32)
                dst_ref[block] = value[:, :channels]
                if e < 6:
                    moved = pltpu.roll(value, 32 * (part + 1), 1)
                    extra = jnp.where(lane // 32 == part, moved, extra)
            if e < 6:
                dst_ref[21 + e] = extra[:, :channels]

    @pl.when(core == 0)
    def _():
        unpack(own_ref, one_ref)
        unpack(other_ref, two_ref)

    @pl.when(core != 0)
    def _():
        unpack(other_ref, one_ref)
        unpack(own_ref, two_ref)


def call(kernel, outs, *args, smem=0, scratch=()):
    specs = [
        pl.BlockSpec(memory_space=pltpu.SMEM if at < smem else pltpu.VMEM) for at in range(len(args))
    ]
    shapes = tuple(jax.ShapeDtypeStruct(shape, dtype) for shape, dtype in outs)
    result = pl.pallas_call(
        kernel,
        out_shape=shapes,
        in_specs=specs,
        out_specs=tuple(pl.BlockSpec(memory_space=pltpu.VMEM) for _ in shapes),
        scratch_shapes=list(scratch),
        compiler_params=pltpu.CompilerParams(vmem_limit_bytes=40 * 1024 * 1024),
    )(*args)
    return result


def to_all(x):
    return lax.all_to_all(x, AXES, 0, 0)


def swap_core(x):
    size = lax.axis_size("gy")
    return lax.ppermute(x, "gy", [(i, i ^ 1) for i in range(size)])


def on_device(
    features, kernel_map, send_rows, counts, weight_one, weight_two,
    first_norm_scale, first_norm_bias, second_norm_scale, second_norm_bias, cotangent,
):
    channels, rows = features.shape
    offsets = kernel_map.shape[0]
    width = send_rows.shape[1]
    grid = (lax.axis_size("gx"), lax.axis_size("gy"))
    devices = grid[0] * grid[1]
    flat = offsets * channels
    table = rows + 8 * width
    piece = -(-21 * channels // (devices * 16)) * 16
    packed = piece * devices
    full = (channels, rows)
    square = (LANES, LANES)
    one_flat = weight_one.reshape(flat, channels)
    two_flat = weight_two.reshape(flat, channels)
    scale_one, bias_one, scale_two, bias_two = [
        v.reshape(1, channels)
        for v in (first_norm_scale, first_norm_bias, second_norm_scale, second_norm_bias)
    ]

    buf, start, pick, place = call(
        functools.partial(open_kernel, grid),
        [((devices, width, LANES), BF16), (full, BF16), (square, BF16), (square, BF16)],
        counts, features, send_rows, smem=1,
    )
    buf = to_all(buf)
    hot, one_t, two_t = call(
        prepare_kernel,
        [((table, offsets * LANES), BF16), ((channels, flat), BF16), ((channels, flat), BF16)],
        kernel_map, one_flat, two_flat,
    )
    buf, hidden_one, taken_zero, flag = call(
        functools.partial(first_kernel, grid),
        [((devices, width, LANES), BF16), (full, F32), ((flat, LANES), BF16), (square, F32)],
        counts, buf, start, hot, one_t, place, smem=1,
    )
    buf = to_all(buf)
    buf, hidden_two, taken_one, norm_one, slope_one, halo_slope, halo_cross, const_one = call(
        functools.partial(second_kernel, grid),
        [
            ((devices, 2, LANES), F32), (full, F32), ((flat, LANES), BF16), (full, F32), (full, F32),
            (square, F32), (square, F32), ((8, LANES), F32),
        ],
        counts, buf, hidden_one, flag, scale_one, bias_one, hot, two_t,
        smem=1, scratch=[pltpu.VMEM((devices, LANES), F32)],
    )
    buf = to_all(buf)
    buf, output, norm_two, grad_sum, const_two = call(
        third_kernel,
        [((devices, 2, LANES), F32), (full, BF16), (full, F32), (full, F32), ((8, LANES), F32)],
        counts, buf, hidden_two, start, cotangent, scale_two, bias_two, smem=1,
    )
    buf = to_all(buf)
    buf, grad_two, table_two, sums_two = call(
        functools.partial(fourth_kernel, grid),
        [((devices, width, LANES), BF16), (full, BF16), (full, F32), ((2, LANES), F32)],
        counts, buf, norm_two, grad_sum, const_two, two_flat, hot, norm_one, slope_one, halo_slope, halo_cross,
        smem=1,
    )
    buf = to_all(buf)
    (packed_two,) = call(weight_two_kernel, [((packed, LANES), BF16)], taken_one, grad_two)
    grad_one, give, keep, grad_norms = call(
        functools.partial(fifth_kernel, grid),
        [(full, BF16), ((packed, LANES), BF16), ((packed, LANES), BF16), ((4, channels), F32)],
        counts, buf, table_two, place, norm_one, slope_one, const_one, sums_two, taken_zero, packed_two,
        smem=1,
    )
    got = swap_core(give)
    table_one, halo_one = call(
        back_kernel, [(full, F32), (square, BF16)], grad_one, one_flat, hot
    )
    (buf,) = call(
        functools.partial(sixth_kernel, grid, width),
        [((devices, width + piece, LANES), BF16)],
        halo_one, keep, got,
    )
    buf = to_all(buf)
    buf, grad_features = call(
        functools.partial(seventh_kernel, grid, width),
        [((devices, piece, LANES), BF16), (full, BF16)],
        counts, buf, table_one, place, grad_sum, smem=1,
    )
    own = to_all(buf).reshape(packed, LANES)
    other = swap_core(own)
    grad_weight_one, grad_weight_two = call(
        last_kernel,
        [(weight_one.shape, F32), (weight_two.shape, F32)],
        own, other,
    )
    return (output, grad_features, grad_weight_one, grad_weight_two, grad_norms)


def solution(mesh):
    return jax.shard_map(
        on_device,
        mesh=mesh,
        in_specs=(
            P(None, ("gx", "gy")),
            P(None, ("gx", "gy")),
            P(None, ("gx", "gy")),
            P(("gx", "gy")),
            P(),
            P(),
            P(),
            P(),
            P(),
            P(),
            P(None, ("gx", "gy")),
        ),
        out_specs=(P(None, ("gx", "gy")), P(None, ("gx", "gy")), P(), P(), P()),
        check_vma=False,
    )
```

```python
import functools

import jax
import jax.numpy as jnp
from jax import lax
from jax.experimental import pallas as pl
from jax.experimental.pallas import tpu as pltpu
from jax.sharding import PartitionSpec as P

EPS = 1e-05
STEP_LIST = ((1, 0), (-1, 0), (0, 1), (0, -1), (1, 1), (1, -1), (-1, 1), (-1, -1))
AXES = ("gx", "gy")
LANES = 128
F32 = jnp.float32
BF16 = jnp.bfloat16


def nn(a, b):
    return lax.dot_general(a, b, (((1,), (0,)), ((), ())), preferred_element_type=F32)


def nt(a, b):
    return lax.dot_general(a, b, (((1,), (1,)), ((), ())), preferred_element_type=F32)


def iota(shape, dim):
    return lax.broadcasted_iota(jnp.int32, shape, dim)


def eye(size):
    return jnp.where(iota((size, size), 0) == iota((size, size), 1), 1.0, 0.0).astype(BF16)


def sigmoid(v):
    return 1.0 / (1.0 + jnp.exp(-v))


def neighbour(place, grid, step):
    i, j = place[0] + step[0], place[1] + step[1]
    inside = (i >= 0) & (i < grid[0]) & (j >= 0) & (j < grid[1])
    return jnp.where(inside, i * grid[1] + j, place[0] * grid[1] + place[1]), inside


def here():
    return lax.axis_index("gx"), lax.axis_index("gy")


def put_blocks(buf_ref, rows, grid, sign, width, base=None):
    place = here()
    for n, (a, b) in enumerate(STEP_LIST):
        dest, _ = neighbour(place, grid, (sign * a, sign * b))
        block = rows[n * width : (n + 1) * width]
        if base is not None:
            block = jnp.where(iota(block.shape, 1) < 96, block, base)
        buf_ref[dest, 0:width, :] = block.astype(BF16)


def take_blocks(buf_ref, grid, sign, width):
    place = here()
    blocks = []
    for a, b in STEP_LIST:
        src, inside = neighbour(place, grid, (sign * a, sign * b))
        block = buf_ref[src, 0:width, :].astype(F32)
        blocks.append(jnp.where(inside, block, 0.0))
    return jnp.concatenate(blocks, axis=0)


def pad_to(x, rows, lanes):
    if x.shape[1] < lanes:
        x = jnp.concatenate([x, jnp.zeros((x.shape[0], lanes - x.shape[1]), x.dtype)], axis=1)
    if x.shape[0] < rows:
        x = jnp.concatenate([x, jnp.zeros((rows - x.shape[0], lanes), x.dtype)], axis=0)
    return x


def cols_to_rows(cols):
    lane = iota((cols[0].shape[0], LANES), 1)
    total = jnp.zeros((cols[0].shape[0], LANES), F32)
    for at, col in enumerate(cols):
        total = jnp.where(lane == at, col, total)
    return pad_to(total, LANES, LANES).T


def rows_to_cols(rows):
    sub = iota((LANES, LANES), 0)
    total = jnp.zeros((LANES, LANES), F32)
    for at, row in enumerate(rows):
        total = jnp.where(sub == at, row, total)
    total = total.T
    return [total[:, at : at + 1] for at in range(len(rows))]


def split3(x):
    high = x.astype(BF16).astype(F32)
    mid = (x - high).astype(BF16).astype(F32)
    low = (x - high - mid).astype(BF16).astype(F32)
    return [high, mid, low]


def pack_rows(pieces, last):
    sub = iota((16, LANES), 0)
    lane = iota((16, LANES), 1)
    total = jnp.zeros((16, LANES), F32)
    for q, piece in enumerate(pieces):
        total = jnp.where(sub // 3 == q, piece, total)
    part = sub % 3
    moved = jnp.where(
        part == 0,
        pltpu.roll(total, 96, 1),
        jnp.where(part == 1, pltpu.roll(total, 64, 1), pltpu.roll(total, 32, 1)),
    )
    moved = jnp.where(sub == 15, last, moved)
    return jnp.where(lane >= 96, moved, 0.0)


def unpack_rows(tiles, groups):
    devices = tiles.shape[0]
    flat = tiles.reshape(devices * 16, LANES)
    sub = iota(tiles.shape, 1)
    lane = iota(tiles.shape, 2)
    part = sub % 3
    moved = [pltpu.roll(flat, 32 * (p + 1), 1).reshape(tiles.shape) for p in range(3)]
    value = jnp.where(part == 0, moved[0], jnp.where(part == 1, moved[1], moved[2]))
    value = jnp.where((lane // 32 == part) & (sub < 15), value, 0.0)
    results = []
    for low, high in groups:
        mask = (sub >= 3 * low) & (sub < 3 * high)
        results.append(jnp.sum(jnp.where(mask, value, 0.0), axis=1))
    return results


def valid_lanes(counts_ref, rows=1):
    return (iota((rows, LANES), 1) < counts_ref[0]).astype(F32)


def open_kernel(
    grid, counts_ref, features_hbm, send_hbm, buf_ref, start_ref, place_ref, features_ref, send_ref, sems
):
    copies = [
        pltpu.make_async_copy(features_hbm, features_ref, sems.at[0]),
        pltpu.make_async_copy(send_hbm, send_ref, sems.at[1]),
    ]
    for copy in copies:
        copy.start()
    for copy in copies:
        copy.wait()
    width = send_ref.shape[1]
    send = send_ref[...].astype(F32).astype(BF16)
    spread = jnp.where(iota((width, LANES), 1) % width == iota((width, LANES), 0), 1.0, 0.0).astype(BF16)
    wide = nn(send, spread)
    wide = jnp.where(iota(wide.shape, 1) // width == iota(wide.shape, 0), wide, 0.0)
    row = jnp.sum(wide, axis=0, keepdims=True)
    place = jnp.where(row == iota((LANES, LANES), 0).astype(F32), 1.0, 0.0).T.astype(BF16)
    place_ref[...] = place
    valid = valid_lanes(counts_ref)
    start = features_ref[...].astype(F32) * valid
    start_ref[...] = start.astype(BF16)
    extra = jnp.where(iota((LANES - 96, LANES), 0) == 0, valid, 0.0)
    rows = nt(place, jnp.concatenate([start, extra], axis=0).astype(BF16))
    put_blocks(buf_ref, rows, grid, 1, width)


def prepare_kernel(map_ref, one_ref, two_ref, hot_ref, one_t_ref, two_t_ref):
    table = hot_ref.shape[0]
    sub = iota((table, LANES), 0)
    for k in range(map_ref.shape[0]):
        hot_ref[:, k * LANES : (k + 1) * LANES] = jnp.where(
            sub == map_ref[k : k + 1, :], 1.0, 0.0
        ).astype(BF16)
    unit = eye(one_ref.shape[1])
    one_t_ref[...] = nt(unit, one_ref[...]).astype(BF16)
    two_t_ref[...] = nt(unit, two_ref[...]).astype(BF16)


def gather(tables, hot_ref, taken_refs):
    channels = tables[0].shape[0]
    taken = nn(jnp.concatenate(tables, axis=0), hot_ref[...]).astype(BF16)
    for at, ref in enumerate(taken_refs):
        for k in range(hot_ref.shape[1] // LANES):
            ref[k * channels : (k + 1) * channels, :] = taken[
                at * channels : (at + 1) * channels, k * LANES : (k + 1) * LANES
            ]


def gather_convolve(table, hot_ref, weight_t_ref, taken_ref):
    gather([table], hot_ref, [taken_ref])
    return nn(weight_t_ref[...], taken_ref[...])


def first_kernel(
    grid, counts_ref, buf_ref, start_ref, hot_ref, weight_ref, place_ref,
    out_buf_ref, hidden_ref, table_ref, flag_ref, taken_ref,
):
    width = buf_ref.shape[1]
    channels = start_ref.shape[0]
    halo_rows = take_blocks(buf_ref, grid, -1, width).astype(BF16)
    flag_ref[...] = jnp.broadcast_to(halo_rows[:, 96:97].astype(F32), (LANES, LANES))
    halo = nt(eye(LANES), halo_rows)[:channels].astype(BF16)
    table = jnp.concatenate([start_ref[...], halo], axis=1)
    table_ref[...] = table
    hidden = gather_convolve(table, hot_ref, weight_ref, taken_ref)
    hidden_ref[...] = hidden
    valid = valid_lanes(counts_ref)
    count = counts_ref[0].astype(F32)
    sums = jnp.sum(hidden * valid, axis=1, keepdims=True)
    centred = (hidden - sums / count) * valid
    spread = jnp.sum(centred * centred, axis=1, keepdims=True)
    stat = cols_to_rows([sums, spread])
    base = pack_rows(split3(stat[0:1]) + split3(stat[1:2])[:2], count)
    out_buf_ref[...] = jnp.broadcast_to(base.astype(BF16)[None], out_buf_ref.shape)
    rows = pad_to(nt(place_ref[...], centred.astype(BF16)), LANES, LANES)
    put_blocks(out_buf_ref, rows, grid, 1, width, base)


def second_kernel(
    grid, counts_ref, buf_ref, hidden_ref, flag_ref, scale_ref, bias_ref, hot_ref, weight_ref,
    out_buf_ref, hidden_two_ref, table_ref, norm_ref, slope_ref, halo_slope_ref, halo_cross_ref,
    const_ref, mean_ref, taken_ref,
):
    width = buf_ref.shape[1]
    channels = hidden_ref.shape[0]
    tiles = buf_ref[...].astype(F32)
    sums, spreads = unpack_rows(tiles, ((0, 3), (3, 5)))
    counts = tiles[:, 15, 96:97]
    total = jnp.sum(counts, axis=0, keepdims=True)
    means = sums / counts
    mean_ref[...] = means
    mean = jnp.sum(sums, axis=0, keepdims=True) / total
    apart = means - mean
    var = jnp.sum(spreads + counts * apart * apart, axis=0, keepdims=True) / total
    rstd = lax.rsqrt(var + EPS)
    scale = pad_to(scale_ref[...], 1, LANES)
    bias = pad_to(bias_ref[...], 1, LANES)
    total_row = jnp.broadcast_to(total, (1, LANES))
    mean_c, rstd_c, scale_c, bias_c = [c[:channels] for c in rows_to_cols([mean, rstd, scale, bias])]
    sub = iota((8, LANES), 0)
    const_ref[...] = jnp.where(sub == 0, scale * rstd, jnp.where(sub == 1, total_row, 0.0))

    valid = valid_lanes(counts_ref)
    normal = (hidden_ref[...] - mean_c) * rstd_c
    norm_ref[...] = normal
    linear = scale_c * normal + bias_c
    sig = sigmoid(linear)
    slope_ref[...] = sig * (1.0 + linear * (1.0 - sig)) * valid
    act = (linear * sig * valid).astype(BF16)

    place = here()
    lifted = []
    for n, (a, b) in enumerate(STEP_LIST):
        src, inside = neighbour(place, grid, (-a, -b))
        block = buf_ref[src, 0:width, :].astype(F32) + mean_ref[pl.ds(src, 1), :]
        lifted.append(jnp.where(inside, block, 0.0))
    lane = iota((LANES, LANES), 1)
    halo = jnp.where(lane < channels, jnp.concatenate(lifted, axis=0), 0.0)
    flag = flag_ref[...]
    halo_normal = (halo - mean) * rstd
    halo_linear = scale * halo_normal + bias
    halo_sig = sigmoid(halo_linear)
    halo_slope = halo_sig * (1.0 + halo_linear * (1.0 - halo_sig)) * flag
    halo_slope_ref[...] = halo_slope
    halo_cross_ref[...] = halo_slope * halo_normal
    halo_act = nt(eye(LANES), (halo_linear * halo_sig * flag).astype(BF16))[:channels].astype(BF16)

    table = jnp.concatenate([act, halo_act], axis=1)
    table_ref[...] = table
    hidden = gather_convolve(table, hot_ref, weight_ref, taken_ref)
    hidden_two_ref[...] = hidden
    count = counts_ref[0].astype(F32)
    sums_two = jnp.sum(hidden * valid, axis=1, keepdims=True)
    centred = (hidden - sums_two / count) * valid
    spread_two = jnp.sum(centred * centred, axis=1, keepdims=True)
    stat = cols_to_rows([sums_two, spread_two])[0:2]
    stat = jnp.where(iota((2, LANES), 1) < 96, stat, count)
    out_buf_ref[...] = jnp.broadcast_to(stat[None], out_buf_ref.shape)


def third_kernel(
    counts_ref, buf_ref, hidden_ref, start_ref, cotangent_ref, scale_ref, bias_ref,
    out_buf_ref, output_ref, norm_ref, grad_ref, const_ref,
):
    channels = hidden_ref.shape[0]
    sums = buf_ref[:, 0, :]
    spreads = buf_ref[:, 1, :]
    counts = sums[:, 96:97]
    total = jnp.sum(counts, axis=0, keepdims=True)
    mean = jnp.sum(sums, axis=0, keepdims=True) / total
    apart = sums / counts - mean
    var = jnp.sum(spreads + counts * apart * apart, axis=0, keepdims=True) / total
    rstd = lax.rsqrt(var + EPS)
    scale = pad_to(scale_ref[...], 1, LANES)
    bias = pad_to(bias_ref[...], 1, LANES)
    total_row = jnp.broadcast_to(total, (1, LANES))
    mean_c, rstd_c, scale_c, bias_c = [c[:channels] for c in rows_to_cols([mean, rstd, scale, bias])]
    sub = iota((8, LANES), 0)
    const_ref[...] = jnp.where(sub == 0, scale * rstd, jnp.where(sub == 1, total_row, 0.0))
    valid = valid_lanes(counts_ref)
    normal = (hidden_ref[...] - mean_c) * rstd_c
    norm_ref[...] = normal
    summed = scale_c * normal + bias_c + start_ref[...].astype(F32)
    sig = sigmoid(summed)
    output_ref[...] = (summed * sig * valid).astype(BF16)
    grad = cotangent_ref[...].astype(F32) * valid * (sig * (1.0 + summed * (1.0 - sig)))
    grad_ref[...] = grad
    dbias = jnp.sum(grad, axis=1, keepdims=True)
    dgain = jnp.sum(grad * normal * valid, axis=1, keepdims=True)
    rows = cols_to_rows([dgain, dbias])[0:2]
    out_buf_ref[...] = jnp.broadcast_to(rows[None], out_buf_ref.shape)


def scatter(grad, weight_ref, hot_ref):
    channels = grad.shape[0]
    terms = nn(weight_ref[...], grad).astype(BF16)
    offsets = hot_ref.shape[1] // LANES
    wide = jnp.concatenate([terms[k * channels : (k + 1) * channels] for k in range(offsets)], axis=1)
    return nt(wide, hot_ref[...])


def row_gradient(grad, normal, const, dgain, dbias, valid):
    channels = grad.shape[0]
    factor, part_bias, part_gain = rows_to_cols([const[0:1], dbias / const[1:2], dgain / const[1:2]])
    return (
        factor[:channels] * (grad - (part_bias[:channels] + normal * part_gain[:channels])) * valid
    ).astype(BF16)


def fourth_kernel(
    grid, counts_ref, buf_ref, norm_ref, grad_ref, const_ref, weight_ref, hot_ref,
    norm_one_ref, slope_ref, halo_slope_ref, halo_cross_ref,
    out_buf_ref, grad_two_ref, table_ref, sums_ref,
):
    channels = norm_ref.shape[0]
    width = out_buf_ref.shape[1]
    valid = valid_lanes(counts_ref)
    both = jnp.sum(buf_ref[...], axis=0)
    sums_ref[...] = both
    grad = row_gradient(grad_ref[...], norm_ref[...], const_ref[...], both[0:1], both[1:2], valid)
    grad_two_ref[...] = grad
    table = scatter(grad, weight_ref, hot_ref)
    local = table[:, :LANES]
    table_ref[...] = local
    halo = pad_to(table[:, LANES : 2 * LANES], LANES, LANES).T
    pulled = local * slope_ref[...]
    dbias = jnp.sum(pulled, axis=1, keepdims=True)
    dgain = jnp.sum(pulled * norm_one_ref[...], axis=1, keepdims=True)
    rows = cols_to_rows([dgain, dbias])
    dgain = rows[0:1] + jnp.sum(halo * halo_cross_ref[...], axis=0, keepdims=True)
    dbias = rows[1:2] + jnp.sum(halo * halo_slope_ref[...], axis=0, keepdims=True)
    base = pack_rows(split3(dgain)[:2] + split3(dbias)[:2], 0.0)
    out_buf_ref[...] = jnp.broadcast_to(base.astype(BF16)[None], out_buf_ref.shape)
    put_blocks(out_buf_ref, halo, grid, -1, width, base)


def packed_weight_grad(taken_ref, grad, put):
    channels = grad.shape[0]
    zero = jnp.zeros((channels, LANES), BF16)

    def taken(k):
        return taken_ref[k * channels : (k + 1) * channels, :]

    for part in range(3):
        upper = jnp.concatenate([grad, zero], axis=1)
        lower = jnp.concatenate([zero[:32], grad[32 * part : 32 * part + 32]], axis=1)
        right = jnp.concatenate([upper, lower], axis=0)
        left = jnp.concatenate(
            [
                jnp.concatenate([taken(3 * e + part) for e in range(6)], axis=0),
                jnp.concatenate([taken(21 + e) for e in range(6)], axis=0),
            ],
            axis=1,
        )
        result = nt(left, right)
        for e in range(6):
            put(3 * e + part, result[e * channels : (e + 1) * channels])
    last = nt(taken_ref[18 * channels : 21 * channels, :], pad_to(grad, LANES, LANES))
    for e in range(3):
        put(18 + e, last[e * channels : (e + 1) * channels])


def fifth_kernel(
    grid, counts_ref, buf_ref, table_ref, place_ref, norm_ref, slope_ref, const_ref, sums_two_ref,
    table_zero_ref, table_act_ref, hot_ref, grad_two_ref,
    grad_one_ref, give_ref, keep_ref, sums_ref, taken_zero_ref, taken_act_ref,
):
    width = buf_ref.shape[1]
    channels = norm_ref.shape[0]
    valid = valid_lanes(counts_ref)
    dgains, dbiases = unpack_rows(buf_ref[...].astype(F32), ((0, 2), (2, 4)))
    dgain = jnp.sum(dgains, axis=0, keepdims=True)
    dbias = jnp.sum(dbiases, axis=0, keepdims=True)
    two = sums_two_ref[...]
    sums_ref[...] = jnp.concatenate([dgain, dbias, two], axis=0)[:, :channels]
    arrived = nt(eye(LANES), take_blocks(buf_ref, grid, 1, width).astype(BF16))[:channels].astype(BF16)
    back = table_ref[...] + nn(arrived, place_ref[...])
    grad = row_gradient(back * slope_ref[...], norm_ref[...], const_ref[...], dgain, dbias, valid)
    grad_one_ref[...] = grad
    gather([table_zero_ref[...], table_act_ref[...]], hot_ref, [taken_zero_ref, taken_act_ref])
    core = lax.axis_index("gy") % 2
    used = 21 * channels

    def store(taken_ref, row_grad, ref):
        def put(block, value):
            ref[block * channels : (block + 1) * channels, :] = value.astype(ref.dtype)

        packed_weight_grad(taken_ref, row_grad, put)
        if ref.shape[0] > used:
            ref[used:, :] = jnp.zeros((ref.shape[0] - used, LANES), ref.dtype)

    @pl.when(core == 0)
    def _():
        store(taken_zero_ref, grad, keep_ref)
        store(taken_act_ref, grad_two_ref[...], give_ref)

    @pl.when(core != 0)
    def _():
        store(taken_zero_ref, grad, give_ref)
        store(taken_act_ref, grad_two_ref[...], keep_ref)


def back_kernel(grad_ref, weight_ref, hot_ref, table_ref, halo_ref):
    table = scatter(grad_ref[...], weight_ref, hot_ref)
    table_ref[...] = table[:, :LANES]
    halo_ref[...] = pad_to(table[:, LANES : 2 * LANES], LANES, LANES).T.astype(BF16)


def sixth_kernel(grid, width, halo_ref, keep_ref, got_ref, out_buf_ref):
    devices, rows = out_buf_ref.shape[0], out_buf_ref.shape[1] - width
    put_blocks(out_buf_ref, halo_ref[...], grid, -1, width)
    total = (keep_ref[...] + got_ref[...].astype(F32)).astype(BF16)
    out_buf_ref[:, width:, :] = total.reshape(devices, rows, LANES)


def seventh_kernel(grid, width, counts_ref, buf_ref, table_ref, place_ref, grad_ref, out_buf_ref, out_ref):
    channels = table_ref.shape[0]
    devices, rows = buf_ref.shape[0], buf_ref.shape[1] - width
    valid = valid_lanes(counts_ref)
    arrived = nt(eye(LANES), take_blocks(buf_ref, grid, 1, width).astype(BF16))[:channels].astype(BF16)
    back = table_ref[...] + nn(arrived, place_ref[...])
    out_ref[...] = ((back + grad_ref[...]) * valid).astype(BF16)
    pieces = []
    for core in range(2):
        total = jnp.zeros((rows, LANES), F32)
        for d in range(core, devices, 2):
            total = total + buf_ref[d, width:, :].astype(F32)
        pieces.append(total.astype(BF16))
    for d in range(devices):
        out_buf_ref[d] = pieces[d % 2]


def unpack(src_ref, out_hbm, block_ref, sems):
    channels = block_ref.shape[1]
    lane = iota((channels, LANES), 1)
    copies = []

    def send(first, count):
        part = pl.ds(first, count)
        copies.append(pltpu.make_async_copy(block_ref.at[part], out_hbm.at[part], sems.at[len(copies)]))
        copies[-1].start()

    for e in range(7):
        extra = jnp.zeros((channels, LANES), F32)
        for part in range(3):
            block = 3 * e + part
            value = src_ref[block * channels : (block + 1) * channels, :].astype(F32)
            block_ref[block] = value[:, :channels]
            if e < 6:
                moved = pltpu.roll(value, 32 * (part + 1), 1)
                extra = jnp.where(lane // 32 == part, moved, extra)
        send(3 * e, 3)
        if e < 6:
            block_ref[21 + e] = extra[:, :channels]
            send(21 + e, 1)
    for copy in copies:
        copy.wait()


def own_kernel(own_ref, small_in, more_in, sums_in, one_hbm, two_hbm, small_out, more_out, sums_out, block_ref, sems):
    core = lax.axis_index("gy") % 2
    small_out[...] = small_in[...]
    more_out[...] = more_in[...]
    sums_out[...] = sums_in[...]

    @pl.when(core == 0)
    def _():
        unpack(own_ref, one_hbm, block_ref, sems)

    @pl.when(core != 0)
    def _():
        unpack(own_ref, two_hbm, block_ref, sems)


def other_kernel(other_ref, one_in, two_in, one_hbm, two_hbm, block_ref, sems):
    core = lax.axis_index("gy") % 2

    @pl.when(core == 0)
    def _():
        unpack(other_ref, two_hbm, block_ref, sems)

    @pl.when(core != 0)
    def _():
        unpack(other_ref, one_hbm, block_ref, sems)


def call(kernel, outs, *args, smem=0, scratch=(), hbm=(), hbm_outs=(), aliases=None):
    def space(at):
        if at in hbm:
            return pltpu.HBM
        return pltpu.SMEM if at < smem else pltpu.VMEM

    shapes = tuple(jax.ShapeDtypeStruct(shape, dtype) for shape, dtype in outs)
    return pl.pallas_call(
        kernel,
        out_shape=shapes,
        in_specs=[pl.BlockSpec(memory_space=space(at)) for at in range(len(args))],
        out_specs=tuple(
            pl.BlockSpec(memory_space=pltpu.HBM if at in hbm_outs else pltpu.VMEM) for at in range(len(shapes))
        ),
        scratch_shapes=list(scratch),
        input_output_aliases=aliases or {},
        compiler_params=pltpu.CompilerParams(vmem_limit_bytes=40 * 1024 * 1024),
    )(*args)


def to_all(x):
    return lax.all_to_all(x, AXES, 0, 0)


def swap_core(x):
    size = lax.axis_size("gy")
    return lax.ppermute(x, "gy", [(i, i ^ 1) for i in range(size)])


def on_device(
    features, kernel_map, send_rows, counts, weight_one, weight_two,
    first_norm_scale, first_norm_bias, second_norm_scale, second_norm_bias, cotangent,
):
    channels, rows = features.shape
    offsets = kernel_map.shape[0]
    width = send_rows.shape[1]
    grid = (lax.axis_size("gx"), lax.axis_size("gy"))
    devices = grid[0] * grid[1]
    flat = offsets * channels
    table = rows + 8 * width
    piece = -(-21 * channels // (devices * 16)) * 16
    packed = piece * devices
    full = (channels, rows)
    square = (LANES, LANES)
    one_flat = weight_one.reshape(flat, channels)
    two_flat = weight_two.reshape(flat, channels)
    scale_one, bias_one, scale_two, bias_two = [
        v.reshape(1, channels)
        for v in (first_norm_scale, first_norm_bias, second_norm_scale, second_norm_bias)
    ]

    taken = pltpu.VMEM((flat, LANES), BF16)
    wide = ((channels, table), BF16)
    buf, start, place = call(
        functools.partial(open_kernel, grid),
        [((devices, width, LANES), BF16), (full, BF16), (square, BF16)],
        counts, features, send_rows, smem=1, hbm=(1, 2),
        scratch=[
            pltpu.VMEM(full, BF16), pltpu.VMEM(send_rows.shape, jnp.int32), pltpu.SemaphoreType.DMA((2,)),
        ],
    )
    buf = to_all(buf)
    hot, one_t, two_t = call(
        prepare_kernel,
        [((table, offsets * LANES), BF16), ((channels, flat), BF16), ((channels, flat), BF16)],
        kernel_map, one_flat, two_flat,
    )
    buf, hidden_one, table_zero, flag = call(
        functools.partial(first_kernel, grid),
        [((devices, width, LANES), BF16), (full, F32), wide, (square, F32)],
        counts, buf, start, hot, one_t, place, smem=1, scratch=[taken],
    )
    buf = to_all(buf)
    buf, hidden_two, table_act, norm_one, slope_one, halo_slope, halo_cross, const_one = call(
        functools.partial(second_kernel, grid),
        [
            ((devices, 2, LANES), F32), (full, F32), wide, (full, F32), (full, F32),
            (square, F32), (square, F32), ((8, LANES), F32),
        ],
        counts, buf, hidden_one, flag, scale_one, bias_one, hot, two_t,
        smem=1, scratch=[pltpu.VMEM((devices, LANES), F32), taken],
    )
    buf = to_all(buf)
    buf, output, norm_two, grad_sum, const_two = call(
        third_kernel,
        [((devices, 2, LANES), F32), (full, BF16), (full, F32), (full, F32), ((8, LANES), F32)],
        counts, buf, hidden_two, start, cotangent, scale_two, bias_two, smem=1,
    )
    buf = to_all(buf)
    buf, grad_two, table_two, sums_two = call(
        functools.partial(fourth_kernel, grid),
        [((devices, width, LANES), BF16), (full, BF16), (full, F32), ((2, LANES), F32)],
        counts, buf, norm_two, grad_sum, const_two, two_flat, hot, norm_one, slope_one, halo_slope, halo_cross,
        smem=1,
    )
    buf = to_all(buf)
    grad_one, give, keep, grad_norms = call(
        functools.partial(fifth_kernel, grid),
        [(full, BF16), ((packed, LANES), BF16), ((packed, LANES), F32), ((4, channels), F32)],
        counts, buf, table_two, place, norm_one, slope_one, const_one, sums_two,
        table_zero, table_act, hot, grad_two, smem=1, scratch=[taken, taken],
    )
    got = swap_core(give)
    table_one, halo_one = call(
        back_kernel, [(full, F32), (square, BF16)], grad_one, one_flat, hot
    )
    (buf,) = call(
        functools.partial(sixth_kernel, grid, width),
        [((devices, width + piece, LANES), BF16)],
        halo_one, keep, got,
    )
    buf = to_all(buf)
    buf, grad_features = call(
        functools.partial(seventh_kernel, grid, width),
        [((devices, piece, LANES), BF16), (full, BF16)],
        counts, buf, table_one, place, grad_sum, smem=1,
    )
    own = to_all(buf).reshape(packed, LANES)
    other = swap_core(own)
    weights = [(weight_one.shape, F32), (weight_two.shape, F32)]
    blocks = [pltpu.VMEM(weight_one.shape, F32), pltpu.SemaphoreType.DMA((13,))]
    grad_weight_one, grad_weight_two, output, grad_features, grad_norms = call(
        own_kernel,
        weights + [(full, BF16), (full, BF16), ((4, channels), F32)],
        own, output, grad_features, grad_norms, hbm_outs=(0, 1), scratch=blocks,
    )
    grad_weight_one, grad_weight_two = call(
        other_kernel, weights, other, grad_weight_one, grad_weight_two,
        hbm=(1, 2), hbm_outs=(0, 1), scratch=blocks, aliases={1: 0, 2: 1},
    )
    return (output, grad_features, grad_weight_one, grad_weight_two, grad_norms)


def solution(mesh):
    return jax.shard_map(
        on_device,
        mesh=mesh,
        in_specs=(
            P(None, ("gx", "gy")),
            P(None, ("gx", "gy")),
            P(None, ("gx", "gy")),
            P(("gx", "gy")),
            P(),
            P(),
            P(),
            P(),
            P(),
            P(),
            P(None, ("gx", "gy")),
        ),
        out_specs=(P(None, ("gx", "gy")), P(None, ("gx", "gy")), P(), P(), P()),
        check_vma=False,
    )
```

```python
import functools

import jax
import jax.numpy as jnp
from jax import lax
from jax.experimental import pallas as pl
from jax.experimental.pallas import tpu as pltpu
from jax.sharding import PartitionSpec as P

EPS = 1e-05
STEP_LIST = ((1, 0), (-1, 0), (0, 1), (0, -1), (1, 1), (1, -1), (-1, 1), (-1, -1))
AXES = ("gx", "gy")
LANES = 128
F32 = jnp.float32
BF16 = jnp.bfloat16


def nn(a, b):
    return lax.dot_general(a, b, (((1,), (0,)), ((), ())), preferred_element_type=F32)


def nt(a, b):
    return lax.dot_general(a, b, (((1,), (1,)), ((), ())), preferred_element_type=F32)


def iota(shape, dim):
    return lax.broadcasted_iota(jnp.int32, shape, dim)


def eye(size):
    return jnp.where(iota((size, size), 0) == iota((size, size), 1), 1.0, 0.0).astype(BF16)


def sigmoid(v):
    return 1.0 / (1.0 + jnp.exp(-v))


def neighbour(place, grid, step):
    i, j = place[0] + step[0], place[1] + step[1]
    inside = (i >= 0) & (i < grid[0]) & (j >= 0) & (j < grid[1])
    return jnp.where(inside, i * grid[1] + j, place[0] * grid[1] + place[1]), inside


def here():
    return lax.axis_index("gx"), lax.axis_index("gy")


def put_blocks(buf_ref, rows, grid, sign, width, base=None):
    place = here()
    for n, (a, b) in enumerate(STEP_LIST):
        dest, _ = neighbour(place, grid, (sign * a, sign * b))
        block = rows[n * width : (n + 1) * width]
        if base is not None:
            block = jnp.where(iota(block.shape, 1) < 96, block, base)
        buf_ref[dest, 0:width, :] = block.astype(BF16)


def take_blocks(buf_ref, grid, sign, width):
    place = here()
    blocks = []
    for a, b in STEP_LIST:
        src, inside = neighbour(place, grid, (sign * a, sign * b))
        block = buf_ref[src, 0:width, :].astype(F32)
        blocks.append(jnp.where(inside, block, 0.0))
    return jnp.concatenate(blocks, axis=0)


def pad_to(x, rows, lanes):
    if x.shape[1] < lanes:
        x = jnp.concatenate([x, jnp.zeros((x.shape[0], lanes - x.shape[1]), x.dtype)], axis=1)
    if x.shape[0] < rows:
        x = jnp.concatenate([x, jnp.zeros((rows - x.shape[0], lanes), x.dtype)], axis=0)
    return x


def cols_to_rows(cols):
    lane = iota((cols[0].shape[0], LANES), 1)
    total = jnp.zeros((cols[0].shape[0], LANES), F32)
    for at, col in enumerate(cols):
        total = jnp.where(lane == at, col, total)
    return pad_to(total, LANES, LANES).T


def rows_to_cols(rows):
    sub = iota((LANES, LANES), 0)
    total = jnp.zeros((LANES, LANES), F32)
    for at, row in enumerate(rows):
        total = jnp.where(sub == at, row, total)
    total = total.T
    return [total[:, at : at + 1] for at in range(len(rows))]


def split3(x):
    high = x.astype(BF16).astype(F32)
    mid = (x - high).astype(BF16).astype(F32)
    low = (x - high - mid).astype(BF16).astype(F32)
    return [high, mid, low]


def pack_rows(pieces, last):
    sub = iota((16, LANES), 0)
    lane = iota((16, LANES), 1)
    total = jnp.zeros((16, LANES), F32)
    for q, piece in enumerate(pieces):
        total = jnp.where(sub // 3 == q, piece, total)
    part = sub % 3
    moved = jnp.where(
        part == 0,
        pltpu.roll(total, 96, 1),
        jnp.where(part == 1, pltpu.roll(total, 64, 1), pltpu.roll(total, 32, 1)),
    )
    moved = jnp.where(sub == 15, last, moved)
    return jnp.where(lane >= 96, moved, 0.0)


def unpack_rows(tiles, groups):
    devices = tiles.shape[0]
    flat = tiles.reshape(devices * 16, LANES)
    sub = iota(tiles.shape, 1)
    lane = iota(tiles.shape, 2)
    part = sub % 3
    moved = [pltpu.roll(flat, 32 * (p + 1), 1).reshape(tiles.shape) for p in range(3)]
    value = jnp.where(part == 0, moved[0], jnp.where(part == 1, moved[1], moved[2]))
    value = jnp.where((lane // 32 == part) & (sub < 15), value, 0.0)
    results = []
    for low, high in groups:
        mask = (sub >= 3 * low) & (sub < 3 * high)
        results.append(jnp.sum(jnp.where(mask, value, 0.0), axis=1))
    return results


def valid_lanes(counts_ref, rows=1):
    return (iota((rows, LANES), 1) < counts_ref[0]).astype(F32)


def open_kernel(
    grid, counts_ref, features_hbm, send_hbm, buf_ref, start_ref, place_ref, features_ref, send_ref, sems
):
    copies = [
        pltpu.make_async_copy(features_hbm, features_ref, sems.at[0]),
        pltpu.make_async_copy(send_hbm, send_ref, sems.at[1]),
    ]
    for copy in copies:
        copy.start()
    for copy in copies:
        copy.wait()
    width = send_ref.shape[1]
    send = send_ref[...].astype(F32).astype(BF16)
    spread = jnp.where(iota((width, LANES), 1) % width == iota((width, LANES), 0), 1.0, 0.0).astype(BF16)
    wide = nn(send, spread)
    wide = jnp.where(iota(wide.shape, 1) // width == iota(wide.shape, 0), wide, 0.0)
    row = jnp.sum(wide, axis=0, keepdims=True)
    place = jnp.where(row == iota((LANES, LANES), 0).astype(F32), 1.0, 0.0).T.astype(BF16)
    place_ref[...] = place
    valid = valid_lanes(counts_ref)
    start = features_ref[...].astype(F32) * valid
    start_ref[...] = start.astype(BF16)
    extra = jnp.where(iota((LANES - 96, LANES), 0) == 0, valid, 0.0)
    rows = nt(place, jnp.concatenate([start, extra], axis=0).astype(BF16))
    put_blocks(buf_ref, rows, grid, 1, width)


def prepare_kernel(
    map_hbm, one_hbm, two_hbm, hot_ref, one_t_ref, two_t_ref, map_ref, one_ref, two_ref, sems
):
    pairs = ((map_hbm, map_ref), (one_hbm, one_ref), (two_hbm, two_ref))
    copies = [pltpu.make_async_copy(src, dst, sems.at[at]) for at, (src, dst) in enumerate(pairs)]
    for copy in copies:
        copy.start()
    copies[0].wait()
    table = hot_ref.shape[0]
    sub = iota((table, LANES), 0)
    for k in range(map_ref.shape[0]):
        part = slice(k * LANES, (k + 1) * LANES)
        hot_ref[:, part] = jnp.where(sub == map_ref[k : k + 1, :], 1.0, 0.0).astype(BF16)
    unit = eye(one_ref.shape[1])
    copies[1].wait()
    one_t_ref[...] = nt(unit, one_ref[...]).astype(BF16)
    copies[2].wait()
    two_t_ref[...] = nt(unit, two_ref[...]).astype(BF16)


def gather(tables, hot_ref, taken_refs):
    channels = tables[0].shape[0]
    taken = nn(jnp.concatenate(tables, axis=0), hot_ref[...]).astype(BF16)
    for at, ref in enumerate(taken_refs):
        for k in range(hot_ref.shape[1] // LANES):
            ref[k * channels : (k + 1) * channels, :] = taken[
                at * channels : (at + 1) * channels, k * LANES : (k + 1) * LANES
            ]


def gather_convolve(table, hot_ref, weight_t_ref, taken_ref):
    gather([table], hot_ref, [taken_ref])
    return nn(weight_t_ref[...], taken_ref[...])


def first_kernel(
    grid, counts_ref, buf_ref, start_ref, hot_ref, weight_ref, place_ref,
    out_buf_ref, hidden_ref, table_ref, flag_ref, taken_ref,
):
    width = buf_ref.shape[1]
    channels = start_ref.shape[0]
    halo_rows = take_blocks(buf_ref, grid, -1, width).astype(BF16)
    flag_ref[...] = jnp.broadcast_to(halo_rows[:, 96:97].astype(F32), (LANES, LANES))
    halo = nt(eye(LANES), halo_rows)[:channels].astype(BF16)
    table = jnp.concatenate([start_ref[...], halo], axis=1)
    table_ref[...] = table
    hidden = gather_convolve(table, hot_ref, weight_ref, taken_ref)
    hidden_ref[...] = hidden
    valid = valid_lanes(counts_ref)
    count = counts_ref[0].astype(F32)
    sums = jnp.sum(hidden * valid, axis=1, keepdims=True)
    centred = (hidden - sums / count) * valid
    spread = jnp.sum(centred * centred, axis=1, keepdims=True)
    stat = cols_to_rows([sums, spread])
    base = pack_rows(split3(stat[0:1]) + split3(stat[1:2])[:2], count)
    out_buf_ref[...] = jnp.broadcast_to(base.astype(BF16)[None], out_buf_ref.shape)
    rows = pad_to(nt(place_ref[...], centred.astype(BF16)), LANES, LANES)
    put_blocks(out_buf_ref, rows, grid, 1, width, base)


def second_kernel(
    grid, counts_ref, buf_ref, hidden_ref, flag_ref, scale_ref, bias_ref, hot_ref, weight_ref,
    out_buf_ref, hidden_two_ref, table_ref, norm_ref, slope_ref, halo_slope_ref, halo_cross_ref,
    const_ref, mean_ref, taken_ref,
):
    width = buf_ref.shape[1]
    channels = hidden_ref.shape[0]
    tiles = buf_ref[...].astype(F32)
    sums, spreads = unpack_rows(tiles, ((0, 3), (3, 5)))
    counts = tiles[:, 15, 96:97]
    total = jnp.sum(counts, axis=0, keepdims=True)
    means = sums / counts
    mean_ref[...] = means
    mean = jnp.sum(sums, axis=0, keepdims=True) / total
    apart = means - mean
    var = jnp.sum(spreads + counts * apart * apart, axis=0, keepdims=True) / total
    rstd = lax.rsqrt(var + EPS)
    scale = pad_to(scale_ref[...], 1, LANES)
    bias = pad_to(bias_ref[...], 1, LANES)
    total_row = jnp.broadcast_to(total, (1, LANES))
    mean_c, rstd_c, scale_c, bias_c = [c[:channels] for c in rows_to_cols([mean, rstd, scale, bias])]
    sub = iota((8, LANES), 0)
    const_ref[...] = jnp.where(sub == 0, scale * rstd, jnp.where(sub == 1, total_row, 0.0))

    valid = valid_lanes(counts_ref)
    normal = (hidden_ref[...] - mean_c) * rstd_c
    norm_ref[...] = normal
    linear = scale_c * normal + bias_c
    sig = sigmoid(linear)
    slope_ref[...] = sig * (1.0 + linear * (1.0 - sig)) * valid
    act = (linear * sig * valid).astype(BF16)

    place = here()
    lifted = []
    for n, (a, b) in enumerate(STEP_LIST):
        src, inside = neighbour(place, grid, (-a, -b))
        block = buf_ref[src, 0:width, :].astype(F32) + mean_ref[pl.ds(src, 1), :]
        lifted.append(jnp.where(inside, block, 0.0))
    lane = iota((LANES, LANES), 1)
    halo = jnp.where(lane < channels, jnp.concatenate(lifted, axis=0), 0.0)
    flag = flag_ref[...]
    halo_normal = (halo - mean) * rstd
    halo_linear = scale * halo_normal + bias
    halo_sig = sigmoid(halo_linear)
    halo_slope = halo_sig * (1.0 + halo_linear * (1.0 - halo_sig)) * flag
    halo_slope_ref[...] = halo_slope
    halo_cross_ref[...] = halo_slope * halo_normal
    halo_act = nt(eye(LANES), (halo_linear * halo_sig * flag).astype(BF16))[:channels].astype(BF16)

    table = jnp.concatenate([act, halo_act], axis=1)
    table_ref[...] = table
    hidden = gather_convolve(table, hot_ref, weight_ref, taken_ref)
    hidden_two_ref[...] = hidden
    count = counts_ref[0].astype(F32)
    sums_two = jnp.sum(hidden * valid, axis=1, keepdims=True)
    centred = (hidden - sums_two / count) * valid
    spread_two = jnp.sum(centred * centred, axis=1, keepdims=True)
    stat = cols_to_rows([sums_two, spread_two])[0:2]
    stat = jnp.where(iota((2, LANES), 1) < 96, stat, count)
    out_buf_ref[...] = jnp.broadcast_to(stat[None], out_buf_ref.shape)


def third_kernel(
    counts_ref, buf_ref, hidden_ref, start_ref, cotangent_ref, scale_ref, bias_ref,
    out_buf_ref, output_ref, norm_ref, grad_ref, const_ref,
):
    channels = hidden_ref.shape[0]
    sums = buf_ref[:, 0, :]
    spreads = buf_ref[:, 1, :]
    counts = sums[:, 96:97]
    total = jnp.sum(counts, axis=0, keepdims=True)
    mean = jnp.sum(sums, axis=0, keepdims=True) / total
    apart = sums / counts - mean
    var = jnp.sum(spreads + counts * apart * apart, axis=0, keepdims=True) / total
    rstd = lax.rsqrt(var + EPS)
    scale = pad_to(scale_ref[...], 1, LANES)
    bias = pad_to(bias_ref[...], 1, LANES)
    total_row = jnp.broadcast_to(total, (1, LANES))
    mean_c, rstd_c, scale_c, bias_c = [c[:channels] for c in rows_to_cols([mean, rstd, scale, bias])]
    sub = iota((8, LANES), 0)
    const_ref[...] = jnp.where(sub == 0, scale * rstd, jnp.where(sub == 1, total_row, 0.0))
    valid = valid_lanes(counts_ref)
    normal = (hidden_ref[...] - mean_c) * rstd_c
    norm_ref[...] = normal
    summed = scale_c * normal + bias_c + start_ref[...].astype(F32)
    sig = sigmoid(summed)
    output_ref[...] = (summed * sig * valid).astype(BF16)
    grad = cotangent_ref[...].astype(F32) * valid * (sig * (1.0 + summed * (1.0 - sig)))
    grad_ref[...] = grad
    dbias = jnp.sum(grad, axis=1, keepdims=True)
    dgain = jnp.sum(grad * normal * valid, axis=1, keepdims=True)
    rows = cols_to_rows([dgain, dbias])[0:2]
    out_buf_ref[...] = jnp.broadcast_to(rows[None], out_buf_ref.shape)


def scatter(grad, weight_ref, hot_ref):
    channels = grad.shape[0]
    terms = nn(weight_ref[...], grad).astype(BF16)
    offsets = hot_ref.shape[1] // LANES
    wide = jnp.concatenate([terms[k * channels : (k + 1) * channels] for k in range(offsets)], axis=1)
    table = pad_to(nt(hot_ref[...], wide), hot_ref.shape[0], LANES)
    return table[:LANES].T[:channels], table[LANES : 2 * LANES]


def row_gradient(grad, normal, const, dgain, dbias, valid):
    channels = grad.shape[0]
    factor, part_bias, part_gain = rows_to_cols([const[0:1], dbias / const[1:2], dgain / const[1:2]])
    return (
        factor[:channels] * (grad - (part_bias[:channels] + normal * part_gain[:channels])) * valid
    ).astype(BF16)


def fourth_kernel(
    grid, counts_ref, buf_ref, norm_ref, grad_ref, const_ref, weight_ref, hot_ref,
    norm_one_ref, slope_ref, halo_slope_ref, halo_cross_ref,
    out_buf_ref, grad_two_ref, table_ref, sums_ref,
):
    channels = norm_ref.shape[0]
    width = out_buf_ref.shape[1]
    valid = valid_lanes(counts_ref)
    both = jnp.sum(buf_ref[...], axis=0)
    sums_ref[...] = both
    grad = row_gradient(grad_ref[...], norm_ref[...], const_ref[...], both[0:1], both[1:2], valid)
    grad_two_ref[...] = grad
    local, halo = scatter(grad, weight_ref, hot_ref)
    table_ref[...] = local
    pulled = local * slope_ref[...]
    dbias = jnp.sum(pulled, axis=1, keepdims=True)
    dgain = jnp.sum(pulled * norm_one_ref[...], axis=1, keepdims=True)
    rows = cols_to_rows([dgain, dbias])
    dgain = rows[0:1] + jnp.sum(halo * halo_cross_ref[...], axis=0, keepdims=True)
    dbias = rows[1:2] + jnp.sum(halo * halo_slope_ref[...], axis=0, keepdims=True)
    base = pack_rows(split3(dgain)[:2] + split3(dbias)[:2], 0.0)
    out_buf_ref[...] = jnp.broadcast_to(base.astype(BF16)[None], out_buf_ref.shape)
    put_blocks(out_buf_ref, halo, grid, -1, width, base)


def packed_weight_grad(taken_ref, grad, put):
    channels = grad.shape[0]
    zero = jnp.zeros((channels, LANES), BF16)

    def taken(k):
        return taken_ref[k * channels : (k + 1) * channels, :]

    for part in range(3):
        upper = jnp.concatenate([grad, zero], axis=1)
        lower = jnp.concatenate([zero[:32], grad[32 * part : 32 * part + 32]], axis=1)
        right = jnp.concatenate([upper, lower], axis=0)
        left = jnp.concatenate(
            [
                jnp.concatenate([taken(3 * e + part) for e in range(6)], axis=0),
                jnp.concatenate([taken(21 + e) for e in range(6)], axis=0),
            ],
            axis=1,
        )
        result = nt(left, right)
        for e in range(6):
            put(3 * e + part, result[e * channels : (e + 1) * channels])
    last = nt(taken_ref[18 * channels : 21 * channels, :], pad_to(grad, LANES, LANES))
    for e in range(3):
        put(18 + e, last[e * channels : (e + 1) * channels])


def fifth_kernel(
    grid, counts_ref, buf_ref, table_ref, place_ref, norm_ref, slope_ref, const_ref, sums_two_ref,
    table_zero_ref, table_act_ref, hot_ref, grad_two_ref,
    grad_one_ref, give_ref, keep_ref, sums_ref, taken_zero_ref, taken_act_ref,
):
    width = buf_ref.shape[1]
    channels = norm_ref.shape[0]
    valid = valid_lanes(counts_ref)
    dgain, dbias = unpack_rows(
        jnp.sum(buf_ref[...].astype(F32), axis=0, keepdims=True), ((0, 2), (2, 4))
    )
    two = sums_two_ref[...]
    sums_ref[...] = jnp.concatenate([dgain, dbias, two], axis=0)[:, :channels]
    arrived = nt(eye(LANES), take_blocks(buf_ref, grid, 1, width).astype(BF16))[:channels].astype(BF16)
    back = table_ref[...] + nn(arrived, place_ref[...])
    grad = row_gradient(back * slope_ref[...], norm_ref[...], const_ref[...], dgain, dbias, valid)
    grad_one_ref[...] = grad
    gather([table_zero_ref[...], table_act_ref[...]], hot_ref, [taken_zero_ref, taken_act_ref])
    core = lax.axis_index("gy") % 2
    used = 21 * channels

    def store(taken_ref, row_grad, ref):
        def put(block, value):
            ref[block * channels : (block + 1) * channels, :] = value.astype(ref.dtype)

        packed_weight_grad(taken_ref, row_grad, put)
        if ref.shape[0] > used:
            ref[used:, :] = jnp.zeros((ref.shape[0] - used, LANES), ref.dtype)

    @pl.when(core == 0)
    def _():
        store(taken_zero_ref, grad, keep_ref)
        store(taken_act_ref, grad_two_ref[...], give_ref)

    @pl.when(core != 0)
    def _():
        store(taken_zero_ref, grad, give_ref)
        store(taken_act_ref, grad_two_ref[...], keep_ref)


def back_kernel(grad_ref, weight_ref, hot_ref, table_ref, halo_ref):
    local, halo = scatter(grad_ref[...], weight_ref, hot_ref)
    table_ref[...] = local
    halo_ref[...] = halo.astype(BF16)


def sixth_kernel(grid, width, halo_ref, keep_ref, got_ref, out_buf_ref):
    devices, rows = out_buf_ref.shape[0], out_buf_ref.shape[1] - width
    put_blocks(out_buf_ref, halo_ref[...], grid, -1, width)
    total = (keep_ref[...] + got_ref[...].astype(F32)).astype(BF16)
    out_buf_ref[:, width:, :] = total.reshape(devices, rows, LANES)


def seventh_kernel(grid, width, counts_ref, buf_ref, table_ref, place_ref, grad_ref, out_buf_ref, out_ref):
    channels = table_ref.shape[0]
    devices, rows = buf_ref.shape[0], buf_ref.shape[1] - width
    valid = valid_lanes(counts_ref)
    arrived = nt(eye(LANES), take_blocks(buf_ref, grid, 1, width).astype(BF16))[:channels].astype(BF16)
    back = table_ref[...] + nn(arrived, place_ref[...])
    out_ref[...] = ((back + grad_ref[...]) * valid).astype(BF16)
    pieces = []
    for core in range(2):
        total = jnp.zeros((rows, LANES), F32)
        for d in range(core, devices, 2):
            total = total + buf_ref[d, width:, :].astype(F32)
        pieces.append(total.astype(BF16))
    for d in range(devices):
        out_buf_ref[d] = pieces[d % 2]


def unpack(src_ref, out_hbm, block_ref, sems):
    channels = block_ref.shape[1]
    lane = iota((channels, LANES), 1)
    copies = []

    def send(first, count):
        part = pl.ds(first, count)
        copies.append(pltpu.make_async_copy(block_ref.at[part], out_hbm.at[part], sems.at[len(copies)]))
        copies[-1].start()

    for e in range(7):
        extra = jnp.zeros((channels, LANES), F32)
        for part in range(3):
            block = 3 * e + part
            value = src_ref[block * channels : (block + 1) * channels, :].astype(F32)
            block_ref[block] = value[:, :channels]
            if e < 6:
                moved = pltpu.roll(value, 32 * (part + 1), 1)
                extra = jnp.where(lane // 32 == part, moved, extra)
        send(3 * e, 3)
        if e < 6:
            block_ref[21 + e] = extra[:, :channels]
            send(21 + e, 1)
    for copy in copies:
        copy.wait()


def own_kernel(own_ref, small_in, more_in, sums_in, one_hbm, two_hbm, small_out, more_out, sums_out, block_ref, sems):
    core = lax.axis_index("gy") % 2
    small_out[...] = small_in[...]
    more_out[...] = more_in[...]
    sums_out[...] = sums_in[...]

    @pl.when(core == 0)
    def _():
        unpack(own_ref, one_hbm, block_ref, sems)

    @pl.when(core != 0)
    def _():
        unpack(own_ref, two_hbm, block_ref, sems)


def other_kernel(other_ref, one_in, two_in, one_hbm, two_hbm, block_ref, sems):
    core = lax.axis_index("gy") % 2

    @pl.when(core == 0)
    def _():
        unpack(other_ref, two_hbm, block_ref, sems)

    @pl.when(core != 0)
    def _():
        unpack(other_ref, one_hbm, block_ref, sems)


def call(kernel, outs, *args, smem=0, scratch=(), hbm=(), hbm_outs=(), aliases=None):
    def space(at):
        if at in hbm:
            return pltpu.HBM
        return pltpu.SMEM if at < smem else pltpu.VMEM

    args = [pltpu.with_memory_space_constraint(x, pltpu.HBM) if at in hbm else x for at, x in enumerate(args)]
    shapes = tuple(jax.ShapeDtypeStruct(shape, dtype) for shape, dtype in outs)
    return pl.pallas_call(
        kernel,
        out_shape=shapes,
        in_specs=[pl.BlockSpec(memory_space=space(at)) for at in range(len(args))],
        out_specs=tuple(
            pl.BlockSpec(memory_space=pltpu.HBM if at in hbm_outs else pltpu.VMEM) for at in range(len(shapes))
        ),
        scratch_shapes=list(scratch),
        input_output_aliases=aliases or {},
        compiler_params=pltpu.CompilerParams(vmem_limit_bytes=40 * 1024 * 1024),
    )(*args)


def to_all(x):
    return lax.all_to_all(x, AXES, 0, 0)


def swap_core(x):
    size = lax.axis_size("gy")
    return lax.ppermute(x, "gy", [(i, i ^ 1) for i in range(size)])


def on_device(
    features, kernel_map, send_rows, counts, weight_one, weight_two,
    first_norm_scale, first_norm_bias, second_norm_scale, second_norm_bias, cotangent,
):
    channels, rows = features.shape
    offsets = kernel_map.shape[0]
    width = send_rows.shape[1]
    grid = (lax.axis_size("gx"), lax.axis_size("gy"))
    devices = grid[0] * grid[1]
    flat = offsets * channels
    table = rows + 8 * width
    piece = -(-21 * channels // (devices * 16)) * 16
    packed = piece * devices
    full = (channels, rows)
    square = (LANES, LANES)
    one_flat = weight_one.reshape(flat, channels)
    two_flat = weight_two.reshape(flat, channels)
    scale_one, bias_one, scale_two, bias_two = [
        v.reshape(1, channels)
        for v in (first_norm_scale, first_norm_bias, second_norm_scale, second_norm_bias)
    ]

    taken = pltpu.VMEM((flat, LANES), BF16)
    wide = ((channels, table), BF16)
    buf, start, place = call(
        functools.partial(open_kernel, grid),
        [((devices, width, LANES), BF16), (full, BF16), (square, BF16)],
        counts, features, send_rows, smem=1, hbm=(1, 2),
        scratch=[
            pltpu.VMEM(full, BF16), pltpu.VMEM(send_rows.shape, jnp.int32), pltpu.SemaphoreType.DMA((2,)),
        ],
    )
    buf = to_all(buf)
    hot, one_t, two_t = call(
        prepare_kernel,
        [
            ((table, offsets * LANES), BF16),
            ((channels, flat), BF16), ((channels, flat), BF16),
        ],
        kernel_map, one_flat, two_flat, hbm=(0, 1, 2),
        scratch=[
            pltpu.VMEM(kernel_map.shape, jnp.int32), pltpu.VMEM((flat, channels), BF16),
            pltpu.VMEM((flat, channels), BF16), pltpu.SemaphoreType.DMA((3,)),
        ],
    )
    buf, hidden_one, table_zero, flag = call(
        functools.partial(first_kernel, grid),
        [((devices, width, LANES), BF16), (full, F32), wide, (square, F32)],
        counts, buf, start, hot, one_t, place, smem=1, scratch=[taken],
    )
    buf = to_all(buf)
    buf, hidden_two, table_act, norm_one, slope_one, halo_slope, halo_cross, const_one = call(
        functools.partial(second_kernel, grid),
        [
            ((devices, 2, LANES), F32), (full, F32), wide, (full, F32), (full, F32),
            (square, F32), (square, F32), ((8, LANES), F32),
        ],
        counts, buf, hidden_one, flag, scale_one, bias_one, hot, two_t,
        smem=1, scratch=[pltpu.VMEM((devices, LANES), F32), taken],
    )
    buf = to_all(buf)
    buf, output, norm_two, grad_sum, const_two = call(
        third_kernel,
        [((devices, 2, LANES), F32), (full, BF16), (full, F32), (full, F32), ((8, LANES), F32)],
        counts, buf, hidden_two, start, cotangent, scale_two, bias_two, smem=1,
    )
    buf = to_all(buf)
    buf, grad_two, table_two, sums_two = call(
        functools.partial(fourth_kernel, grid),
        [((devices, width, LANES), BF16), (full, BF16), (full, F32), ((2, LANES), F32)],
        counts, buf, norm_two, grad_sum, const_two, two_flat, hot, norm_one, slope_one, halo_slope, halo_cross,
        smem=1,
    )
    buf = to_all(buf)
    grad_one, give, keep, grad_norms = call(
        functools.partial(fifth_kernel, grid),
        [(full, BF16), ((packed, LANES), BF16), ((packed, LANES), F32), ((4, channels), F32)],
        counts, buf, table_two, place, norm_one, slope_one, const_one, sums_two,
        table_zero, table_act, hot, grad_two, smem=1, scratch=[taken, taken],
    )
    got = swap_core(give)
    table_one, halo_one = call(
        back_kernel, [(full, F32), (square, BF16)], grad_one, one_flat, hot
    )
    (buf,) = call(
        functools.partial(sixth_kernel, grid, width),
        [((devices, width + piece, LANES), BF16)],
        halo_one, keep, got,
    )
    buf = to_all(buf)
    buf, grad_features = call(
        functools.partial(seventh_kernel, grid, width),
        [((devices, piece, LANES), BF16), (full, BF16)],
        counts, buf, table_one, place, grad_sum, smem=1,
    )
    own = to_all(buf).reshape(packed, LANES)
    other = swap_core(own)
    weights = [(weight_one.shape, F32), (weight_two.shape, F32)]
    blocks = [pltpu.VMEM(weight_one.shape, F32), pltpu.SemaphoreType.DMA((13,))]
    grad_weight_one, grad_weight_two, output, grad_features, grad_norms = call(
        own_kernel,
        weights + [(full, BF16), (full, BF16), ((4, channels), F32)],
        own, output, grad_features, grad_norms, hbm_outs=(0, 1), scratch=blocks,
    )
    grad_weight_one, grad_weight_two = call(
        other_kernel, weights, other, grad_weight_one, grad_weight_two,
        hbm=(1, 2), hbm_outs=(0, 1), scratch=blocks, aliases={1: 0, 2: 1},
    )
    return (output, grad_features, grad_weight_one, grad_weight_two, grad_norms)


def solution(mesh):
    return jax.shard_map(
        on_device,
        mesh=mesh,
        in_specs=(
            P(None, ("gx", "gy")),
            P(None, ("gx", "gy")),
            P(None, ("gx", "gy")),
            P(("gx", "gy")),
            P(),
            P(),
            P(),
            P(),
            P(),
            P(),
            P(None, ("gx", "gy")),
        ),
        out_specs=(P(None, ("gx", "gy")), P(None, ("gx", "gy")), P(), P(), P()),
        check_vma=False,
    )
```

```python
import functools

import jax
import jax.numpy as jnp
from jax import lax
from jax.experimental import pallas as pl
from jax.experimental.pallas import tpu as pltpu
from jax.sharding import PartitionSpec as P

EPS = 1e-05
STEP_LIST = ((1, 0), (-1, 0), (0, 1), (0, -1), (1, 1), (1, -1), (-1, 1), (-1, -1))
AXES = ("gx", "gy")
LANES = 128
F32 = jnp.float32
BF16 = jnp.bfloat16


def nn(a, b):
    return lax.dot_general(a, b, (((1,), (0,)), ((), ())), preferred_element_type=F32)


def nt(a, b):
    return lax.dot_general(a, b, (((1,), (1,)), ((), ())), preferred_element_type=F32)


def iota(shape, dim):
    return lax.broadcasted_iota(jnp.int32, shape, dim)


def eye(size):
    return jnp.where(iota((size, size), 0) == iota((size, size), 1), 1.0, 0.0).astype(BF16)


def sigmoid(v):
    return 1.0 / (1.0 + jnp.exp(-v))


def neighbour(place, grid, step):
    i, j = place[0] + step[0], place[1] + step[1]
    inside = (i >= 0) & (i < grid[0]) & (j >= 0) & (j < grid[1])
    return jnp.where(inside, i * grid[1] + j, place[0] * grid[1] + place[1]), inside


def here():
    return lax.axis_index("gx"), lax.axis_index("gy")


def put_blocks(buf_ref, rows, grid, sign, width, base=None):
    place = here()
    for n, (a, b) in enumerate(STEP_LIST):
        dest, _ = neighbour(place, grid, (sign * a, sign * b))
        block = rows[n * width : (n + 1) * width]
        if base is not None:
            block = jnp.where(iota(block.shape, 1) < 96, block, base)
        buf_ref[dest, 0:width, :] = block.astype(BF16)


def take_blocks(buf_ref, grid, sign, width):
    place = here()
    blocks = []
    for a, b in STEP_LIST:
        src, inside = neighbour(place, grid, (sign * a, sign * b))
        block = buf_ref[src, 0:width, :].astype(F32)
        blocks.append(jnp.where(inside, block, 0.0))
    return jnp.concatenate(blocks, axis=0)


def pad_to(x, rows, lanes):
    if x.shape[1] < lanes:
        x = jnp.concatenate([x, jnp.zeros((x.shape[0], lanes - x.shape[1]), x.dtype)], axis=1)
    if x.shape[0] < rows:
        x = jnp.concatenate([x, jnp.zeros((rows - x.shape[0], lanes), x.dtype)], axis=0)
    return x


def cols_to_rows(cols):
    lane = iota((cols[0].shape[0], LANES), 1)
    total = jnp.zeros((cols[0].shape[0], LANES), F32)
    for at, col in enumerate(cols):
        total = jnp.where(lane == at, col, total)
    return pad_to(total, LANES, LANES).T


def rows_to_cols(rows):
    sub = iota((LANES, LANES), 0)
    total = jnp.zeros((LANES, LANES), F32)
    for at, row in enumerate(rows):
        total = jnp.where(sub == at, row, total)
    total = total.T
    return [total[:, at : at + 1] for at in range(len(rows))]


def split3(x):
    high = x.astype(BF16).astype(F32)
    mid = (x - high).astype(BF16).astype(F32)
    low = (x - high - mid).astype(BF16).astype(F32)
    return [high, mid, low]


def pack_rows(pieces, last):
    sub = iota((16, LANES), 0)
    lane = iota((16, LANES), 1)
    total = jnp.zeros((16, LANES), F32)
    for q, piece in enumerate(pieces):
        total = jnp.where(sub // 3 == q, piece, total)
    part = sub % 3
    moved = jnp.where(
        part == 0,
        pltpu.roll(total, 96, 1),
        jnp.where(part == 1, pltpu.roll(total, 64, 1), pltpu.roll(total, 32, 1)),
    )
    moved = jnp.where(sub == 15, last, moved)
    return jnp.where(lane >= 96, moved, 0.0)


def unpack_rows(tiles, groups):
    devices = tiles.shape[0]
    flat = tiles.reshape(devices * 16, LANES)
    sub = iota(tiles.shape, 1)
    lane = iota(tiles.shape, 2)
    part = sub % 3
    moved = [pltpu.roll(flat, 32 * (p + 1), 1).reshape(tiles.shape) for p in range(3)]
    value = jnp.where(part == 0, moved[0], jnp.where(part == 1, moved[1], moved[2]))
    value = jnp.where((lane // 32 == part) & (sub < 15), value, 0.0)
    results = []
    for low, high in groups:
        mask = (sub >= 3 * low) & (sub < 3 * high)
        results.append(jnp.sum(jnp.where(mask, value, 0.0), axis=1))
    return results


def valid_lanes(counts_ref, rows=1):
    return (iota((rows, LANES), 1) < counts_ref[0]).astype(F32)


def open_kernel(
    grid, counts_ref, features_hbm, send_hbm, buf_ref, start_ref, place_ref, features_ref, send_ref, sems
):
    copies = [
        pltpu.make_async_copy(features_hbm, features_ref, sems.at[0]),
        pltpu.make_async_copy(send_hbm, send_ref, sems.at[1]),
    ]
    for copy in copies:
        copy.start()
    for copy in copies:
        copy.wait()
    width = send_ref.shape[1]
    send = send_ref[...].astype(F32).astype(BF16)
    spread = jnp.where(iota((width, LANES), 1) % width == iota((width, LANES), 0), 1.0, 0.0).astype(BF16)
    wide = nn(send, spread)
    wide = jnp.where(iota(wide.shape, 1) // width == iota(wide.shape, 0), wide, 0.0)
    row = jnp.sum(wide, axis=0, keepdims=True)
    place = jnp.where(row == iota((LANES, LANES), 0).astype(F32), 1.0, 0.0).T.astype(BF16)
    place_ref[...] = place
    valid = valid_lanes(counts_ref)
    start = features_ref[...].astype(F32) * valid
    start_ref[...] = start.astype(BF16)
    extra = jnp.where(iota((LANES - 96, LANES), 0) == 0, valid, 0.0)
    rows = nt(place, jnp.concatenate([start, extra], axis=0).astype(BF16))
    put_blocks(buf_ref, rows, grid, 1, width)


def prepare_kernel(
    map_hbm, one_hbm, two_hbm, hot_ref, one_t_ref, two_t_ref, map_ref, one_ref, two_ref, sems
):
    pairs = ((map_hbm, map_ref), (one_hbm, one_ref), (two_hbm, two_ref))
    copies = [pltpu.make_async_copy(src, dst, sems.at[at]) for at, (src, dst) in enumerate(pairs)]
    for copy in copies:
        copy.start()
    copies[0].wait()
    table = hot_ref.shape[0]
    sub = iota((table, LANES), 0)
    for k in range(map_ref.shape[0]):
        part = slice(k * LANES, (k + 1) * LANES)
        hot_ref[:, part] = jnp.where(sub == map_ref[k : k + 1, :], 1.0, 0.0).astype(BF16)
    unit = eye(one_ref.shape[1])
    copies[1].wait()
    one_t_ref[...] = nt(unit, one_ref[...]).astype(BF16)
    copies[2].wait()
    two_t_ref[...] = nt(unit, two_ref[...]).astype(BF16)


def gather(tables, hot_ref, taken_refs):
    channels = tables[0].shape[0]
    taken = nn(jnp.concatenate(tables, axis=0), hot_ref[...]).astype(BF16)
    for at, ref in enumerate(taken_refs):
        for k in range(hot_ref.shape[1] // LANES):
            ref[k * channels : (k + 1) * channels, :] = taken[
                at * channels : (at + 1) * channels, k * LANES : (k + 1) * LANES
            ]


def gather_convolve(table, hot_ref, weight_t_ref, taken_ref):
    gather([table], hot_ref, [taken_ref])
    return nn(weight_t_ref[...], taken_ref[...])


def first_kernel(
    grid, counts_ref, buf_ref, start_ref, hot_ref, weight_ref, place_ref,
    out_buf_ref, hidden_ref, taken_ref, flag_ref,
):
    width = buf_ref.shape[1]
    channels = start_ref.shape[0]
    halo_rows = take_blocks(buf_ref, grid, -1, width).astype(BF16)
    flag_ref[...] = jnp.broadcast_to(halo_rows[:, 96:97].astype(F32), (LANES, LANES))
    halo = nt(eye(LANES), halo_rows)[:channels].astype(BF16)
    table = jnp.concatenate([start_ref[...], halo], axis=1)
    hidden = gather_convolve(table, hot_ref, weight_ref, taken_ref)
    hidden_ref[...] = hidden
    valid = valid_lanes(counts_ref)
    count = counts_ref[0].astype(F32)
    sums = jnp.sum(hidden * valid, axis=1, keepdims=True)
    centred = (hidden - sums / count) * valid
    spread = jnp.sum(centred * centred, axis=1, keepdims=True)
    stat = cols_to_rows([sums, spread])
    base = pack_rows(split3(stat[0:1]) + split3(stat[1:2])[:2], count)
    out_buf_ref[...] = jnp.broadcast_to(base.astype(BF16)[None], out_buf_ref.shape)
    rows = pad_to(nt(place_ref[...], centred.astype(BF16)), LANES, LANES)
    put_blocks(out_buf_ref, rows, grid, 1, width, base)


def second_kernel(
    grid, counts_ref, buf_ref, hidden_ref, flag_ref, scale_ref, bias_ref, hot_ref, weight_ref,
    out_buf_ref, hidden_two_ref, taken_ref, norm_ref, slope_ref, halo_slope_ref, halo_cross_ref,
    const_ref, mean_ref,
):
    width = buf_ref.shape[1]
    channels = hidden_ref.shape[0]
    tiles = buf_ref[...].astype(F32)
    sums, spreads = unpack_rows(tiles, ((0, 3), (3, 5)))
    counts = tiles[:, 15, 96:97]
    total = jnp.sum(counts, axis=0, keepdims=True)
    means = sums / counts
    mean_ref[...] = means
    mean = jnp.sum(sums, axis=0, keepdims=True) / total
    apart = means - mean
    var = jnp.sum(spreads + counts * apart * apart, axis=0, keepdims=True) / total
    rstd = lax.rsqrt(var + EPS)
    scale = pad_to(scale_ref[...], 1, LANES)
    bias = pad_to(bias_ref[...], 1, LANES)
    total_row = jnp.broadcast_to(total, (1, LANES))
    mean_c, rstd_c, scale_c, bias_c = [c[:channels] for c in rows_to_cols([mean, rstd, scale, bias])]
    sub = iota((8, LANES), 0)
    const_ref[...] = jnp.where(sub == 0, scale * rstd, jnp.where(sub == 1, total_row, 0.0))

    valid = valid_lanes(counts_ref)
    normal = (hidden_ref[...] - mean_c) * rstd_c
    norm_ref[...] = normal
    linear = scale_c * normal + bias_c
    sig = sigmoid(linear)
    slope_ref[...] = sig * (1.0 + linear * (1.0 - sig)) * valid
    act = (linear * sig * valid).astype(BF16)

    place = here()
    lifted = []
    for n, (a, b) in enumerate(STEP_LIST):
        src, inside = neighbour(place, grid, (-a, -b))
        block = buf_ref[src, 0:width, :].astype(F32) + mean_ref[pl.ds(src, 1), :]
        lifted.append(jnp.where(inside, block, 0.0))
    lane = iota((LANES, LANES), 1)
    halo = jnp.where(lane < channels, jnp.concatenate(lifted, axis=0), 0.0)
    flag = flag_ref[...]
    halo_normal = (halo - mean) * rstd
    halo_linear = scale * halo_normal + bias
    halo_sig = sigmoid(halo_linear)
    halo_slope = halo_sig * (1.0 + halo_linear * (1.0 - halo_sig)) * flag
    halo_slope_ref[...] = halo_slope
    halo_cross_ref[...] = halo_slope * halo_normal
    halo_act = nt(eye(LANES), (halo_linear * halo_sig * flag).astype(BF16))[:channels].astype(BF16)

    table = jnp.concatenate([act, halo_act], axis=1)
    hidden = gather_convolve(table, hot_ref, weight_ref, taken_ref)
    hidden_two_ref[...] = hidden
    count = counts_ref[0].astype(F32)
    sums_two = jnp.sum(hidden * valid, axis=1, keepdims=True)
    centred = (hidden - sums_two / count) * valid
    spread_two = jnp.sum(centred * centred, axis=1, keepdims=True)
    stat = cols_to_rows([sums_two, spread_two])[0:2]
    stat = jnp.where(iota((2, LANES), 1) < 96, stat, count)
    out_buf_ref[...] = jnp.broadcast_to(stat[None], out_buf_ref.shape)


def third_kernel(
    counts_ref, buf_ref, hidden_ref, start_ref, cotangent_ref, scale_ref, bias_ref,
    out_buf_ref, output_ref, norm_ref, grad_ref, const_ref,
):
    channels = hidden_ref.shape[0]
    sums = buf_ref[:, 0, :]
    spreads = buf_ref[:, 1, :]
    counts = sums[:, 96:97]
    total = jnp.sum(counts, axis=0, keepdims=True)
    mean = jnp.sum(sums, axis=0, keepdims=True) / total
    apart = sums / counts - mean
    var = jnp.sum(spreads + counts * apart * apart, axis=0, keepdims=True) / total
    rstd = lax.rsqrt(var + EPS)
    scale = pad_to(scale_ref[...], 1, LANES)
    bias = pad_to(bias_ref[...], 1, LANES)
    total_row = jnp.broadcast_to(total, (1, LANES))
    mean_c, rstd_c, scale_c, bias_c = [c[:channels] for c in rows_to_cols([mean, rstd, scale, bias])]
    sub = iota((8, LANES), 0)
    const_ref[...] = jnp.where(sub == 0, scale * rstd, jnp.where(sub == 1, total_row, 0.0))
    valid = valid_lanes(counts_ref)
    normal = (hidden_ref[...] - mean_c) * rstd_c
    norm_ref[...] = normal
    summed = scale_c * normal + bias_c + start_ref[...].astype(F32)
    sig = sigmoid(summed)
    output_ref[...] = (summed * sig * valid).astype(BF16)
    grad = cotangent_ref[...].astype(F32) * valid * (sig * (1.0 + summed * (1.0 - sig)))
    grad_ref[...] = grad
    dbias = jnp.sum(grad, axis=1, keepdims=True)
    dgain = jnp.sum(grad * normal * valid, axis=1, keepdims=True)
    rows = cols_to_rows([dgain, dbias])[0:2]
    out_buf_ref[...] = jnp.broadcast_to(rows[None], out_buf_ref.shape)


def scatter(grad, weight_ref, hot_ref):
    channels = grad.shape[0]
    terms = nn(weight_ref[...], grad).astype(BF16)
    offsets = hot_ref.shape[1] // LANES
    wide = jnp.concatenate([terms[k * channels : (k + 1) * channels] for k in range(offsets)], axis=1)
    table = pad_to(nt(hot_ref[...], wide), hot_ref.shape[0], LANES)
    return table[:LANES].T[:channels], table[LANES : 2 * LANES]


def row_gradient(grad, normal, const, dgain, dbias, valid):
    channels = grad.shape[0]
    factor, part_bias, part_gain = rows_to_cols([const[0:1], dbias / const[1:2], dgain / const[1:2]])
    return (
        factor[:channels] * (grad - (part_bias[:channels] + normal * part_gain[:channels])) * valid
    ).astype(BF16)


def fourth_kernel(
    grid, counts_ref, buf_ref, norm_ref, grad_ref, const_ref, weight_ref, hot_ref,
    norm_one_ref, slope_ref, halo_slope_ref, halo_cross_ref,
    out_buf_ref, grad_two_ref, table_ref, sums_ref,
):
    channels = norm_ref.shape[0]
    width = out_buf_ref.shape[1]
    valid = valid_lanes(counts_ref)
    both = jnp.sum(buf_ref[...], axis=0)
    sums_ref[...] = both
    grad = row_gradient(grad_ref[...], norm_ref[...], const_ref[...], both[0:1], both[1:2], valid)
    grad_two_ref[...] = grad
    local, halo = scatter(grad, weight_ref, hot_ref)
    table_ref[...] = local
    pulled = local * slope_ref[...]
    dbias = jnp.sum(pulled, axis=1, keepdims=True)
    dgain = jnp.sum(pulled * norm_one_ref[...], axis=1, keepdims=True)
    rows = cols_to_rows([dgain, dbias])
    dgain = rows[0:1] + jnp.sum(halo * halo_cross_ref[...], axis=0, keepdims=True)
    dbias = rows[1:2] + jnp.sum(halo * halo_slope_ref[...], axis=0, keepdims=True)
    base = pack_rows(split3(dgain)[:2] + split3(dbias)[:2], 0.0)
    out_buf_ref[...] = jnp.broadcast_to(base.astype(BF16)[None], out_buf_ref.shape)
    put_blocks(out_buf_ref, halo, grid, -1, width, base)


def packed_weight_grad(taken_ref, grad, put):
    channels = grad.shape[0]
    zero = jnp.zeros((channels, LANES), BF16)

    def taken(k):
        return taken_ref[k * channels : (k + 1) * channels, :]

    for part in range(3):
        upper = jnp.concatenate([grad, zero], axis=1)
        lower = jnp.concatenate([zero[:32], grad[32 * part : 32 * part + 32]], axis=1)
        right = jnp.concatenate([upper, lower], axis=0)
        left = jnp.concatenate(
            [
                jnp.concatenate([taken(3 * e + part) for e in range(6)], axis=0),
                jnp.concatenate([taken(21 + e) for e in range(6)], axis=0),
            ],
            axis=1,
        )
        result = nt(left, right)
        for e in range(6):
            put(3 * e + part, result[e * channels : (e + 1) * channels])
    last = nt(taken_ref[18 * channels : 21 * channels, :], pad_to(grad, LANES, LANES))
    for e in range(3):
        put(18 + e, last[e * channels : (e + 1) * channels])


def store_packed(taken_ref, grad, ref):
    channels = grad.shape[0]
    used = 21 * channels

    def put(block, value):
        ref[block * channels : (block + 1) * channels, :] = value.astype(ref.dtype)

    packed_weight_grad(taken_ref, grad, put)
    if ref.shape[0] > used:
        ref[used:, :] = jnp.zeros((ref.shape[0] - used, LANES), ref.dtype)


def fifth_kernel(
    grid, counts_ref, buf_ref, table_ref, place_ref, norm_ref, slope_ref, const_ref, sums_two_ref,
    taken_zero_ref, taken_act_ref, grad_two_ref,
    grad_one_ref, give_ref, sums_ref,
):
    width = buf_ref.shape[1]
    channels = norm_ref.shape[0]
    valid = valid_lanes(counts_ref)
    dgain, dbias = unpack_rows(
        jnp.sum(buf_ref[...].astype(F32), axis=0, keepdims=True), ((0, 2), (2, 4))
    )
    two = sums_two_ref[...]
    sums_ref[...] = jnp.concatenate([dgain, dbias, two], axis=0)[:, :channels]
    arrived = nt(eye(LANES), take_blocks(buf_ref, grid, 1, width).astype(BF16))[:channels].astype(BF16)
    back = table_ref[...] + nn(arrived, place_ref[...])
    grad = row_gradient(back * slope_ref[...], norm_ref[...], const_ref[...], dgain, dbias, valid)
    grad_one_ref[...] = grad
    core = lax.axis_index("gy") % 2

    @pl.when(core == 0)
    def _():
        store_packed(taken_act_ref, grad_two_ref[...], give_ref)

    @pl.when(core != 0)
    def _():
        store_packed(taken_zero_ref, grad, give_ref)


def back_kernel(
    grad_ref, weight_ref, hot_ref, taken_zero_ref, taken_act_ref, grad_two_ref, table_ref, halo_ref, keep_ref
):
    core = lax.axis_index("gy") % 2

    @pl.when(core == 0)
    def _():
        store_packed(taken_zero_ref, grad_ref[...], keep_ref)

    @pl.when(core != 0)
    def _():
        store_packed(taken_act_ref, grad_two_ref[...], keep_ref)

    local, halo = scatter(grad_ref[...], weight_ref, hot_ref)
    table_ref[...] = local
    halo_ref[...] = halo.astype(BF16)


def sixth_kernel(grid, width, halo_ref, keep_ref, got_ref, out_buf_ref):
    devices, rows = out_buf_ref.shape[0], out_buf_ref.shape[1] - width
    put_blocks(out_buf_ref, halo_ref[...], grid, -1, width)
    total = (keep_ref[...] + got_ref[...].astype(F32)).astype(BF16)
    out_buf_ref[:, width:, :] = total.reshape(devices, rows, LANES)


def seventh_kernel(grid, width, counts_ref, buf_ref, table_ref, place_ref, grad_ref, out_buf_ref, out_ref):
    channels = table_ref.shape[0]
    devices, rows = buf_ref.shape[0], buf_ref.shape[1] - width
    valid = valid_lanes(counts_ref)
    arrived = nt(eye(LANES), take_blocks(buf_ref, grid, 1, width).astype(BF16))[:channels].astype(BF16)
    back = table_ref[...] + nn(arrived, place_ref[...])
    out_ref[...] = ((back + grad_ref[...]) * valid).astype(BF16)
    pieces = []
    for core in range(2):
        total = jnp.zeros((rows, LANES), F32)
        for d in range(core, devices, 2):
            total = total + buf_ref[d, width:, :].astype(F32)
        pieces.append(total.astype(BF16))
    for d in range(devices):
        out_buf_ref[d] = pieces[d % 2]


def unpack(src_ref, out_hbm, block_ref, sems):
    channels = block_ref.shape[1]
    lane = iota((channels, LANES), 1)
    copies = []

    def send(first, count):
        part = pl.ds(first, count)
        copies.append(pltpu.make_async_copy(block_ref.at[part], out_hbm.at[part], sems.at[len(copies)]))
        copies[-1].start()

    for e in range(7):
        extra = jnp.zeros((channels, LANES), F32)
        for part in range(3):
            block = 3 * e + part
            value = src_ref[block * channels : (block + 1) * channels, :].astype(F32)
            block_ref[block] = value[:, :channels]
            if e < 6:
                moved = pltpu.roll(value, 32 * (part + 1), 1)
                extra = jnp.where(lane // 32 == part, moved, extra)
        send(3 * e, 3)
        if e < 6:
            block_ref[21 + e] = extra[:, :channels]
            send(21 + e, 1)
    for copy in copies:
        copy.wait()


def own_kernel(own_ref, small_in, more_in, sums_in, one_hbm, two_hbm, small_out, more_out, sums_out, block_ref, sems):
    core = lax.axis_index("gy") % 2
    small_out[...] = small_in[...]
    more_out[...] = more_in[...]
    sums_out[...] = sums_in[...]

    @pl.when(core == 0)
    def _():
        unpack(own_ref, one_hbm, block_ref, sems)

    @pl.when(core != 0)
    def _():
        unpack(own_ref, two_hbm, block_ref, sems)


def other_kernel(other_ref, one_in, two_in, one_hbm, two_hbm, block_ref, sems):
    core = lax.axis_index("gy") % 2

    @pl.when(core == 0)
    def _():
        unpack(other_ref, two_hbm, block_ref, sems)

    @pl.when(core != 0)
    def _():
        unpack(other_ref, one_hbm, block_ref, sems)


def call(kernel, outs, *args, smem=0, scratch=(), hbm=(), hbm_outs=(), aliases=None, carry=()):
    n_in, n_out = len(args), len(outs)
    aliases = dict(aliases or {})
    aliases.update({n_in + at: n_out + at for at in range(len(carry))})

    def space(at):
        if at >= n_in:
            return pl.ANY
        if at in hbm:
            return pltpu.HBM
        return pltpu.SMEM if at < smem else pltpu.VMEM

    def out_space(at):
        if at >= n_out:
            return pl.ANY
        return pltpu.HBM if at in hbm_outs else pltpu.VMEM

    def body(*refs):
        first_out = n_in + len(carry)
        kernel(*refs[:n_in], *refs[first_out : first_out + n_out], *refs[first_out + n_out + len(carry) :])

    args = [pltpu.with_memory_space_constraint(x, pltpu.HBM) if at in hbm else x for at, x in enumerate(args)]
    outs = list(outs) + [(x.shape, x.dtype) for x in carry]
    return pl.pallas_call(
        body,
        out_shape=tuple(jax.ShapeDtypeStruct(shape, dtype) for shape, dtype in outs),
        in_specs=[pl.BlockSpec(memory_space=space(at)) for at in range(n_in + len(carry))],
        out_specs=tuple(pl.BlockSpec(memory_space=out_space(at)) for at in range(len(outs))),
        scratch_shapes=list(scratch),
        input_output_aliases=aliases,
        compiler_params=pltpu.CompilerParams(vmem_limit_bytes=40 * 1024 * 1024),
    )(*args, *carry)


def to_all(x):
    return lax.all_to_all(x, AXES, 0, 0)


def swap_core(x):
    size = lax.axis_size("gy")
    return lax.ppermute(x, "gy", [(i, i ^ 1) for i in range(size)])


def on_device(
    features, kernel_map, send_rows, counts, weight_one, weight_two,
    first_norm_scale, first_norm_bias, second_norm_scale, second_norm_bias, cotangent,
):
    channels, rows = features.shape
    offsets = kernel_map.shape[0]
    width = send_rows.shape[1]
    grid = (lax.axis_size("gx"), lax.axis_size("gy"))
    devices = grid[0] * grid[1]
    flat = offsets * channels
    table = rows + 8 * width
    piece = -(-21 * channels // (devices * 16)) * 16
    packed = piece * devices
    full = (channels, rows)
    square = (LANES, LANES)
    one_flat = weight_one.reshape(flat, channels)
    two_flat = weight_two.reshape(flat, channels)
    scale_one, bias_one, scale_two, bias_two = [
        v.reshape(1, channels)
        for v in (first_norm_scale, first_norm_bias, second_norm_scale, second_norm_bias)
    ]

    taken = ((flat, LANES), BF16)
    buf, start, place = call(
        functools.partial(open_kernel, grid),
        [((devices, width, LANES), BF16), (full, BF16), (square, BF16)],
        counts, features, send_rows, smem=1, hbm=(1, 2),
        scratch=[
            pltpu.VMEM(full, BF16), pltpu.VMEM(send_rows.shape, jnp.int32), pltpu.SemaphoreType.DMA((2,)),
        ],
    )
    buf = to_all(buf)
    hot, one_t, two_t = call(
        prepare_kernel,
        [
            ((table, offsets * LANES), BF16),
            ((channels, flat), BF16), ((channels, flat), BF16),
        ],
        kernel_map, one_flat, two_flat, hbm=(0, 1, 2),
        scratch=[
            pltpu.VMEM(kernel_map.shape, jnp.int32), pltpu.VMEM((flat, channels), BF16),
            pltpu.VMEM((flat, channels), BF16), pltpu.SemaphoreType.DMA((3,)),
        ],
    )
    buf, hidden_one, taken_zero, flag = call(
        functools.partial(first_kernel, grid),
        [((devices, width, LANES), BF16), (full, F32), taken, (square, F32)],
        counts, buf, start, hot, one_t, place, smem=1,
    )
    buf = to_all(buf)
    buf, hidden_two, taken_act, norm_one, slope_one, halo_slope, halo_cross, const_one, taken_zero = call(
        functools.partial(second_kernel, grid),
        [
            ((devices, 2, LANES), F32), (full, F32), taken, (full, F32), (full, F32),
            (square, F32), (square, F32), ((8, LANES), F32),
        ],
        counts, buf, hidden_one, flag, scale_one, bias_one, hot, two_t,
        smem=1, scratch=[pltpu.VMEM((devices, LANES), F32)], carry=[taken_zero],
    )
    buf = to_all(buf)
    buf, output, norm_two, grad_sum, const_two, taken_zero, taken_act = call(
        third_kernel,
        [((devices, 2, LANES), F32), (full, BF16), (full, F32), (full, F32), ((8, LANES), F32)],
        counts, buf, hidden_two, start, cotangent, scale_two, bias_two, smem=1, carry=[taken_zero, taken_act],
    )
    buf = to_all(buf)
    buf, grad_two, table_two, sums_two, taken_zero, taken_act = call(
        functools.partial(fourth_kernel, grid),
        [((devices, width, LANES), BF16), (full, BF16), (full, F32), ((2, LANES), F32)],
        counts, buf, norm_two, grad_sum, const_two, two_flat, hot, norm_one, slope_one, halo_slope, halo_cross,
        smem=1, carry=[taken_zero, taken_act],
    )
    buf = to_all(buf)
    grad_one, give, grad_norms = call(
        functools.partial(fifth_kernel, grid),
        [(full, BF16), ((packed, LANES), BF16), ((4, channels), F32)],
        counts, buf, table_two, place, norm_one, slope_one, const_one, sums_two,
        taken_zero, taken_act, grad_two, smem=1,
    )
    got = swap_core(give)
    table_one, halo_one, keep = call(
        back_kernel,
        [(full, F32), (square, BF16), ((packed, LANES), F32)],
        grad_one, one_flat, hot, taken_zero, taken_act, grad_two,
    )
    (buf,) = call(
        functools.partial(sixth_kernel, grid, width),
        [((devices, width + piece, LANES), BF16)],
        halo_one, keep, got,
    )
    buf = to_all(buf)
    buf, grad_features = call(
        functools.partial(seventh_kernel, grid, width),
        [((devices, piece, LANES), BF16), (full, BF16)],
        counts, buf, table_one, place, grad_sum, smem=1,
    )
    own = to_all(buf).reshape(packed, LANES)
    other = swap_core(own)
    weights = [(weight_one.shape, F32), (weight_two.shape, F32)]
    blocks = [pltpu.VMEM(weight_one.shape, F32), pltpu.SemaphoreType.DMA((13,))]
    grad_weight_one, grad_weight_two, output, grad_features, grad_norms = call(
        own_kernel,
        weights + [(full, BF16), (full, BF16), ((4, channels), F32)],
        own, output, grad_features, grad_norms, hbm_outs=(0, 1), scratch=blocks,
    )
    grad_weight_one, grad_weight_two = call(
        other_kernel, weights, other, grad_weight_one, grad_weight_two,
        hbm=(1, 2), hbm_outs=(0, 1), scratch=blocks, aliases={1: 0, 2: 1},
    )
    return (output, grad_features, grad_weight_one, grad_weight_two, grad_norms)


def solution(mesh):
    return jax.shard_map(
        on_device,
        mesh=mesh,
        in_specs=(
            P(None, ("gx", "gy")),
            P(None, ("gx", "gy")),
            P(None, ("gx", "gy")),
            P(("gx", "gy")),
            P(),
            P(),
            P(),
            P(),
            P(),
            P(),
            P(None, ("gx", "gy")),
        ),
        out_specs=(P(None, ("gx", "gy")), P(None, ("gx", "gy")), P(), P(), P()),
        check_vma=False,
    )
```

```python
import functools

import jax
import jax.numpy as jnp
from jax import lax
from jax.experimental import pallas as pl
from jax.experimental.pallas import tpu as pltpu
from jax.sharding import PartitionSpec as P

EPS = 1e-05
STEP_LIST = ((1, 0), (-1, 0), (0, 1), (0, -1), (1, 1), (1, -1), (-1, 1), (-1, -1))
AXES = ("gx", "gy")
LANES = 128
F32 = jnp.float32
BF16 = jnp.bfloat16


def nn(a, b):
    return lax.dot_general(a, b, (((1,), (0,)), ((), ())), preferred_element_type=F32)


def nt(a, b):
    return lax.dot_general(a, b, (((1,), (1,)), ((), ())), preferred_element_type=F32)


def iota(shape, dim):
    return lax.broadcasted_iota(jnp.int32, shape, dim)


def eye(size):
    return jnp.where(iota((size, size), 0) == iota((size, size), 1), 1.0, 0.0).astype(BF16)


def sigmoid(v):
    return 1.0 / (1.0 + jnp.exp(-v))


def neighbour(place, grid, step):
    i, j = place[0] + step[0], place[1] + step[1]
    inside = (i >= 0) & (i < grid[0]) & (j >= 0) & (j < grid[1])
    return jnp.where(inside, i * grid[1] + j, place[0] * grid[1] + place[1]), inside


def here():
    return lax.axis_index("gx"), lax.axis_index("gy")


def put_blocks(buf_ref, rows, grid, sign, width, base=None):
    place = here()
    for n, (a, b) in enumerate(STEP_LIST):
        dest, _ = neighbour(place, grid, (sign * a, sign * b))
        block = rows[n * width : (n + 1) * width]
        if base is not None:
            block = jnp.where(iota(block.shape, 1) < 96, block, base)
        buf_ref[dest, 0:width, :] = block.astype(BF16)


def take_blocks(buf_ref, grid, sign, width):
    place = here()
    blocks = []
    for a, b in STEP_LIST:
        src, inside = neighbour(place, grid, (sign * a, sign * b))
        block = buf_ref[src, 0:width, :].astype(F32)
        blocks.append(jnp.where(inside, block, 0.0))
    return jnp.concatenate(blocks, axis=0)


def pad_to(x, rows, lanes):
    if x.shape[1] < lanes:
        x = jnp.concatenate([x, jnp.zeros((x.shape[0], lanes - x.shape[1]), x.dtype)], axis=1)
    if x.shape[0] < rows:
        x = jnp.concatenate([x, jnp.zeros((rows - x.shape[0], lanes), x.dtype)], axis=0)
    return x


def cols_to_rows(cols):
    lane = iota((cols[0].shape[0], LANES), 1)
    total = jnp.zeros((cols[0].shape[0], LANES), F32)
    for at, col in enumerate(cols):
        total = jnp.where(lane == at, col, total)
    return pad_to(total, LANES, LANES).T


def rows_to_cols(rows):
    sub = iota((LANES, LANES), 0)
    total = jnp.zeros((LANES, LANES), F32)
    for at, row in enumerate(rows):
        total = jnp.where(sub == at, row, total)
    total = total.T
    return [total[:, at : at + 1] for at in range(len(rows))]


def split3(x):
    high = x.astype(BF16).astype(F32)
    mid = (x - high).astype(BF16).astype(F32)
    low = (x - high - mid).astype(BF16).astype(F32)
    return [high, mid, low]


def pack_rows(pieces, last):
    sub = iota((16, LANES), 0)
    lane = iota((16, LANES), 1)
    total = jnp.zeros((16, LANES), F32)
    for q, piece in enumerate(pieces):
        total = jnp.where(sub // 3 == q, piece, total)
    part = sub % 3
    moved = jnp.where(
        part == 0,
        pltpu.roll(total, 96, 1),
        jnp.where(part == 1, pltpu.roll(total, 64, 1), pltpu.roll(total, 32, 1)),
    )
    moved = jnp.where(sub == 15, last, moved)
    return jnp.where(lane >= 96, moved, 0.0)


def unpack_rows(tiles, groups):
    devices = tiles.shape[0]
    flat = tiles.reshape(devices * 16, LANES)
    sub = iota(tiles.shape, 1)
    lane = iota(tiles.shape, 2)
    part = sub % 3
    moved = [pltpu.roll(flat, 32 * (p + 1), 1).reshape(tiles.shape) for p in range(3)]
    value = jnp.where(part == 0, moved[0], jnp.where(part == 1, moved[1], moved[2]))
    value = jnp.where((lane // 32 == part) & (sub < 15), value, 0.0)
    results = []
    for low, high in groups:
        mask = (sub >= 3 * low) & (sub < 3 * high)
        results.append(jnp.sum(jnp.where(mask, value, 0.0), axis=1))
    return results


def valid_lanes(counts_ref, rows=1):
    return (iota((rows, LANES), 1) < counts_ref[0]).astype(F32)


def open_kernel(
    grid, counts_ref, features_hbm, send_hbm, map_hbm, one_hbm,
    buf_ref, start_ref, place_ref, hot_ref, one_ref, features_ref, send_ref, map_ref, sems,
):
    pairs = ((features_hbm, features_ref), (send_hbm, send_ref), (map_hbm, map_ref), (one_hbm, one_ref))
    copies = [pltpu.make_async_copy(src, dst, sems.at[at]) for at, (src, dst) in enumerate(pairs)]
    for copy in copies:
        copy.start()
    for copy in copies[:2]:
        copy.wait()
    width = send_ref.shape[1]
    send = send_ref[...].astype(F32).astype(BF16)
    spread = jnp.where(iota((width, LANES), 1) % width == iota((width, LANES), 0), 1.0, 0.0).astype(BF16)
    wide = nn(send, spread)
    wide = jnp.where(iota(wide.shape, 1) // width == iota(wide.shape, 0), wide, 0.0)
    row = jnp.sum(wide, axis=0, keepdims=True)
    place = jnp.where(row == iota((LANES, LANES), 0).astype(F32), 1.0, 0.0).T.astype(BF16)
    place_ref[...] = place
    valid = valid_lanes(counts_ref)
    start = features_ref[...].astype(F32) * valid
    start_ref[...] = start.astype(BF16)
    extra = jnp.where(iota((LANES - 96, LANES), 0) == 0, valid, 0.0)
    rows = nt(place, jnp.concatenate([start, extra], axis=0).astype(BF16))
    put_blocks(buf_ref, rows, grid, 1, width)
    copies[2].wait()
    sub = iota((hot_ref.shape[0], LANES), 0)
    for k in range(map_ref.shape[0]):
        hot_ref[:, k * LANES : (k + 1) * LANES] = jnp.where(
            sub == map_ref[k : k + 1, :], 1.0, 0.0
        ).astype(BF16)
    copies[3].wait()


def gather(tables, hot_ref, taken_refs):
    channels = tables[0].shape[0]
    taken = nn(jnp.concatenate(tables, axis=0), hot_ref[...]).astype(BF16)
    for at, ref in enumerate(taken_refs):
        for k in range(hot_ref.shape[1] // LANES):
            ref[k * channels : (k + 1) * channels, :] = taken[
                at * channels : (at + 1) * channels, k * LANES : (k + 1) * LANES
            ]


def gather_convolve(table, hot_ref, weight_ref, taken_ref):
    gather([table], hot_ref, [taken_ref])
    return lax.dot_general(
        weight_ref[...], taken_ref[...], (((0,), (0,)), ((), ())), preferred_element_type=F32
    )


def first_kernel(
    grid, counts_ref, buf_ref, start_ref, hot_ref, weight_ref, place_ref,
    out_buf_ref, hidden_ref, taken_ref, flag_ref,
):
    width = buf_ref.shape[1]
    channels = start_ref.shape[0]
    halo_rows = take_blocks(buf_ref, grid, -1, width).astype(BF16)
    flag_ref[...] = jnp.broadcast_to(halo_rows[:, 96:97].astype(F32), (LANES, LANES))
    halo = nt(eye(LANES), halo_rows)[:channels].astype(BF16)
    table = jnp.concatenate([start_ref[...], halo], axis=1)
    hidden = gather_convolve(table, hot_ref, weight_ref, taken_ref)
    hidden_ref[...] = hidden
    valid = valid_lanes(counts_ref)
    count = counts_ref[0].astype(F32)
    sums = jnp.sum(hidden * valid, axis=1, keepdims=True)
    centred = (hidden - sums / count) * valid
    spread = jnp.sum(centred * centred, axis=1, keepdims=True)
    stat = cols_to_rows([sums, spread])
    base = pack_rows(split3(stat[0:1]) + split3(stat[1:2])[:2], count)
    out_buf_ref[...] = jnp.broadcast_to(base.astype(BF16)[None], out_buf_ref.shape)
    rows = pad_to(nt(place_ref[...], centred.astype(BF16)), LANES, LANES)
    put_blocks(out_buf_ref, rows, grid, 1, width, base)


def second_kernel(
    grid, counts_ref, buf_ref, hidden_ref, flag_ref, scale_ref, bias_ref, hot_ref, weight_ref,
    out_buf_ref, hidden_two_ref, taken_ref, norm_ref, slope_ref, halo_slope_ref, halo_cross_ref,
    const_ref, mean_ref,
):
    width = buf_ref.shape[1]
    channels = hidden_ref.shape[0]
    tiles = buf_ref[...].astype(F32)
    sums, spreads = unpack_rows(tiles, ((0, 3), (3, 5)))
    counts = tiles[:, 15, 96:97]
    total = jnp.sum(counts, axis=0, keepdims=True)
    means = sums / counts
    mean_ref[...] = means
    mean = jnp.sum(sums, axis=0, keepdims=True) / total
    apart = means - mean
    var = jnp.sum(spreads + counts * apart * apart, axis=0, keepdims=True) / total
    rstd = lax.rsqrt(var + EPS)
    scale = pad_to(scale_ref[...], 1, LANES)
    bias = pad_to(bias_ref[...], 1, LANES)
    total_row = jnp.broadcast_to(total, (1, LANES))
    mean_c, rstd_c, scale_c, bias_c = [c[:channels] for c in rows_to_cols([mean, rstd, scale, bias])]
    sub = iota((8, LANES), 0)
    const_ref[...] = jnp.where(sub == 0, scale * rstd, jnp.where(sub == 1, total_row, 0.0))

    valid = valid_lanes(counts_ref)
    normal = (hidden_ref[...] - mean_c) * rstd_c
    norm_ref[...] = normal
    linear = scale_c * normal + bias_c
    sig = sigmoid(linear)
    slope_ref[...] = sig * (1.0 + linear * (1.0 - sig)) * valid
    act = (linear * sig * valid).astype(BF16)

    place = here()
    lifted = []
    for n, (a, b) in enumerate(STEP_LIST):
        src, inside = neighbour(place, grid, (-a, -b))
        block = buf_ref[src, 0:width, :].astype(F32) + mean_ref[pl.ds(src, 1), :]
        lifted.append(jnp.where(inside, block, 0.0))
    lane = iota((LANES, LANES), 1)
    halo = jnp.where(lane < channels, jnp.concatenate(lifted, axis=0), 0.0)
    flag = flag_ref[...]
    halo_normal = (halo - mean) * rstd
    halo_linear = scale * halo_normal + bias
    halo_sig = sigmoid(halo_linear)
    halo_slope = halo_sig * (1.0 + halo_linear * (1.0 - halo_sig)) * flag
    halo_slope_ref[...] = halo_slope
    halo_cross_ref[...] = halo_slope * halo_normal
    halo_act = nt(eye(LANES), (halo_linear * halo_sig * flag).astype(BF16))[:channels].astype(BF16)

    table = jnp.concatenate([act, halo_act], axis=1)
    hidden = gather_convolve(table, hot_ref, weight_ref, taken_ref)
    hidden_two_ref[...] = hidden
    count = counts_ref[0].astype(F32)
    sums_two = jnp.sum(hidden * valid, axis=1, keepdims=True)
    centred = (hidden - sums_two / count) * valid
    spread_two = jnp.sum(centred * centred, axis=1, keepdims=True)
    stat = cols_to_rows([sums_two, spread_two])[0:2]
    stat = jnp.where(iota((2, LANES), 1) < 96, stat, count)
    out_buf_ref[...] = jnp.broadcast_to(stat[None], out_buf_ref.shape)


def third_kernel(
    counts_ref, buf_ref, hidden_ref, start_ref, cotangent_ref, scale_ref, bias_ref,
    out_buf_ref, output_ref, norm_ref, grad_ref, const_ref,
):
    channels = hidden_ref.shape[0]
    sums = buf_ref[:, 0, :]
    spreads = buf_ref[:, 1, :]
    counts = sums[:, 96:97]
    total = jnp.sum(counts, axis=0, keepdims=True)
    mean = jnp.sum(sums, axis=0, keepdims=True) / total
    apart = sums / counts - mean
    var = jnp.sum(spreads + counts * apart * apart, axis=0, keepdims=True) / total
    rstd = lax.rsqrt(var + EPS)
    scale = pad_to(scale_ref[...], 1, LANES)
    bias = pad_to(bias_ref[...], 1, LANES)
    total_row = jnp.broadcast_to(total, (1, LANES))
    mean_c, rstd_c, scale_c, bias_c = [c[:channels] for c in rows_to_cols([mean, rstd, scale, bias])]
    sub = iota((8, LANES), 0)
    const_ref[...] = jnp.where(sub == 0, scale * rstd, jnp.where(sub == 1, total_row, 0.0))
    valid = valid_lanes(counts_ref)
    normal = (hidden_ref[...] - mean_c) * rstd_c
    norm_ref[...] = normal
    summed = scale_c * normal + bias_c + start_ref[...].astype(F32)
    sig = sigmoid(summed)
    output_ref[...] = (summed * sig * valid).astype(BF16)
    grad = cotangent_ref[...].astype(F32) * valid * (sig * (1.0 + summed * (1.0 - sig)))
    grad_ref[...] = grad
    dbias = jnp.sum(grad, axis=1, keepdims=True)
    dgain = jnp.sum(grad * normal * valid, axis=1, keepdims=True)
    rows = cols_to_rows([dgain, dbias])[0:2]
    out_buf_ref[...] = jnp.broadcast_to(rows[None], out_buf_ref.shape)


def scatter(grad, weight_ref, hot_ref):
    channels = grad.shape[0]
    terms = nn(weight_ref[...], grad).astype(BF16)
    offsets = hot_ref.shape[1] // LANES
    wide = jnp.concatenate([terms[k * channels : (k + 1) * channels] for k in range(offsets)], axis=1)
    table = pad_to(nt(hot_ref[...], wide), hot_ref.shape[0], LANES)
    return table[:LANES].T[:channels], table[LANES : 2 * LANES]


def row_gradient(grad, normal, const, dgain, dbias, valid):
    channels = grad.shape[0]
    factor, part_bias, part_gain = rows_to_cols([const[0:1], dbias / const[1:2], dgain / const[1:2]])
    return (
        factor[:channels] * (grad - (part_bias[:channels] + normal * part_gain[:channels])) * valid
    ).astype(BF16)


def fourth_kernel(
    grid, counts_ref, buf_ref, norm_ref, grad_ref, const_ref, weight_ref, hot_ref,
    norm_one_ref, slope_ref, halo_slope_ref, halo_cross_ref,
    out_buf_ref, grad_two_ref, table_ref, sums_ref,
):
    channels = norm_ref.shape[0]
    width = out_buf_ref.shape[1]
    valid = valid_lanes(counts_ref)
    both = jnp.sum(buf_ref[...], axis=0)
    sums_ref[...] = both
    grad = row_gradient(grad_ref[...], norm_ref[...], const_ref[...], both[0:1], both[1:2], valid)
    grad_two_ref[...] = grad
    local, halo = scatter(grad, weight_ref, hot_ref)
    table_ref[...] = local
    pulled = local * slope_ref[...]
    dbias = jnp.sum(pulled, axis=1, keepdims=True)
    dgain = jnp.sum(pulled * norm_one_ref[...], axis=1, keepdims=True)
    rows = cols_to_rows([dgain, dbias])
    dgain = rows[0:1] + jnp.sum(halo * halo_cross_ref[...], axis=0, keepdims=True)
    dbias = rows[1:2] + jnp.sum(halo * halo_slope_ref[...], axis=0, keepdims=True)
    base = pack_rows(split3(dgain)[:2] + split3(dbias)[:2], 0.0)
    out_buf_ref[...] = jnp.broadcast_to(base.astype(BF16)[None], out_buf_ref.shape)
    put_blocks(out_buf_ref, halo, grid, -1, width, base)


def packed_weight_grad(taken_ref, grad, put):
    channels = grad.shape[0]
    zero = jnp.zeros((channels, LANES), BF16)

    def taken(k):
        return taken_ref[k * channels : (k + 1) * channels, :]

    for part in range(3):
        upper = jnp.concatenate([grad, zero], axis=1)
        lower = jnp.concatenate([zero[:32], grad[32 * part : 32 * part + 32]], axis=1)
        right = jnp.concatenate([upper, lower], axis=0)
        left = jnp.concatenate(
            [
                jnp.concatenate([taken(3 * e + part) for e in range(6)], axis=0),
                jnp.concatenate([taken(21 + e) for e in range(6)], axis=0),
            ],
            axis=1,
        )
        result = nt(left, right)
        for e in range(6):
            put(3 * e + part, result[e * channels : (e + 1) * channels])
    last = nt(taken_ref[18 * channels : 21 * channels, :], pad_to(grad, LANES, LANES))
    for e in range(3):
        put(18 + e, last[e * channels : (e + 1) * channels])


def store_packed(taken_ref, grad, ref):
    channels = grad.shape[0]
    used = 21 * channels

    def put(block, value):
        ref[block * channels : (block + 1) * channels, :] = value.astype(ref.dtype)

    packed_weight_grad(taken_ref, grad, put)
    if ref.shape[0] > used:
        ref[used:, :] = jnp.zeros((ref.shape[0] - used, LANES), ref.dtype)


def fifth_kernel(
    grid, counts_ref, buf_ref, table_ref, place_ref, norm_ref, slope_ref, const_ref, sums_two_ref,
    taken_zero_ref, taken_act_ref, grad_two_ref,
    grad_one_ref, give_ref, sums_ref,
):
    width = buf_ref.shape[1]
    channels = norm_ref.shape[0]
    valid = valid_lanes(counts_ref)
    dgain, dbias = unpack_rows(
        jnp.sum(buf_ref[...].astype(F32), axis=0, keepdims=True), ((0, 2), (2, 4))
    )
    two = sums_two_ref[...]
    sums_ref[...] = jnp.concatenate([dgain, dbias, two], axis=0)[:, :channels]
    arrived = nt(eye(LANES), take_blocks(buf_ref, grid, 1, width).astype(BF16))[:channels].astype(BF16)
    back = table_ref[...] + nn(arrived, place_ref[...])
    grad = row_gradient(back * slope_ref[...], norm_ref[...], const_ref[...], dgain, dbias, valid)
    grad_one_ref[...] = grad
    core = lax.axis_index("gy") % 2

    @pl.when(core == 0)
    def _():
        store_packed(taken_act_ref, grad_two_ref[...], give_ref)

    @pl.when(core != 0)
    def _():
        store_packed(taken_zero_ref, grad, give_ref)


def back_kernel(
    grad_ref, weight_ref, hot_ref, taken_zero_ref, taken_act_ref, grad_two_ref, table_ref, halo_ref, keep_ref
):
    core = lax.axis_index("gy") % 2

    @pl.when(core == 0)
    def _():
        store_packed(taken_zero_ref, grad_ref[...], keep_ref)

    @pl.when(core != 0)
    def _():
        store_packed(taken_act_ref, grad_two_ref[...], keep_ref)

    local, halo = scatter(grad_ref[...], weight_ref, hot_ref)
    table_ref[...] = local
    halo_ref[...] = halo.astype(BF16)


def sixth_kernel(grid, width, halo_ref, keep_ref, got_ref, out_buf_ref):
    devices, rows = out_buf_ref.shape[0], out_buf_ref.shape[1] - width
    put_blocks(out_buf_ref, halo_ref[...], grid, -1, width)
    total = (keep_ref[...] + got_ref[...].astype(F32)).astype(BF16)
    out_buf_ref[:, width:, :] = total.reshape(devices, rows, LANES)


def seventh_kernel(grid, width, counts_ref, buf_ref, table_ref, place_ref, grad_ref, out_buf_ref, out_ref):
    channels = table_ref.shape[0]
    devices, rows = buf_ref.shape[0], buf_ref.shape[1] - width
    valid = valid_lanes(counts_ref)
    arrived = nt(eye(LANES), take_blocks(buf_ref, grid, 1, width).astype(BF16))[:channels].astype(BF16)
    back = table_ref[...] + nn(arrived, place_ref[...])
    out_ref[...] = ((back + grad_ref[...]) * valid).astype(BF16)
    pieces = []
    for core in range(2):
        total = jnp.zeros((rows, LANES), F32)
        for d in range(core, devices, 2):
            total = total + buf_ref[d, width:, :].astype(F32)
        pieces.append(total.astype(BF16))
    for d in range(devices):
        out_buf_ref[d] = pieces[d % 2]


def unpack(src_ref, out_hbm, block_ref, sems):
    channels = block_ref.shape[1]
    lane = iota((channels, LANES), 1)
    copies = []

    def send(first, count):
        part = pl.ds(first, count)
        copies.append(pltpu.make_async_copy(block_ref.at[part], out_hbm.at[part], sems.at[len(copies)]))
        copies[-1].start()

    for e in range(7):
        extra = jnp.zeros((channels, LANES), F32)
        for part in range(3):
            block = 3 * e + part
            value = src_ref[block * channels : (block + 1) * channels, :].astype(F32)
            block_ref[block] = value[:, :channels]
            if e < 6:
                moved = pltpu.roll(value, 32 * (part + 1), 1)
                extra = jnp.where(lane // 32 == part, moved, extra)
        send(3 * e, 3)
        if e < 6:
            block_ref[21 + e] = extra[:, :channels]
            send(21 + e, 1)
    for copy in copies:
        copy.wait()


def own_kernel(own_ref, small_in, more_in, sums_in, one_hbm, two_hbm, small_out, more_out, sums_out, block_ref, sems):
    core = lax.axis_index("gy") % 2
    small_out[...] = small_in[...]
    more_out[...] = more_in[...]
    sums_out[...] = sums_in[...]

    @pl.when(core == 0)
    def _():
        unpack(own_ref, one_hbm, block_ref, sems)

    @pl.when(core != 0)
    def _():
        unpack(own_ref, two_hbm, block_ref, sems)


def other_kernel(other_ref, one_in, two_in, one_hbm, two_hbm, block_ref, sems):
    core = lax.axis_index("gy") % 2

    @pl.when(core == 0)
    def _():
        unpack(other_ref, two_hbm, block_ref, sems)

    @pl.when(core != 0)
    def _():
        unpack(other_ref, one_hbm, block_ref, sems)


def call(kernel, outs, *args, smem=0, scratch=(), hbm=(), hbm_outs=(), aliases=None, carry=()):
    n_in, n_out = len(args), len(outs)
    aliases = dict(aliases or {})
    aliases.update({n_in + at: n_out + at for at in range(len(carry))})

    def space(at):
        if at >= n_in:
            return pl.ANY
        if at in hbm:
            return pltpu.HBM
        return pltpu.SMEM if at < smem else pltpu.VMEM

    def out_space(at):
        if at >= n_out:
            return pl.ANY
        return pltpu.HBM if at in hbm_outs else pltpu.VMEM

    def body(*refs):
        first_out = n_in + len(carry)
        kernel(*refs[:n_in], *refs[first_out : first_out + n_out], *refs[first_out + n_out + len(carry) :])

    args = [pltpu.with_memory_space_constraint(x, pltpu.HBM) if at in hbm else x for at, x in enumerate(args)]
    outs = list(outs) + [(x.shape, x.dtype) for x in carry]
    return pl.pallas_call(
        body,
        out_shape=tuple(jax.ShapeDtypeStruct(shape, dtype) for shape, dtype in outs),
        in_specs=[pl.BlockSpec(memory_space=space(at)) for at in range(n_in + len(carry))],
        out_specs=tuple(pl.BlockSpec(memory_space=out_space(at)) for at in range(len(outs))),
        scratch_shapes=list(scratch),
        input_output_aliases=aliases,
        compiler_params=pltpu.CompilerParams(vmem_limit_bytes=40 * 1024 * 1024),
    )(*args, *carry)


def to_all(x):
    return lax.all_to_all(x, AXES, 0, 0)


def swap_core(x):
    size = lax.axis_size("gy")
    return lax.ppermute(x, "gy", [(i, i ^ 1) for i in range(size)])


def on_device(
    features, kernel_map, send_rows, counts, weight_one, weight_two,
    first_norm_scale, first_norm_bias, second_norm_scale, second_norm_bias, cotangent,
):
    channels, rows = features.shape
    offsets = kernel_map.shape[0]
    width = send_rows.shape[1]
    grid = (lax.axis_size("gx"), lax.axis_size("gy"))
    devices = grid[0] * grid[1]
    flat = offsets * channels
    table = rows + 8 * width
    piece = -(-21 * channels // (devices * 16)) * 16
    packed = piece * devices
    full = (channels, rows)
    square = (LANES, LANES)
    one_flat = weight_one.reshape(flat, channels)
    two_flat = weight_two.reshape(flat, channels)
    scale_one, bias_one, scale_two, bias_two = [
        v.reshape(1, channels)
        for v in (first_norm_scale, first_norm_bias, second_norm_scale, second_norm_bias)
    ]

    taken = ((flat, LANES), BF16)
    buf, start, place, hot, one_near = call(
        functools.partial(open_kernel, grid),
        [
            ((devices, width, LANES), BF16), (full, BF16), (square, BF16),
            ((table, offsets * LANES), BF16), (one_flat.shape, BF16),
        ],
        counts, features, send_rows, kernel_map, one_flat, smem=1, hbm=(1, 2, 3, 4),
        scratch=[
            pltpu.VMEM(full, BF16), pltpu.VMEM(send_rows.shape, jnp.int32),
            pltpu.VMEM(kernel_map.shape, jnp.int32), pltpu.SemaphoreType.DMA((4,)),
        ],
    )
    buf = to_all(buf)
    buf, hidden_one, taken_zero, flag = call(
        functools.partial(first_kernel, grid),
        [((devices, width, LANES), BF16), (full, F32), taken, (square, F32)],
        counts, buf, start, hot, one_near, place, smem=1,
    )
    buf = to_all(buf)
    buf, hidden_two, taken_act, norm_one, slope_one, halo_slope, halo_cross, const_one, taken_zero = call(
        functools.partial(second_kernel, grid),
        [
            ((devices, 2, LANES), F32), (full, F32), taken, (full, F32), (full, F32),
            (square, F32), (square, F32), ((8, LANES), F32),
        ],
        counts, buf, hidden_one, flag, scale_one, bias_one, hot, two_flat,
        smem=1, scratch=[pltpu.VMEM((devices, LANES), F32)], carry=[taken_zero],
    )
    buf = to_all(buf)
    buf, output, norm_two, grad_sum, const_two, taken_zero, taken_act = call(
        third_kernel,
        [((devices, 2, LANES), F32), (full, BF16), (full, F32), (full, F32), ((8, LANES), F32)],
        counts, buf, hidden_two, start, cotangent, scale_two, bias_two, smem=1, carry=[taken_zero, taken_act],
    )
    buf = to_all(buf)
    buf, grad_two, table_two, sums_two, taken_zero, taken_act = call(
        functools.partial(fourth_kernel, grid),
        [((devices, width, LANES), BF16), (full, BF16), (full, F32), ((2, LANES), F32)],
        counts, buf, norm_two, grad_sum, const_two, two_flat, hot, norm_one, slope_one, halo_slope, halo_cross,
        smem=1, carry=[taken_zero, taken_act],
    )
    buf = to_all(buf)
    grad_one, give, grad_norms = call(
        functools.partial(fifth_kernel, grid),
        [(full, BF16), ((packed, LANES), BF16), ((4, channels), F32)],
        counts, buf, table_two, place, norm_one, slope_one, const_one, sums_two,
        taken_zero, taken_act, grad_two, smem=1,
    )
    got = swap_core(give)
    table_one, halo_one, keep = call(
        back_kernel,
        [(full, F32), (square, BF16), ((packed, LANES), F32)],
        grad_one, one_flat, hot, taken_zero, taken_act, grad_two,
    )
    (buf,) = call(
        functools.partial(sixth_kernel, grid, width),
        [((devices, width + piece, LANES), BF16)],
        halo_one, keep, got,
    )
    buf = to_all(buf)
    buf, grad_features = call(
        functools.partial(seventh_kernel, grid, width),
        [((devices, piece, LANES), BF16), (full, BF16)],
        counts, buf, table_one, place, grad_sum, smem=1,
    )
    own = to_all(buf).reshape(packed, LANES)
    other = swap_core(own)
    weights = [(weight_one.shape, F32), (weight_two.shape, F32)]
    blocks = [pltpu.VMEM(weight_one.shape, F32), pltpu.SemaphoreType.DMA((13,))]
    grad_weight_one, grad_weight_two, output, grad_features, grad_norms = call(
        own_kernel,
        weights + [(full, BF16), (full, BF16), ((4, channels), F32)],
        own, output, grad_features, grad_norms, hbm_outs=(0, 1), scratch=blocks,
    )
    grad_weight_one, grad_weight_two = call(
        other_kernel, weights, other, grad_weight_one, grad_weight_two,
        hbm=(1, 2), hbm_outs=(0, 1), scratch=blocks, aliases={1: 0, 2: 1},
    )
    return (output, grad_features, grad_weight_one, grad_weight_two, grad_norms)


def solution(mesh):
    return jax.shard_map(
        on_device,
        mesh=mesh,
        in_specs=(
            P(None, ("gx", "gy")),
            P(None, ("gx", "gy")),
            P(None, ("gx", "gy")),
            P(("gx", "gy")),
            P(),
            P(),
            P(),
            P(),
            P(),
            P(),
            P(None, ("gx", "gy")),
        ),
        out_specs=(P(None, ("gx", "gy")), P(None, ("gx", "gy")), P(), P(), P()),
        check_vma=False,
    )
```

```python
import functools

import jax
import jax.numpy as jnp
from jax import lax
from jax.experimental import pallas as pl
from jax.experimental.pallas import tpu as pltpu
from jax.sharding import PartitionSpec as P

EPS = 1e-05
STEP_LIST = ((1, 0), (-1, 0), (0, 1), (0, -1), (1, 1), (1, -1), (-1, 1), (-1, -1))
AXES = ("gx", "gy")
LANES = 128
F32 = jnp.float32
BF16 = jnp.bfloat16


def nn(a, b):
    return lax.dot_general(a, b, (((1,), (0,)), ((), ())), preferred_element_type=F32)


def nt(a, b):
    return lax.dot_general(a, b, (((1,), (1,)), ((), ())), preferred_element_type=F32)


def tn(a, b):
    return lax.dot_general(a, b, (((0,), (0,)), ((), ())), preferred_element_type=F32)


def iota(shape, dim):
    return lax.broadcasted_iota(jnp.int32, shape, dim)


def sigmoid(v):
    return 1.0 / (1.0 + jnp.exp(-v))


def neighbour(place, grid, step):
    i, j = place[0] + step[0], place[1] + step[1]
    inside = (i >= 0) & (i < grid[0]) & (j >= 0) & (j < grid[1])
    return jnp.where(inside, i * grid[1] + j, place[0] * grid[1] + place[1]), inside


def here():
    return lax.axis_index("gx"), lax.axis_index("gy")


def put_blocks(buf_ref, rows, grid, sign, width, base=None):
    place = here()
    for n, (a, b) in enumerate(STEP_LIST):
        dest, _ = neighbour(place, grid, (sign * a, sign * b))
        block = rows[n * width : (n + 1) * width]
        if base is not None:
            block = jnp.where(iota(block.shape, 1) < 96, block, base)
        buf_ref[dest, 0:width, :] = block.astype(BF16)


def take_blocks(buf_ref, grid, sign, width):
    place = here()
    blocks = []
    for a, b in STEP_LIST:
        src, inside = neighbour(place, grid, (sign * a, sign * b))
        block = buf_ref[src, 0:width, :].astype(F32)
        blocks.append(jnp.where(inside, block, 0.0))
    return jnp.concatenate(blocks, axis=0)


def pad_to(x, rows, lanes):
    if x.shape[1] < lanes:
        x = jnp.concatenate([x, jnp.zeros((x.shape[0], lanes - x.shape[1]), x.dtype)], axis=1)
    if x.shape[0] < rows:
        x = jnp.concatenate([x, jnp.zeros((rows - x.shape[0], lanes), x.dtype)], axis=0)
    return x


def cols_to_rows(cols):
    lane = iota((cols[0].shape[0], LANES), 1)
    total = jnp.zeros((cols[0].shape[0], LANES), F32)
    for at, col in enumerate(cols):
        total = jnp.where(lane == at, col, total)
    return pad_to(total, LANES, LANES).T


def rows_to_cols(rows):
    sub = iota((LANES, LANES), 0)
    total = jnp.zeros((LANES, LANES), F32)
    for at, row in enumerate(rows):
        total = jnp.where(sub == at, row, total)
    total = total.T
    return [total[:, at : at + 1] for at in range(len(rows))]


def split3(x):
    high = x.astype(BF16).astype(F32)
    mid = (x - high).astype(BF16).astype(F32)
    low = (x - high - mid).astype(BF16).astype(F32)
    return [high, mid, low]


def pack_rows(pieces, last):
    sub = iota((16, LANES), 0)
    lane = iota((16, LANES), 1)
    total = jnp.zeros((16, LANES), F32)
    for q, piece in enumerate(pieces):
        total = jnp.where(sub // 3 == q, piece, total)
    part = sub % 3
    moved = jnp.where(
        part == 0,
        pltpu.roll(total, 96, 1),
        jnp.where(part == 1, pltpu.roll(total, 64, 1), pltpu.roll(total, 32, 1)),
    )
    moved = jnp.where(sub == 15, last, moved)
    return jnp.where(lane >= 96, moved, 0.0)


def unpack_rows(tiles, groups):
    devices = tiles.shape[0]
    flat = tiles.reshape(devices * 16, LANES)
    sub = iota(tiles.shape, 1)
    lane = iota(tiles.shape, 2)
    part = sub % 3
    moved = [pltpu.roll(flat, 32 * (p + 1), 1).reshape(tiles.shape) for p in range(3)]
    value = jnp.where(part == 0, moved[0], jnp.where(part == 1, moved[1], moved[2]))
    value = jnp.where((lane // 32 == part) & (sub < 15), value, 0.0)
    results = []
    for low, high in groups:
        mask = (sub >= 3 * low) & (sub < 3 * high)
        results.append(jnp.sum(jnp.where(mask, value, 0.0), axis=1))
    return results


def valid_lanes(counts_ref, rows=1):
    return (iota((rows, LANES), 1) < counts_ref[0]).astype(F32)


def open_kernel(
    grid, counts_ref, features_hbm, send_hbm, map_hbm, one_hbm,
    buf_ref, start_ref, place_ref, hot_ref, one_ref, features_ref, send_ref, map_ref, sems,
):
    pairs = ((features_hbm, features_ref), (send_hbm, send_ref), (map_hbm, map_ref), (one_hbm, one_ref))
    copies = [pltpu.make_async_copy(src, dst, sems.at[at]) for at, (src, dst) in enumerate(pairs)]
    for copy in copies:
        copy.start()
    for copy in copies[:2]:
        copy.wait()
    width = send_ref.shape[1]
    send = send_ref[...].astype(F32).astype(BF16)
    spread = jnp.where(iota((width, LANES), 1) % width == iota((width, LANES), 0), 1.0, 0.0).astype(BF16)
    wide = nn(send, spread)
    wide = jnp.where(iota(wide.shape, 1) // width == iota(wide.shape, 0), wide, 0.0)
    row = jnp.sum(wide, axis=0, keepdims=True)
    place = jnp.where(row == iota((LANES, LANES), 0).astype(F32), 1.0, 0.0).T.astype(BF16)
    place_ref[...] = place
    valid = valid_lanes(counts_ref)
    start = features_ref[...].astype(F32) * valid
    start_ref[...] = start.astype(BF16)
    extra = jnp.where(iota((LANES - 96, LANES), 0) == 0, valid, 0.0)
    rows = nt(place, jnp.concatenate([start, extra], axis=0).astype(BF16))
    put_blocks(buf_ref, rows, grid, 1, width)
    copies[2].wait()
    sub = iota((hot_ref.shape[0], LANES), 0).astype(jnp.int16)
    columns = map_ref[...].astype(jnp.int16)
    one, zero = jnp.ones(sub.shape, BF16), jnp.zeros(sub.shape, BF16)
    for k in range(map_ref.shape[0]):
        hot_ref[:, k * LANES : (k + 1) * LANES] = jnp.where(sub == columns[k : k + 1, :], one, zero)
    copies[3].wait()


def gather(tables, hot_ref, taken_refs):
    channels = tables[0].shape[0]
    taken = nn(jnp.concatenate(tables, axis=0), hot_ref[...]).astype(BF16)
    for at, ref in enumerate(taken_refs):
        for k in range(hot_ref.shape[1] // LANES):
            ref[k * channels : (k + 1) * channels, :] = taken[
                at * channels : (at + 1) * channels, k * LANES : (k + 1) * LANES
            ]


def gather_convolve(table, hot_ref, weight_ref, taken_ref):
    gather([table], hot_ref, [taken_ref])
    return tn(weight_ref[...], taken_ref[...])


def first_kernel(
    grid, counts_ref, buf_ref, start_ref, hot_ref, weight_ref, place_ref,
    out_buf_ref, hidden_ref, taken_ref, flag_ref,
):
    width = buf_ref.shape[1]
    channels = start_ref.shape[0]
    halo_rows = take_blocks(buf_ref, grid, -1, width)
    flag_ref[...] = jnp.broadcast_to(halo_rows[:, 96:97], (LANES, LANES))
    halo = halo_rows.T[:channels].astype(BF16)
    table = jnp.concatenate([start_ref[...], halo], axis=1)
    hidden = gather_convolve(table, hot_ref, weight_ref, taken_ref)
    hidden_ref[...] = hidden
    valid = valid_lanes(counts_ref)
    count = counts_ref[0].astype(F32)
    sums = jnp.sum(hidden * valid, axis=1, keepdims=True)
    centred = (hidden - sums / count) * valid
    spread = jnp.sum(centred * centred, axis=1, keepdims=True)
    stat = cols_to_rows([sums, spread])
    base = pack_rows(split3(stat[0:1]) + split3(stat[1:2])[:2], count)
    out_buf_ref[...] = jnp.broadcast_to(base.astype(BF16)[None], out_buf_ref.shape)
    rows = pad_to(nt(place_ref[...], centred.astype(BF16)), LANES, LANES)
    put_blocks(out_buf_ref, rows, grid, 1, width, base)


def second_kernel(
    grid, counts_ref, buf_ref, hidden_ref, flag_ref, scale_ref, bias_ref, hot_ref, weight_ref,
    out_buf_ref, hidden_two_ref, taken_ref, norm_ref, slope_ref, halo_slope_ref, halo_cross_ref,
    const_ref, mean_ref,
):
    width = buf_ref.shape[1]
    channels = hidden_ref.shape[0]
    tiles = buf_ref[...].astype(F32)
    sums, spreads = unpack_rows(tiles, ((0, 3), (3, 5)))
    counts = tiles[:, 15, 96:97]
    total = jnp.sum(counts, axis=0, keepdims=True)
    means = sums / counts
    mean_ref[...] = means
    mean = jnp.sum(sums, axis=0, keepdims=True) / total
    apart = means - mean
    var = jnp.sum(spreads + counts * apart * apart, axis=0, keepdims=True) / total
    rstd = lax.rsqrt(var + EPS)
    scale = pad_to(scale_ref[...], 1, LANES)
    bias = pad_to(bias_ref[...], 1, LANES)
    total_row = jnp.broadcast_to(total, (1, LANES))
    mean_c, rstd_c, scale_c, bias_c = [c[:channels] for c in rows_to_cols([mean, rstd, scale, bias])]
    sub = iota((8, LANES), 0)
    const_ref[...] = jnp.where(sub == 0, scale * rstd, jnp.where(sub == 1, total_row, 0.0))

    valid = valid_lanes(counts_ref)
    normal = (hidden_ref[...] - mean_c) * rstd_c
    norm_ref[...] = normal
    linear = scale_c * normal + bias_c
    sig = sigmoid(linear)
    slope_ref[...] = sig * (1.0 + linear * (1.0 - sig)) * valid
    act = (linear * sig * valid).astype(BF16)

    place = here()
    lifted = []
    for n, (a, b) in enumerate(STEP_LIST):
        src, inside = neighbour(place, grid, (-a, -b))
        block = buf_ref[src, 0:width, :].astype(F32) + mean_ref[pl.ds(src, 1), :]
        lifted.append(jnp.where(inside, block, 0.0))
    lane = iota((LANES, LANES), 1)
    halo = jnp.where(lane < channels, jnp.concatenate(lifted, axis=0), 0.0)
    flag = flag_ref[...]
    halo_normal = (halo - mean) * rstd
    halo_linear = scale * halo_normal + bias
    halo_sig = sigmoid(halo_linear)
    halo_slope = halo_sig * (1.0 + halo_linear * (1.0 - halo_sig)) * flag
    halo_slope_ref[...] = halo_slope
    halo_cross_ref[...] = halo_slope * halo_normal
    halo_act = (halo_linear * halo_sig * flag).T[:channels].astype(BF16)

    table = jnp.concatenate([act, halo_act], axis=1)
    hidden = gather_convolve(table, hot_ref, weight_ref, taken_ref)
    hidden_two_ref[...] = hidden
    count = counts_ref[0].astype(F32)
    sums_two = jnp.sum(hidden * valid, axis=1, keepdims=True)
    centred = (hidden - sums_two / count) * valid
    spread_two = jnp.sum(centred * centred, axis=1, keepdims=True)
    stat = cols_to_rows([sums_two, spread_two])[0:2]
    stat = jnp.where(iota((2, LANES), 1) < 96, stat, count)
    out_buf_ref[...] = jnp.broadcast_to(stat[None], out_buf_ref.shape)


def third_kernel(
    counts_ref, buf_ref, hidden_ref, start_ref, cotangent_ref, scale_ref, bias_ref,
    out_buf_ref, output_ref, norm_ref, grad_ref, const_ref,
):
    channels = hidden_ref.shape[0]
    sums = buf_ref[:, 0, :]
    spreads = buf_ref[:, 1, :]
    counts = sums[:, 96:97]
    total = jnp.sum(counts, axis=0, keepdims=True)
    mean = jnp.sum(sums, axis=0, keepdims=True) / total
    apart = sums / counts - mean
    var = jnp.sum(spreads + counts * apart * apart, axis=0, keepdims=True) / total
    rstd = lax.rsqrt(var + EPS)
    scale = pad_to(scale_ref[...], 1, LANES)
    bias = pad_to(bias_ref[...], 1, LANES)
    total_row = jnp.broadcast_to(total, (1, LANES))
    mean_c, rstd_c, scale_c, bias_c = [c[:channels] for c in rows_to_cols([mean, rstd, scale, bias])]
    sub = iota((8, LANES), 0)
    const_ref[...] = jnp.where(sub == 0, scale * rstd, jnp.where(sub == 1, total_row, 0.0))
    valid = valid_lanes(counts_ref)
    normal = (hidden_ref[...] - mean_c) * rstd_c
    norm_ref[...] = normal
    summed = scale_c * normal + bias_c + start_ref[...].astype(F32)
    sig = sigmoid(summed)
    output_ref[...] = (summed * sig * valid).astype(BF16)
    grad = cotangent_ref[...].astype(F32) * valid * (sig * (1.0 + summed * (1.0 - sig)))
    grad_ref[...] = grad
    dbias = jnp.sum(grad, axis=1, keepdims=True)
    dgain = jnp.sum(grad * normal * valid, axis=1, keepdims=True)
    rows = cols_to_rows([dgain, dbias])[0:2]
    out_buf_ref[...] = jnp.broadcast_to(rows[None], out_buf_ref.shape)


def scatter(grad, weight_ref, hot_ref):
    channels = grad.shape[0]
    terms = nn(weight_ref[...], grad).astype(BF16)
    offsets = hot_ref.shape[1] // LANES
    wide = jnp.concatenate([terms[k * channels : (k + 1) * channels] for k in range(offsets)], axis=1)
    table = pad_to(nt(hot_ref[...], wide), hot_ref.shape[0], LANES)
    return table[:LANES].T[:channels], table[LANES : 2 * LANES]


def row_gradient(grad, normal, const, dgain, dbias, valid):
    channels = grad.shape[0]
    factor, part_bias, part_gain = rows_to_cols([const[0:1], dbias / const[1:2], dgain / const[1:2]])
    return (
        factor[:channels] * (grad - (part_bias[:channels] + normal * part_gain[:channels])) * valid
    ).astype(BF16)


def fourth_kernel(
    grid, counts_ref, buf_ref, norm_ref, grad_ref, const_ref, weight_ref, hot_ref,
    norm_one_ref, slope_ref, halo_slope_ref, halo_cross_ref,
    out_buf_ref, grad_two_ref, table_ref, sums_ref,
):
    channels = norm_ref.shape[0]
    width = out_buf_ref.shape[1]
    valid = valid_lanes(counts_ref)
    both = jnp.sum(buf_ref[...], axis=0)
    sums_ref[...] = both
    grad = row_gradient(grad_ref[...], norm_ref[...], const_ref[...], both[0:1], both[1:2], valid)
    grad_two_ref[...] = grad
    local, halo = scatter(grad, weight_ref, hot_ref)
    table_ref[...] = local
    pulled = local * slope_ref[...]
    dbias = jnp.sum(pulled, axis=1, keepdims=True)
    dgain = jnp.sum(pulled * norm_one_ref[...], axis=1, keepdims=True)
    rows = cols_to_rows([dgain, dbias])
    dgain = rows[0:1] + jnp.sum(halo * halo_cross_ref[...], axis=0, keepdims=True)
    dbias = rows[1:2] + jnp.sum(halo * halo_slope_ref[...], axis=0, keepdims=True)
    base = pack_rows(split3(dgain)[:2] + split3(dbias)[:2], 0.0)
    out_buf_ref[...] = jnp.broadcast_to(base.astype(BF16)[None], out_buf_ref.shape)
    put_blocks(out_buf_ref, halo, grid, -1, width, base)


def packed_weight_grad(taken_ref, grad, put):
    channels = grad.shape[0]
    zero = jnp.zeros((channels, LANES), BF16)

    def taken(k):
        return taken_ref[k * channels : (k + 1) * channels, :]

    for part in range(3):
        upper = jnp.concatenate([grad, zero], axis=1)
        lower = jnp.concatenate([zero[:32], grad[32 * part : 32 * part + 32]], axis=1)
        right = jnp.concatenate([upper, lower], axis=0)
        left = jnp.concatenate(
            [
                jnp.concatenate([taken(3 * e + part) for e in range(6)], axis=0),
                jnp.concatenate([taken(21 + e) for e in range(6)], axis=0),
            ],
            axis=1,
        )
        result = nt(left, right)
        for e in range(6):
            put(3 * e + part, result[e * channels : (e + 1) * channels])
    last = nt(taken_ref[18 * channels : 21 * channels, :], pad_to(grad, LANES, LANES))
    for e in range(3):
        put(18 + e, last[e * channels : (e + 1) * channels])


def store_packed(taken_ref, grad, ref):
    channels = grad.shape[0]
    used = 21 * channels

    def put(block, value):
        ref[block * channels : (block + 1) * channels, :] = value.astype(ref.dtype)

    packed_weight_grad(taken_ref, grad, put)
    if ref.shape[0] > used:
        ref[used:, :] = jnp.zeros((ref.shape[0] - used, LANES), ref.dtype)


def fifth_kernel(
    grid, counts_ref, buf_ref, table_ref, place_ref, norm_ref, slope_ref, const_ref, sums_two_ref,
    taken_zero_ref, taken_act_ref, grad_two_ref,
    grad_one_ref, give_ref, sums_ref,
):
    width = buf_ref.shape[1]
    channels = norm_ref.shape[0]
    valid = valid_lanes(counts_ref)
    dgain, dbias = unpack_rows(
        jnp.sum(buf_ref[...].astype(F32), axis=0, keepdims=True), ((0, 2), (2, 4))
    )
    two = sums_two_ref[...]
    sums_ref[...] = jnp.concatenate([dgain, dbias, two], axis=0)[:, :channels]
    arrived = take_blocks(buf_ref, grid, 1, width).astype(BF16)
    back = table_ref[...] + tn(arrived, place_ref[...])[:channels]
    grad = row_gradient(back * slope_ref[...], norm_ref[...], const_ref[...], dgain, dbias, valid)
    grad_one_ref[...] = grad
    core = lax.axis_index("gy") % 2

    @pl.when(core == 0)
    def _():
        store_packed(taken_act_ref, grad_two_ref[...], give_ref)

    @pl.when(core != 0)
    def _():
        store_packed(taken_zero_ref, grad, give_ref)


def back_kernel(
    grad_ref, weight_ref, hot_ref, taken_zero_ref, taken_act_ref, grad_two_ref, table_ref, halo_ref, keep_ref
):
    core = lax.axis_index("gy") % 2

    @pl.when(core == 0)
    def _():
        store_packed(taken_zero_ref, grad_ref[...], keep_ref)

    @pl.when(core != 0)
    def _():
        store_packed(taken_act_ref, grad_two_ref[...], keep_ref)

    local, halo = scatter(grad_ref[...], weight_ref, hot_ref)
    table_ref[...] = local
    halo_ref[...] = halo.astype(BF16)


def sixth_kernel(grid, width, halo_ref, keep_ref, got_ref, out_buf_ref):
    devices, rows = out_buf_ref.shape[0], out_buf_ref.shape[1] - width
    put_blocks(out_buf_ref, halo_ref[...], grid, -1, width)
    total = (keep_ref[...] + got_ref[...].astype(F32)).astype(BF16)
    out_buf_ref[:, width:, :] = total.reshape(devices, rows, LANES)


def seventh_kernel(grid, width, buf_ref, out_buf_ref, halo_ref):
    halo_ref[...] = take_blocks(buf_ref, grid, 1, width).astype(BF16)
    devices, rows = buf_ref.shape[0], buf_ref.shape[1] - width
    pieces = []
    for core in range(2):
        total = jnp.zeros((rows, LANES), F32)
        for d in range(core, devices, 2):
            total = total + buf_ref[d, width:, :].astype(F32)
        pieces.append(total.astype(BF16))
    for d in range(devices):
        out_buf_ref[d] = pieces[d % 2]


def unpack(src_ref, out_hbm, block_ref, sems):
    channels = block_ref.shape[1]
    lane = iota((channels, LANES), 1)
    copies = []

    def send(first, count):
        part = pl.ds(first, count)
        copies.append(pltpu.make_async_copy(block_ref.at[part], out_hbm.at[part], sems.at[len(copies)]))
        copies[-1].start()

    for e in range(7):
        extra = jnp.zeros((channels, LANES), F32)
        for part in range(3):
            block = 3 * e + part
            value = src_ref[block * channels : (block + 1) * channels, :].astype(F32)
            block_ref[block] = value[:, :channels]
            if e < 6:
                moved = pltpu.roll(value, 32 * (part + 1), 1)
                extra = jnp.where(lane // 32 == part, moved, extra)
        send(3 * e, 3)
        if e < 6:
            block_ref[21 + e] = extra[:, :channels]
            send(21 + e, 1)
    for copy in copies:
        copy.wait()


def own_kernel(
    counts_ref, own_ref, small_in, sums_in, halo_ref, table_ref, place_ref, grad_ref,
    one_hbm, two_hbm, small_hbm, sums_hbm, more_hbm, more_ref, block_ref, sems, small_sems,
):
    core = lax.axis_index("gy") % 2
    channels = table_ref.shape[0]
    back = table_ref[...] + tn(halo_ref[...], place_ref[...])[:channels]
    more_ref[...] = ((back + grad_ref[...]) * valid_lanes(counts_ref)).astype(BF16)
    pairs = ((small_in, small_hbm), (sums_in, sums_hbm), (more_ref, more_hbm))
    copies = [pltpu.make_async_copy(src, dst, small_sems.at[at]) for at, (src, dst) in enumerate(pairs)]
    for copy in copies:
        copy.start()

    @pl.when(core == 0)
    def _():
        unpack(own_ref, one_hbm, block_ref, sems)

    @pl.when(core != 0)
    def _():
        unpack(own_ref, two_hbm, block_ref, sems)

    for copy in copies:
        copy.wait()


def other_kernel(other_ref, one_in, two_in, one_hbm, two_hbm, block_ref, sems):
    core = lax.axis_index("gy") % 2

    @pl.when(core == 0)
    def _():
        unpack(other_ref, two_hbm, block_ref, sems)

    @pl.when(core != 0)
    def _():
        unpack(other_ref, one_hbm, block_ref, sems)


def call(kernel, outs, *args, smem=0, scratch=(), hbm=(), hbm_outs=(), aliases=None, carry=()):
    n_in, n_out = len(args), len(outs)
    aliases = dict(aliases or {})
    aliases.update({n_in + at: n_out + at for at in range(len(carry))})

    def space(at):
        if at >= n_in:
            return pl.ANY
        if at in hbm:
            return pltpu.HBM
        return pltpu.SMEM if at < smem else pltpu.VMEM

    def out_space(at):
        if at >= n_out:
            return pl.ANY
        return pltpu.HBM if at in hbm_outs else pltpu.VMEM

    def body(*refs):
        first_out = n_in + len(carry)
        kernel(*refs[:n_in], *refs[first_out : first_out + n_out], *refs[first_out + n_out + len(carry) :])

    args = [pltpu.with_memory_space_constraint(x, pltpu.HBM) if at in hbm else x for at, x in enumerate(args)]
    outs = list(outs) + [(x.shape, x.dtype) for x in carry]
    return pl.pallas_call(
        body,
        out_shape=tuple(jax.ShapeDtypeStruct(shape, dtype) for shape, dtype in outs),
        in_specs=[pl.BlockSpec(memory_space=space(at)) for at in range(n_in + len(carry))],
        out_specs=tuple(pl.BlockSpec(memory_space=out_space(at)) for at in range(len(outs))),
        scratch_shapes=list(scratch),
        input_output_aliases=aliases,
        compiler_params=pltpu.CompilerParams(vmem_limit_bytes=40 * 1024 * 1024),
    )(*args, *carry)


def to_all(x):
    return lax.all_to_all(x, AXES, 0, 0)


def swap_core(x):
    size = lax.axis_size("gy")
    return lax.ppermute(x, "gy", [(i, i ^ 1) for i in range(size)])


def on_device(
    features, kernel_map, send_rows, counts, weight_one, weight_two,
    first_norm_scale, first_norm_bias, second_norm_scale, second_norm_bias, cotangent,
):
    channels, rows = features.shape
    offsets = kernel_map.shape[0]
    width = send_rows.shape[1]
    grid = (lax.axis_size("gx"), lax.axis_size("gy"))
    devices = grid[0] * grid[1]
    flat = offsets * channels
    table = rows + 8 * width
    piece = -(-21 * channels // (devices * 16)) * 16
    packed = piece * devices
    full = (channels, rows)
    square = (LANES, LANES)
    one_flat = weight_one.reshape(flat, channels)
    two_flat = weight_two.reshape(flat, channels)
    scale_one, bias_one, scale_two, bias_two = [
        v.reshape(1, channels)
        for v in (first_norm_scale, first_norm_bias, second_norm_scale, second_norm_bias)
    ]

    taken = ((flat, LANES), BF16)
    buf, start, place, hot, one_near = call(
        functools.partial(open_kernel, grid),
        [
            ((devices, width, LANES), BF16), (full, BF16), (square, BF16),
            ((table, offsets * LANES), BF16), (one_flat.shape, BF16),
        ],
        counts, features, send_rows, kernel_map, one_flat, smem=1, hbm=(1, 2, 3, 4),
        scratch=[
            pltpu.VMEM(full, BF16), pltpu.VMEM(send_rows.shape, jnp.int32),
            pltpu.VMEM(kernel_map.shape, jnp.int32), pltpu.SemaphoreType.DMA((4,)),
        ],
    )
    buf = to_all(buf)
    buf, hidden_one, taken_zero, flag = call(
        functools.partial(first_kernel, grid),
        [((devices, width, LANES), BF16), (full, F32), taken, (square, F32)],
        counts, buf, start, hot, one_near, place, smem=1,
    )
    buf = to_all(buf)
    buf, hidden_two, taken_act, norm_one, slope_one, halo_slope, halo_cross, const_one, taken_zero = call(
        functools.partial(second_kernel, grid),
        [
            ((devices, 2, LANES), F32), (full, F32), taken, (full, F32), (full, F32),
            (square, F32), (square, F32), ((8, LANES), F32),
        ],
        counts, buf, hidden_one, flag, scale_one, bias_one, hot, two_flat,
        smem=1, scratch=[pltpu.VMEM((devices, LANES), F32)], carry=[taken_zero],
    )
    buf = to_all(buf)
    buf, output, norm_two, grad_sum, const_two, taken_zero, taken_act = call(
        third_kernel,
        [((devices, 2, LANES), F32), (full, BF16), (full, F32), (full, F32), ((8, LANES), F32)],
        counts, buf, hidden_two, start, cotangent, scale_two, bias_two, smem=1, carry=[taken_zero, taken_act],
    )
    buf = to_all(buf)
    buf, grad_two, table_two, sums_two, taken_zero, taken_act = call(
        functools.partial(fourth_kernel, grid),
        [((devices, width, LANES), BF16), (full, BF16), (full, F32), ((2, LANES), F32)],
        counts, buf, norm_two, grad_sum, const_two, two_flat, hot, norm_one, slope_one, halo_slope, halo_cross,
        smem=1, carry=[taken_zero, taken_act],
    )
    buf = to_all(buf)
    grad_one, give, grad_norms = call(
        functools.partial(fifth_kernel, grid),
        [(full, BF16), ((packed, LANES), BF16), ((4, channels), F32)],
        counts, buf, table_two, place, norm_one, slope_one, const_one, sums_two,
        taken_zero, taken_act, grad_two, smem=1,
    )
    got = swap_core(give)
    table_one, halo_one, keep = call(
        back_kernel,
        [(full, F32), (square, BF16), ((packed, LANES), F32)],
        grad_one, one_flat, hot, taken_zero, taken_act, grad_two,
    )
    (buf,) = call(
        functools.partial(sixth_kernel, grid, width),
        [((devices, width + piece, LANES), BF16)],
        halo_one, keep, got,
    )
    buf = to_all(buf)
    buf, halo = call(
        functools.partial(seventh_kernel, grid, width),
        [((devices, piece, LANES), BF16), (square, BF16)],
        buf,
    )
    own = to_all(buf).reshape(packed, LANES)
    other = swap_core(own)
    weights = [(weight_one.shape, F32), (weight_two.shape, F32)]
    blocks = [pltpu.VMEM(weight_one.shape, F32), pltpu.SemaphoreType.DMA((13,))]
    grad_weight_one, grad_weight_two, output, grad_norms, grad_features = call(
        own_kernel,
        weights + [(full, BF16), ((4, channels), F32), (full, BF16)],
        counts, own, output, grad_norms, halo, table_one, place, grad_sum, smem=1, hbm_outs=(0, 1, 2, 3, 4),
        scratch=[pltpu.VMEM(full, BF16)] + blocks + [pltpu.SemaphoreType.DMA((3,))],
    )
    grad_weight_one, grad_weight_two = call(
        other_kernel, weights, other, grad_weight_one, grad_weight_two,
        hbm=(1, 2), hbm_outs=(0, 1), scratch=blocks, aliases={1: 0, 2: 1},
    )
    return (output, grad_features, grad_weight_one, grad_weight_two, grad_norms)


def solution(mesh):
    return jax.shard_map(
        on_device,
        mesh=mesh,
        in_specs=(
            P(None, ("gx", "gy")),
            P(None, ("gx", "gy")),
            P(None, ("gx", "gy")),
            P(("gx", "gy")),
            P(),
            P(),
            P(),
            P(),
            P(),
            P(),
            P(None, ("gx", "gy")),
        ),
        out_specs=(P(None, ("gx", "gy")), P(None, ("gx", "gy")), P(), P(), P()),
        check_vma=False,
    )
```

```python
import functools

import jax
import jax.numpy as jnp
from jax import lax
from jax.experimental import pallas as pl
from jax.experimental.pallas import tpu as pltpu
from jax.sharding import PartitionSpec as P

EPS = 1e-05
STEP_LIST = ((1, 0), (-1, 0), (0, 1), (0, -1), (1, 1), (1, -1), (-1, 1), (-1, -1))
AXES = ("gx", "gy")
LANES = 128
F32 = jnp.float32
BF16 = jnp.bfloat16


def nn(a, b):
    return lax.dot_general(a, b, (((1,), (0,)), ((), ())), preferred_element_type=F32)


def nt(a, b):
    return lax.dot_general(a, b, (((1,), (1,)), ((), ())), preferred_element_type=F32)


def tn(a, b):
    return lax.dot_general(a, b, (((0,), (0,)), ((), ())), preferred_element_type=F32)


def iota(shape, dim):
    return lax.broadcasted_iota(jnp.int32, shape, dim)


def sigmoid(v):
    return 1.0 / (1.0 + jnp.exp(-v))


def neighbour(place, grid, step):
    i, j = place[0] + step[0], place[1] + step[1]
    inside = (i >= 0) & (i < grid[0]) & (j >= 0) & (j < grid[1])
    return jnp.where(inside, i * grid[1] + j, place[0] * grid[1] + place[1]), inside


def here():
    return lax.axis_index("gx"), lax.axis_index("gy")


def put_blocks(buf_ref, rows, grid, sign, width, base=None):
    place = here()
    for n, (a, b) in enumerate(STEP_LIST):
        dest, _ = neighbour(place, grid, (sign * a, sign * b))
        block = rows[n * width : (n + 1) * width]
        if base is not None:
            block = jnp.where(iota(block.shape, 1) < 96, block, base)
        buf_ref[dest, 0:width, :] = block.astype(BF16)


def take_blocks(buf_ref, grid, sign, width):
    place = here()
    blocks = []
    for a, b in STEP_LIST:
        src, inside = neighbour(place, grid, (sign * a, sign * b))
        block = buf_ref[src, 0:width, :].astype(F32)
        blocks.append(jnp.where(inside, block, 0.0))
    return jnp.concatenate(blocks, axis=0)


def pad_to(x, rows, lanes):
    if x.shape[1] < lanes:
        x = jnp.concatenate([x, jnp.zeros((x.shape[0], lanes - x.shape[1]), x.dtype)], axis=1)
    if x.shape[0] < rows:
        x = jnp.concatenate([x, jnp.zeros((rows - x.shape[0], lanes), x.dtype)], axis=0)
    return x


def turn(x):
    return pad_to(x, LANES, LANES).T


def lane_sums(x):
    return jnp.sum(turn(x), axis=0, keepdims=True)


def rows_to_cols(rows, channels):
    return [jnp.broadcast_to(row, (LANES, LANES)).T[:channels] for row in rows]


def centre(hidden, counts_ref):
    count = counts_ref[0].astype(F32)
    mask = (iota((LANES, LANES), 0) < counts_ref[0]).astype(F32)
    turned = turn(hidden)
    sums = jnp.sum(turned * mask, axis=0, keepdims=True)
    centred = (turned - sums / count) * mask
    return sums, centred, jnp.sum(centred * centred, axis=0, keepdims=True)


def split3(x):
    high = x.astype(BF16).astype(F32)
    mid = (x - high).astype(BF16).astype(F32)
    low = (x - high - mid).astype(BF16).astype(F32)
    return [high, mid, low]


def pack_rows(pieces, last):
    sub = iota((16, LANES), 0)
    lane = iota((16, LANES), 1)
    total = jnp.zeros((16, LANES), F32)
    for q, piece in enumerate(pieces):
        total = jnp.where(sub // 3 == q, piece, total)
    part = sub % 3
    moved = jnp.where(
        part == 0,
        pltpu.roll(total, 96, 1),
        jnp.where(part == 1, pltpu.roll(total, 64, 1), pltpu.roll(total, 32, 1)),
    )
    moved = jnp.where(sub == 15, last, moved)
    return jnp.where(lane >= 96, moved, 0.0)


def unpack_rows(tiles, groups):
    devices = tiles.shape[0]
    flat = tiles.reshape(devices * 16, LANES)
    sub = iota(tiles.shape, 1)
    lane = iota(tiles.shape, 2)
    part = sub % 3
    moved = [pltpu.roll(flat, 32 * (p + 1), 1).reshape(tiles.shape) for p in range(3)]
    value = jnp.where(part == 0, moved[0], jnp.where(part == 1, moved[1], moved[2]))
    value = jnp.where((lane // 32 == part) & (sub < 15), value, 0.0)
    results = []
    for low, high in groups:
        mask = (sub >= 3 * low) & (sub < 3 * high)
        results.append(jnp.sum(jnp.where(mask, value, 0.0), axis=1))
    return results


def valid_lanes(counts_ref, rows=1):
    return (iota((rows, LANES), 1) < counts_ref[0]).astype(F32)


def open_kernel(
    grid, counts_ref, features_hbm, send_hbm, map_hbm, one_hbm,
    buf_ref, start_ref, place_ref, hot_ref, one_ref, features_ref, send_ref, map_ref, sems,
):
    pairs = ((features_hbm, features_ref), (send_hbm, send_ref), (map_hbm, map_ref), (one_hbm, one_ref))
    copies = [pltpu.make_async_copy(src, dst, sems.at[at]) for at, (src, dst) in enumerate(pairs)]
    for copy in copies:
        copy.start()
    for copy in copies[:2]:
        copy.wait()
    width = send_ref.shape[1]
    send = send_ref[...].astype(F32).astype(BF16)
    spread = jnp.where(iota((width, LANES), 1) % width == iota((width, LANES), 0), 1.0, 0.0).astype(BF16)
    wide = nn(send, spread)
    wide = jnp.where(iota(wide.shape, 1) // width == iota(wide.shape, 0), wide, 0.0)
    row = jnp.sum(wide, axis=0, keepdims=True)
    place = jnp.where(row == iota((LANES, LANES), 0).astype(F32), 1.0, 0.0).T.astype(BF16)
    place_ref[...] = place
    valid = valid_lanes(counts_ref)
    start = features_ref[...].astype(F32) * valid
    start_ref[...] = start.astype(BF16)
    extra = jnp.where(iota((LANES - 96, LANES), 0) == 0, valid, 0.0)
    rows = nt(place, jnp.concatenate([start, extra], axis=0).astype(BF16))
    put_blocks(buf_ref, rows, grid, 1, width)
    copies[2].wait()
    sub = iota((hot_ref.shape[0], LANES), 0).astype(jnp.int16)
    columns = map_ref[...].astype(jnp.int16)
    one, zero = jnp.ones(sub.shape, BF16), jnp.zeros(sub.shape, BF16)
    for k in range(map_ref.shape[0]):
        hot_ref[:, k * LANES : (k + 1) * LANES] = jnp.where(sub == columns[k : k + 1, :], one, zero)
    copies[3].wait()


def gather(tables, hot_ref, taken_refs):
    channels = tables[0].shape[0]
    taken = nn(jnp.concatenate(tables, axis=0), hot_ref[...]).astype(BF16)
    for at, ref in enumerate(taken_refs):
        for k in range(hot_ref.shape[1] // LANES):
            ref[k * channels : (k + 1) * channels, :] = taken[
                at * channels : (at + 1) * channels, k * LANES : (k + 1) * LANES
            ]


def gather_convolve(table, hot_ref, weight_ref, taken_ref):
    gather([table], hot_ref, [taken_ref])
    return tn(weight_ref[...], taken_ref[...])


def first_kernel(
    grid, counts_ref, buf_ref, start_ref, hot_ref, weight_ref, place_ref,
    out_buf_ref, hidden_ref, taken_ref, flag_ref,
):
    width = buf_ref.shape[1]
    channels = start_ref.shape[0]
    halo_rows = take_blocks(buf_ref, grid, -1, width)
    flag_ref[...] = jnp.broadcast_to(halo_rows[:, 96:97], (LANES, LANES))
    halo = halo_rows.T[:channels].astype(BF16)
    table = jnp.concatenate([start_ref[...], halo], axis=1)
    hidden = gather_convolve(table, hot_ref, weight_ref, taken_ref)
    hidden_ref[...] = hidden
    sums, centred, spread = centre(hidden, counts_ref)
    base = pack_rows(split3(sums) + split3(spread)[:2], counts_ref[0].astype(F32))
    out_buf_ref[...] = jnp.broadcast_to(base.astype(BF16)[None], out_buf_ref.shape)
    rows = nn(place_ref[...], centred.astype(BF16))
    put_blocks(out_buf_ref, rows, grid, 1, width, base)


def second_kernel(
    grid, counts_ref, buf_ref, hidden_ref, flag_ref, scale_ref, bias_ref, hot_ref, weight_ref,
    out_buf_ref, hidden_two_ref, taken_ref, norm_ref, slope_ref, halo_slope_ref, halo_cross_ref,
    const_ref, mean_ref,
):
    width = buf_ref.shape[1]
    channels = hidden_ref.shape[0]
    tiles = buf_ref[...].astype(F32)
    sums, spreads = unpack_rows(tiles, ((0, 3), (3, 5)))
    counts = tiles[:, 15, 96:97]
    total = jnp.sum(counts, axis=0, keepdims=True)
    means = sums / counts
    mean_ref[...] = means
    mean = jnp.sum(sums, axis=0, keepdims=True) / total
    apart = means - mean
    var = jnp.sum(spreads + counts * apart * apart, axis=0, keepdims=True) / total
    rstd = lax.rsqrt(var + EPS)
    scale = pad_to(scale_ref[...], 1, LANES)
    bias = pad_to(bias_ref[...], 1, LANES)
    total_row = jnp.broadcast_to(total, (1, LANES))
    mean_c, rstd_c, scale_c, bias_c = rows_to_cols([mean, rstd, scale, bias], channels)
    sub = iota((8, LANES), 0)
    const_ref[...] = jnp.where(sub == 0, scale * rstd, jnp.where(sub == 1, total_row, 0.0))

    valid = valid_lanes(counts_ref)
    normal = (hidden_ref[...] - mean_c) * rstd_c
    norm_ref[...] = normal
    linear = scale_c * normal + bias_c
    sig = sigmoid(linear)
    slope_ref[...] = sig * (1.0 + linear * (1.0 - sig)) * valid
    act = (linear * sig * valid).astype(BF16)

    place = here()
    lifted = []
    for n, (a, b) in enumerate(STEP_LIST):
        src, inside = neighbour(place, grid, (-a, -b))
        block = buf_ref[src, 0:width, :].astype(F32) + mean_ref[pl.ds(src, 1), :]
        lifted.append(jnp.where(inside, block, 0.0))
    lane = iota((LANES, LANES), 1)
    halo = jnp.where(lane < channels, jnp.concatenate(lifted, axis=0), 0.0)
    flag = flag_ref[...]
    halo_normal = (halo - mean) * rstd
    halo_linear = scale * halo_normal + bias
    halo_sig = sigmoid(halo_linear)
    halo_slope = halo_sig * (1.0 + halo_linear * (1.0 - halo_sig)) * flag
    halo_slope_ref[...] = halo_slope
    halo_cross_ref[...] = halo_slope * halo_normal
    halo_act = (halo_linear * halo_sig * flag).T[:channels].astype(BF16)

    table = jnp.concatenate([act, halo_act], axis=1)
    hidden = gather_convolve(table, hot_ref, weight_ref, taken_ref)
    hidden_two_ref[...] = hidden
    sums_two, _, spread_two = centre(hidden, counts_ref)
    stat = jnp.concatenate([sums_two, spread_two], axis=0)
    stat = jnp.where(iota((2, LANES), 1) < 96, stat, counts_ref[0].astype(F32))
    out_buf_ref[...] = jnp.broadcast_to(stat[None], out_buf_ref.shape)


def third_kernel(
    counts_ref, buf_ref, hidden_ref, start_ref, cotangent_ref, scale_ref, bias_ref,
    out_buf_ref, output_ref, norm_ref, grad_ref, const_ref,
):
    channels = hidden_ref.shape[0]
    sums = buf_ref[:, 0, :]
    spreads = buf_ref[:, 1, :]
    counts = sums[:, 96:97]
    total = jnp.sum(counts, axis=0, keepdims=True)
    mean = jnp.sum(sums, axis=0, keepdims=True) / total
    apart = sums / counts - mean
    var = jnp.sum(spreads + counts * apart * apart, axis=0, keepdims=True) / total
    rstd = lax.rsqrt(var + EPS)
    scale = pad_to(scale_ref[...], 1, LANES)
    bias = pad_to(bias_ref[...], 1, LANES)
    total_row = jnp.broadcast_to(total, (1, LANES))
    mean_c, rstd_c, scale_c, bias_c = rows_to_cols([mean, rstd, scale, bias], channels)
    sub = iota((8, LANES), 0)
    const_ref[...] = jnp.where(sub == 0, scale * rstd, jnp.where(sub == 1, total_row, 0.0))
    valid = valid_lanes(counts_ref)
    normal = (hidden_ref[...] - mean_c) * rstd_c
    norm_ref[...] = normal
    summed = scale_c * normal + bias_c + start_ref[...].astype(F32)
    sig = sigmoid(summed)
    output_ref[...] = (summed * sig * valid).astype(BF16)
    grad = cotangent_ref[...].astype(F32) * valid * (sig * (1.0 + summed * (1.0 - sig)))
    grad_ref[...] = grad
    rows = jnp.concatenate([lane_sums(grad * normal * valid), lane_sums(grad)], axis=0)
    out_buf_ref[...] = jnp.broadcast_to(rows[None], out_buf_ref.shape)


def scatter(grad, weight_ref, hot_ref):
    channels = grad.shape[0]
    terms = nn(weight_ref[...], grad).astype(BF16)
    offsets = hot_ref.shape[1] // LANES
    wide = jnp.concatenate([terms[k * channels : (k + 1) * channels] for k in range(offsets)], axis=1)
    table = pad_to(nt(hot_ref[...], wide), hot_ref.shape[0], LANES)
    return table[:LANES].T[:channels], table[LANES : 2 * LANES]


def row_gradient(grad, normal, const, dgain, dbias, valid):
    channels = grad.shape[0]
    factor, part_bias, part_gain = rows_to_cols(
        [const[0:1], dbias / const[1:2], dgain / const[1:2]], channels
    )
    return (factor * (grad - (part_bias + normal * part_gain)) * valid).astype(BF16)


def fourth_kernel(
    grid, counts_ref, buf_ref, norm_ref, grad_ref, const_ref, weight_ref, hot_ref,
    norm_one_ref, slope_ref, halo_slope_ref, halo_cross_ref,
    out_buf_ref, grad_two_ref, table_ref, sums_ref,
):
    channels = norm_ref.shape[0]
    width = out_buf_ref.shape[1]
    valid = valid_lanes(counts_ref)
    both = jnp.sum(buf_ref[...], axis=0)
    sums_ref[...] = both
    grad = row_gradient(grad_ref[...], norm_ref[...], const_ref[...], both[0:1], both[1:2], valid)
    grad_two_ref[...] = grad
    local, halo = scatter(grad, weight_ref, hot_ref)
    table_ref[...] = local
    pulled = local * slope_ref[...]
    dgain = lane_sums(pulled * norm_one_ref[...]) + jnp.sum(halo * halo_cross_ref[...], axis=0, keepdims=True)
    dbias = lane_sums(pulled) + jnp.sum(halo * halo_slope_ref[...], axis=0, keepdims=True)
    base = pack_rows(split3(dgain)[:2] + split3(dbias)[:2], 0.0)
    out_buf_ref[...] = jnp.broadcast_to(base.astype(BF16)[None], out_buf_ref.shape)
    put_blocks(out_buf_ref, halo, grid, -1, width, base)


def packed_weight_grad(taken_ref, grad, put):
    channels = grad.shape[0]
    zero = jnp.zeros((channels, LANES), BF16)

    def taken(k):
        return taken_ref[k * channels : (k + 1) * channels, :]

    for part in range(3):
        upper = jnp.concatenate([grad, zero], axis=1)
        lower = jnp.concatenate([zero[:32], grad[32 * part : 32 * part + 32]], axis=1)
        right = jnp.concatenate([upper, lower], axis=0)
        left = jnp.concatenate(
            [
                jnp.concatenate([taken(3 * e + part) for e in range(6)], axis=0),
                jnp.concatenate([taken(21 + e) for e in range(6)], axis=0),
            ],
            axis=1,
        )
        result = nt(left, right)
        for e in range(6):
            put(3 * e + part, result[e * channels : (e + 1) * channels])
    last = nt(taken_ref[18 * channels : 21 * channels, :], pad_to(grad, LANES, LANES))
    for e in range(3):
        put(18 + e, last[e * channels : (e + 1) * channels])


def store_packed(taken_ref, grad, ref):
    channels = grad.shape[0]
    used = 21 * channels

    def put(block, value):
        ref[block * channels : (block + 1) * channels, :] = value.astype(ref.dtype)

    packed_weight_grad(taken_ref, grad, put)
    if ref.shape[0] > used:
        ref[used:, :] = jnp.zeros((ref.shape[0] - used, LANES), ref.dtype)


def fifth_kernel(
    grid, counts_ref, buf_ref, table_ref, place_ref, norm_ref, slope_ref, const_ref, sums_two_ref,
    taken_zero_ref, taken_act_ref, grad_two_ref,
    grad_one_ref, give_ref, sums_ref,
):
    width = buf_ref.shape[1]
    channels = norm_ref.shape[0]
    valid = valid_lanes(counts_ref)
    dgain, dbias = unpack_rows(
        jnp.sum(buf_ref[...].astype(F32), axis=0, keepdims=True), ((0, 2), (2, 4))
    )
    two = sums_two_ref[...]
    sums_ref[...] = jnp.concatenate([dgain, dbias, two], axis=0)[:, :channels]
    arrived = take_blocks(buf_ref, grid, 1, width).astype(BF16)
    back = table_ref[...] + tn(arrived, place_ref[...])[:channels]
    grad = row_gradient(back * slope_ref[...], norm_ref[...], const_ref[...], dgain, dbias, valid)
    grad_one_ref[...] = grad
    core = lax.axis_index("gy") % 2

    @pl.when(core == 0)
    def _():
        store_packed(taken_act_ref, grad_two_ref[...], give_ref)

    @pl.when(core != 0)
    def _():
        store_packed(taken_zero_ref, grad, give_ref)


def back_kernel(
    grad_ref, weight_ref, hot_ref, taken_zero_ref, taken_act_ref, grad_two_ref, table_ref, halo_ref, keep_ref
):
    core = lax.axis_index("gy") % 2

    @pl.when(core == 0)
    def _():
        store_packed(taken_zero_ref, grad_ref[...], keep_ref)

    @pl.when(core != 0)
    def _():
        store_packed(taken_act_ref, grad_two_ref[...], keep_ref)

    local, halo = scatter(grad_ref[...], weight_ref, hot_ref)
    table_ref[...] = local
    halo_ref[...] = halo.astype(BF16)


def sixth_kernel(grid, width, halo_ref, keep_ref, got_ref, out_buf_ref):
    devices, rows = out_buf_ref.shape[0], out_buf_ref.shape[1] - width
    put_blocks(out_buf_ref, halo_ref[...], grid, -1, width)
    total = (keep_ref[...] + got_ref[...].astype(F32)).astype(BF16)
    out_buf_ref[:, width:, :] = total.reshape(devices, rows, LANES)


def seventh_kernel(grid, width, buf_ref, out_buf_ref, halo_ref):
    halo_ref[...] = take_blocks(buf_ref, grid, 1, width).astype(BF16)
    devices, rows = buf_ref.shape[0], buf_ref.shape[1] - width
    pieces = []
    for core in range(2):
        total = jnp.zeros((rows, LANES), F32)
        for d in range(core, devices, 2):
            total = total + buf_ref[d, width:, :].astype(F32)
        pieces.append(total.astype(BF16))
    for d in range(devices):
        out_buf_ref[d] = pieces[d % 2]


def unpack(src_ref, out_hbm, block_ref, sems):
    channels = block_ref.shape[1]
    lane = iota((channels, LANES), 1)
    copies = []

    def send(first, count):
        part = pl.ds(first, count)
        copies.append(pltpu.make_async_copy(block_ref.at[part], out_hbm.at[part], sems.at[len(copies)]))
        copies[-1].start()

    for e in range(7):
        extra = jnp.zeros((channels, LANES), F32)
        for part in range(3):
            block = 3 * e + part
            value = src_ref[block * channels : (block + 1) * channels, :].astype(F32)
            block_ref[block] = value[:, :channels]
            if e < 6:
                moved = pltpu.roll(value, 32 * (part + 1), 1)
                extra = jnp.where(lane // 32 == part, moved, extra)
        send(3 * e, 3)
        if e < 6:
            block_ref[21 + e] = extra[:, :channels]
            send(21 + e, 1)
    for copy in copies:
        copy.wait()


def own_kernel(
    counts_ref, own_ref, small_in, sums_in, halo_ref, table_ref, place_ref, grad_ref,
    one_hbm, two_hbm, small_hbm, sums_hbm, more_hbm, more_ref, block_ref, sems, small_sems,
):
    core = lax.axis_index("gy") % 2
    channels = table_ref.shape[0]
    back = table_ref[...] + tn(halo_ref[...], place_ref[...])[:channels]
    more_ref[...] = ((back + grad_ref[...]) * valid_lanes(counts_ref)).astype(BF16)
    pairs = ((small_in, small_hbm), (sums_in, sums_hbm), (more_ref, more_hbm))
    copies = [pltpu.make_async_copy(src, dst, small_sems.at[at]) for at, (src, dst) in enumerate(pairs)]
    for copy in copies:
        copy.start()

    @pl.when(core == 0)
    def _():
        unpack(own_ref, one_hbm, block_ref, sems)

    @pl.when(core != 0)
    def _():
        unpack(own_ref, two_hbm, block_ref, sems)

    for copy in copies:
        copy.wait()


def other_kernel(other_ref, one_in, two_in, one_hbm, two_hbm, block_ref, sems):
    core = lax.axis_index("gy") % 2

    @pl.when(core == 0)
    def _():
        unpack(other_ref, two_hbm, block_ref, sems)

    @pl.when(core != 0)
    def _():
        unpack(other_ref, one_hbm, block_ref, sems)


def call(kernel, outs, *args, smem=0, scratch=(), hbm=(), hbm_outs=(), aliases=None, carry=()):
    n_in, n_out = len(args), len(outs)
    aliases = dict(aliases or {})
    aliases.update({n_in + at: n_out + at for at in range(len(carry))})

    def space(at):
        if at >= n_in:
            return pl.ANY
        if at in hbm:
            return pltpu.HBM
        return pltpu.SMEM if at < smem else pltpu.VMEM

    def out_space(at):
        if at >= n_out:
            return pl.ANY
        return pltpu.HBM if at in hbm_outs else pltpu.VMEM

    def body(*refs):
        first_out = n_in + len(carry)
        kernel(*refs[:n_in], *refs[first_out : first_out + n_out], *refs[first_out + n_out + len(carry) :])

    args = [pltpu.with_memory_space_constraint(x, pltpu.HBM) if at in hbm else x for at, x in enumerate(args)]
    outs = list(outs) + [(x.shape, x.dtype) for x in carry]
    return pl.pallas_call(
        body,
        out_shape=tuple(jax.ShapeDtypeStruct(shape, dtype) for shape, dtype in outs),
        in_specs=[pl.BlockSpec(memory_space=space(at)) for at in range(n_in + len(carry))],
        out_specs=tuple(pl.BlockSpec(memory_space=out_space(at)) for at in range(len(outs))),
        scratch_shapes=list(scratch),
        input_output_aliases=aliases,
        compiler_params=pltpu.CompilerParams(vmem_limit_bytes=40 * 1024 * 1024),
    )(*args, *carry)


def to_all(x):
    return lax.all_to_all(x, AXES, 0, 0)


def swap_core(x):
    size = lax.axis_size("gy")
    return lax.ppermute(x, "gy", [(i, i ^ 1) for i in range(size)])


def on_device(
    features, kernel_map, send_rows, counts, weight_one, weight_two,
    first_norm_scale, first_norm_bias, second_norm_scale, second_norm_bias, cotangent,
):
    channels, rows = features.shape
    offsets = kernel_map.shape[0]
    width = send_rows.shape[1]
    grid = (lax.axis_size("gx"), lax.axis_size("gy"))
    devices = grid[0] * grid[1]
    flat = offsets * channels
    table = rows + 8 * width
    piece = -(-21 * channels // (devices * 16)) * 16
    packed = piece * devices
    full = (channels, rows)
    square = (LANES, LANES)
    one_flat = weight_one.reshape(flat, channels)
    two_flat = weight_two.reshape(flat, channels)
    scale_one, bias_one, scale_two, bias_two = [
        v.reshape(1, channels)
        for v in (first_norm_scale, first_norm_bias, second_norm_scale, second_norm_bias)
    ]

    taken = ((flat, LANES), BF16)
    buf, start, place, hot, one_near = call(
        functools.partial(open_kernel, grid),
        [
            ((devices, width, LANES), BF16), (full, BF16), (square, BF16),
            ((table, offsets * LANES), BF16), (one_flat.shape, BF16),
        ],
        counts, features, send_rows, kernel_map, one_flat, smem=1, hbm=(1, 2, 3, 4),
        scratch=[
            pltpu.VMEM(full, BF16), pltpu.VMEM(send_rows.shape, jnp.int32),
            pltpu.VMEM(kernel_map.shape, jnp.int32), pltpu.SemaphoreType.DMA((4,)),
        ],
    )
    buf = to_all(buf)
    buf, hidden_one, taken_zero, flag = call(
        functools.partial(first_kernel, grid),
        [((devices, width, LANES), BF16), (full, F32), taken, (square, F32)],
        counts, buf, start, hot, one_near, place, smem=1,
    )
    buf = to_all(buf)
    buf, hidden_two, taken_act, norm_one, slope_one, halo_slope, halo_cross, const_one, taken_zero = call(
        functools.partial(second_kernel, grid),
        [
            ((devices, 2, LANES), F32), (full, F32), taken, (full, F32), (full, F32),
            (square, F32), (square, F32), ((8, LANES), F32),
        ],
        counts, buf, hidden_one, flag, scale_one, bias_one, hot, two_flat,
        smem=1, scratch=[pltpu.VMEM((devices, LANES), F32)], carry=[taken_zero],
    )
    buf = to_all(buf)
    buf, output, norm_two, grad_sum, const_two, taken_zero, taken_act = call(
        third_kernel,
        [((devices, 2, LANES), F32), (full, BF16), (full, F32), (full, F32), ((8, LANES), F32)],
        counts, buf, hidden_two, start, cotangent, scale_two, bias_two, smem=1, carry=[taken_zero, taken_act],
    )
    buf = to_all(buf)
    buf, grad_two, table_two, sums_two, taken_zero, taken_act = call(
        functools.partial(fourth_kernel, grid),
        [((devices, width, LANES), BF16), (full, BF16), (full, F32), ((2, LANES), F32)],
        counts, buf, norm_two, grad_sum, const_two, two_flat, hot, norm_one, slope_one, halo_slope, halo_cross,
        smem=1, carry=[taken_zero, taken_act],
    )
    buf = to_all(buf)
    grad_one, give, grad_norms = call(
        functools.partial(fifth_kernel, grid),
        [(full, BF16), ((packed, LANES), BF16), ((4, channels), F32)],
        counts, buf, table_two, place, norm_one, slope_one, const_one, sums_two,
        taken_zero, taken_act, grad_two, smem=1,
    )
    got = swap_core(give)
    table_one, halo_one, keep = call(
        back_kernel,
        [(full, F32), (square, BF16), ((packed, LANES), F32)],
        grad_one, one_flat, hot, taken_zero, taken_act, grad_two,
    )
    (buf,) = call(
        functools.partial(sixth_kernel, grid, width),
        [((devices, width + piece, LANES), BF16)],
        halo_one, keep, got,
    )
    buf = to_all(buf)
    buf, halo = call(
        functools.partial(seventh_kernel, grid, width),
        [((devices, piece, LANES), BF16), (square, BF16)],
        buf,
    )
    own = to_all(buf).reshape(packed, LANES)
    other = swap_core(own)
    weights = [(weight_one.shape, F32), (weight_two.shape, F32)]
    blocks = [pltpu.VMEM(weight_one.shape, F32), pltpu.SemaphoreType.DMA((13,))]
    grad_weight_one, grad_weight_two, output, grad_norms, grad_features = call(
        own_kernel,
        weights + [(full, BF16), ((4, channels), F32), (full, BF16)],
        counts, own, output, grad_norms, halo, table_one, place, grad_sum, smem=1, hbm_outs=(0, 1, 2, 3, 4),
        scratch=[pltpu.VMEM(full, BF16)] + blocks + [pltpu.SemaphoreType.DMA((3,))],
    )
    grad_weight_one, grad_weight_two = call(
        other_kernel, weights, other, grad_weight_one, grad_weight_two,
        hbm=(1, 2), hbm_outs=(0, 1), scratch=blocks, aliases={1: 0, 2: 1},
    )
    return (output, grad_features, grad_weight_one, grad_weight_two, grad_norms)


def solution(mesh):
    return jax.shard_map(
        on_device,
        mesh=mesh,
        in_specs=(
            P(None, ("gx", "gy")),
            P(None, ("gx", "gy")),
            P(None, ("gx", "gy")),
            P(("gx", "gy")),
            P(),
            P(),
            P(),
            P(),
            P(),
            P(),
            P(None, ("gx", "gy")),
        ),
        out_specs=(P(None, ("gx", "gy")), P(None, ("gx", "gy")), P(), P(), P()),
        check_vma=False,
    )
```

```python
import functools

import jax
import jax.numpy as jnp
from jax import lax
from jax.experimental import pallas as pl
from jax.experimental.pallas import tpu as pltpu
from jax.sharding import PartitionSpec as P

EPS = 1e-05
STEP_LIST = ((1, 0), (-1, 0), (0, 1), (0, -1), (1, 1), (1, -1), (-1, 1), (-1, -1))
AXES = ("gx", "gy")
LANES = 128
F32 = jnp.float32
BF16 = jnp.bfloat16


def nn(a, b):
    return lax.dot_general(a, b, (((1,), (0,)), ((), ())), preferred_element_type=F32)


def nt(a, b):
    return lax.dot_general(a, b, (((1,), (1,)), ((), ())), preferred_element_type=F32)


def tn(a, b):
    return lax.dot_general(a, b, (((0,), (0,)), ((), ())), preferred_element_type=F32)


def iota(shape, dim):
    return lax.broadcasted_iota(jnp.int32, shape, dim)


def sigmoid(v):
    return 1.0 / (1.0 + jnp.exp(-v))


def neighbour(place, grid, step):
    i, j = place[0] + step[0], place[1] + step[1]
    inside = (i >= 0) & (i < grid[0]) & (j >= 0) & (j < grid[1])
    return jnp.where(inside, i * grid[1] + j, place[0] * grid[1] + place[1]), inside


def here():
    return lax.axis_index("gx"), lax.axis_index("gy")


def put_blocks(buf_ref, rows, grid, sign, width, base=None):
    place = here()
    for n, (a, b) in enumerate(STEP_LIST):
        dest, _ = neighbour(place, grid, (sign * a, sign * b))
        block = rows[n * width : (n + 1) * width]
        if base is not None:
            block = jnp.where(iota(block.shape, 1) < 96, block, base)
        buf_ref[dest, 0:width, :] = block.astype(BF16)


def take_blocks(buf_ref, grid, sign, width):
    place = here()
    blocks = []
    for a, b in STEP_LIST:
        src, inside = neighbour(place, grid, (sign * a, sign * b))
        block = buf_ref[src, 0:width, :].astype(F32)
        blocks.append(jnp.where(inside, block, 0.0))
    return jnp.concatenate(blocks, axis=0)


def pad_to(x, rows, lanes):
    if x.shape[1] < lanes:
        x = jnp.concatenate([x, jnp.zeros((x.shape[0], lanes - x.shape[1]), x.dtype)], axis=1)
    if x.shape[0] < rows:
        x = jnp.concatenate([x, jnp.zeros((rows - x.shape[0], lanes), x.dtype)], axis=0)
    return x


def turn(x):
    return pad_to(x, LANES, LANES).T


def lane_sums(x):
    return jnp.sum(turn(x), axis=0, keepdims=True)


def rows_to_cols(rows, channels):
    return [jnp.broadcast_to(row, (LANES, LANES)).T[:channels] for row in rows]


def centre(hidden, counts_ref):
    count = counts_ref[0].astype(F32)
    mask = (iota((LANES, LANES), 0) < counts_ref[0]).astype(F32)
    turned = turn(hidden)
    sums = jnp.sum(turned * mask, axis=0, keepdims=True)
    centred = (turned - sums / count) * mask
    return sums, centred, jnp.sum(centred * centred, axis=0, keepdims=True)


def split3(x):
    high = x.astype(BF16).astype(F32)
    mid = (x - high).astype(BF16).astype(F32)
    low = (x - high - mid).astype(BF16).astype(F32)
    return [high, mid, low]


def pack_rows(pieces, last):
    sub = iota((16, LANES), 0)
    lane = iota((16, LANES), 1)
    total = jnp.zeros((16, LANES), F32)
    for q, piece in enumerate(pieces):
        total = jnp.where(sub // 3 == q, piece, total)
    part = sub % 3
    moved = jnp.where(
        part == 0,
        pltpu.roll(total, 96, 1),
        jnp.where(part == 1, pltpu.roll(total, 64, 1), pltpu.roll(total, 32, 1)),
    )
    moved = jnp.where(sub == 15, last, moved)
    return jnp.where(lane >= 96, moved, 0.0)


def unpack_rows(tiles, groups):
    devices = tiles.shape[0]
    flat = tiles.reshape(devices * 16, LANES)
    sub = iota(tiles.shape, 1)
    lane = iota(tiles.shape, 2)
    part = sub % 3
    moved = [pltpu.roll(flat, 32 * (p + 1), 1).reshape(tiles.shape) for p in range(3)]
    value = jnp.where(part == 0, moved[0], jnp.where(part == 1, moved[1], moved[2]))
    value = jnp.where((lane // 32 == part) & (sub < 15), value, 0.0)
    results = []
    for low, high in groups:
        mask = (sub >= 3 * low) & (sub < 3 * high)
        results.append(jnp.sum(jnp.where(mask, value, 0.0), axis=1))
    return results


def valid_lanes(counts_ref, rows=1):
    return (iota((rows, LANES), 1) < counts_ref[0]).astype(F32)


def open_kernel(
    grid, counts_ref, features_hbm, send_hbm, map_hbm, one_hbm,
    buf_ref, start_ref, place_ref, hot_ref, one_ref, features_ref, send_ref, map_ref, sems,
):
    pairs = ((features_hbm, features_ref), (send_hbm, send_ref), (map_hbm, map_ref), (one_hbm, one_ref))
    copies = [pltpu.make_async_copy(src, dst, sems.at[at]) for at, (src, dst) in enumerate(pairs)]
    for copy in copies:
        copy.start()
    for copy in copies[:3]:
        copy.wait()
    width = send_ref.shape[1]
    send = pad_to(send_ref[...].astype(F32), LANES, LANES).T
    lane = iota((width, LANES), 1).astype(F32)
    place = jnp.concatenate(
        [jnp.where(lane == send[:width, n : n + 1], 1.0, 0.0) for n in range(send_ref.shape[0])], axis=0
    ).astype(BF16)
    place_ref[...] = place
    valid = valid_lanes(counts_ref)
    start = features_ref[...].astype(F32) * valid
    start_ref[...] = start.astype(BF16)
    extra = jnp.where(iota((LANES - 96, LANES), 0) == 0, valid, 0.0)
    rows = nt(place, jnp.concatenate([start, extra], axis=0).astype(BF16))
    put_blocks(buf_ref, rows, grid, 1, width)
    sub = iota((hot_ref.shape[0], LANES), 0).astype(jnp.int16)
    columns = map_ref[...].astype(jnp.int16)
    one, zero = jnp.ones(sub.shape, BF16), jnp.zeros(sub.shape, BF16)
    for k in range(map_ref.shape[0]):
        hot_ref[:, k * LANES : (k + 1) * LANES] = jnp.where(sub == columns[k : k + 1, :], one, zero)
    copies[3].wait()


def gather(tables, hot_ref, taken_refs):
    channels = tables[0].shape[0]
    taken = nn(jnp.concatenate(tables, axis=0), hot_ref[...]).astype(BF16)
    for at, ref in enumerate(taken_refs):
        for k in range(hot_ref.shape[1] // LANES):
            ref[k * channels : (k + 1) * channels, :] = taken[
                at * channels : (at + 1) * channels, k * LANES : (k + 1) * LANES
            ]


def gather_convolve(table, hot_ref, weight_ref, taken_ref):
    gather([table], hot_ref, [taken_ref])
    return tn(weight_ref[...], taken_ref[...])


def first_kernel(
    grid, counts_ref, buf_ref, start_ref, hot_ref, weight_ref, place_ref,
    out_buf_ref, hidden_ref, taken_ref, flag_ref,
):
    width = buf_ref.shape[1]
    channels = start_ref.shape[0]
    halo_rows = take_blocks(buf_ref, grid, -1, width)
    flag_ref[...] = jnp.broadcast_to(halo_rows[:, 96:97], (LANES, LANES))
    halo = halo_rows.T[:channels].astype(BF16)
    table = jnp.concatenate([start_ref[...], halo], axis=1)
    hidden = gather_convolve(table, hot_ref, weight_ref, taken_ref)
    hidden_ref[...] = hidden
    sums, centred, spread = centre(hidden, counts_ref)
    base = pack_rows(split3(sums) + split3(spread)[:2], counts_ref[0].astype(F32))
    out_buf_ref[...] = jnp.broadcast_to(base.astype(BF16)[None], out_buf_ref.shape)
    rows = nn(place_ref[...], centred.astype(BF16))
    put_blocks(out_buf_ref, rows, grid, 1, width, base)


def second_kernel(
    grid, counts_ref, buf_ref, hidden_ref, flag_ref, scale_ref, bias_ref, hot_ref, weight_ref,
    out_buf_ref, hidden_two_ref, taken_ref, norm_ref, slope_ref, halo_slope_ref, halo_cross_ref,
    const_ref, mean_ref,
):
    width = buf_ref.shape[1]
    channels = hidden_ref.shape[0]
    tiles = buf_ref[...].astype(F32)
    sums, spreads = unpack_rows(tiles, ((0, 3), (3, 5)))
    counts = tiles[:, 15, 96:97]
    total = jnp.sum(counts, axis=0, keepdims=True)
    means = sums / counts
    mean_ref[...] = means
    mean = jnp.sum(sums, axis=0, keepdims=True) / total
    apart = means - mean
    var = jnp.sum(spreads + counts * apart * apart, axis=0, keepdims=True) / total
    rstd = lax.rsqrt(var + EPS)
    scale = pad_to(scale_ref[...], 1, LANES)
    bias = pad_to(bias_ref[...], 1, LANES)
    total_row = jnp.broadcast_to(total, (1, LANES))
    mean_c, rstd_c, scale_c, bias_c = rows_to_cols([mean, rstd, scale, bias], channels)
    sub = iota((8, LANES), 0)
    const_ref[...] = jnp.where(sub == 0, scale * rstd, jnp.where(sub == 1, total_row, 0.0))

    valid = valid_lanes(counts_ref)
    normal = (hidden_ref[...] - mean_c) * rstd_c
    norm_ref[...] = normal
    linear = scale_c * normal + bias_c
    sig = sigmoid(linear)
    slope_ref[...] = sig * (1.0 + linear * (1.0 - sig)) * valid
    act = (linear * sig * valid).astype(BF16)

    place = here()
    lifted = []
    for n, (a, b) in enumerate(STEP_LIST):
        src, inside = neighbour(place, grid, (-a, -b))
        block = buf_ref[src, 0:width, :].astype(F32) + mean_ref[pl.ds(src, 1), :]
        lifted.append(jnp.where(inside, block, 0.0))
    lane = iota((LANES, LANES), 1)
    halo = jnp.where(lane < channels, jnp.concatenate(lifted, axis=0), 0.0)
    flag = flag_ref[...]
    halo_normal = (halo - mean) * rstd
    halo_linear = scale * halo_normal + bias
    halo_sig = sigmoid(halo_linear)
    halo_slope = halo_sig * (1.0 + halo_linear * (1.0 - halo_sig)) * flag
    halo_slope_ref[...] = halo_slope
    halo_cross_ref[...] = halo_slope * halo_normal
    halo_act = (halo_linear * halo_sig * flag).T[:channels].astype(BF16)

    table = jnp.concatenate([act, halo_act], axis=1)
    hidden = gather_convolve(table, hot_ref, weight_ref, taken_ref)
    hidden_two_ref[...] = hidden
    sums_two, _, spread_two = centre(hidden, counts_ref)
    stat = jnp.concatenate([sums_two, spread_two], axis=0)
    stat = jnp.where(iota((2, LANES), 1) < 96, stat, counts_ref[0].astype(F32))
    out_buf_ref[...] = jnp.broadcast_to(stat[None], out_buf_ref.shape)


def third_kernel(
    counts_ref, buf_ref, hidden_ref, start_ref, cotangent_ref, scale_ref, bias_ref,
    out_buf_ref, output_ref, norm_ref, grad_ref, const_ref,
):
    channels = hidden_ref.shape[0]
    sums = buf_ref[:, 0, :]
    spreads = buf_ref[:, 1, :]
    counts = sums[:, 96:97]
    total = jnp.sum(counts, axis=0, keepdims=True)
    mean = jnp.sum(sums, axis=0, keepdims=True) / total
    apart = sums / counts - mean
    var = jnp.sum(spreads + counts * apart * apart, axis=0, keepdims=True) / total
    rstd = lax.rsqrt(var + EPS)
    scale = pad_to(scale_ref[...], 1, LANES)
    bias = pad_to(bias_ref[...], 1, LANES)
    total_row = jnp.broadcast_to(total, (1, LANES))
    mean_c, rstd_c, scale_c, bias_c = rows_to_cols([mean, rstd, scale, bias], channels)
    sub = iota((8, LANES), 0)
    const_ref[...] = jnp.where(sub == 0, scale * rstd, jnp.where(sub == 1, total_row, 0.0))
    valid = valid_lanes(counts_ref)
    normal = (hidden_ref[...] - mean_c) * rstd_c
    norm_ref[...] = normal
    summed = scale_c * normal + bias_c + start_ref[...].astype(F32)
    sig = sigmoid(summed)
    output_ref[...] = (summed * sig * valid).astype(BF16)
    grad = cotangent_ref[...].astype(F32) * valid * (sig * (1.0 + summed * (1.0 - sig)))
    grad_ref[...] = grad
    rows = jnp.concatenate([lane_sums(grad * normal * valid), lane_sums(grad)], axis=0)
    out_buf_ref[...] = jnp.broadcast_to(rows[None], out_buf_ref.shape)


def scatter(grad, weight_ref, hot_ref):
    channels = grad.shape[0]
    terms = nn(weight_ref[...], grad).astype(BF16)
    offsets = hot_ref.shape[1] // LANES
    wide = jnp.concatenate([terms[k * channels : (k + 1) * channels] for k in range(offsets)], axis=1)
    table = pad_to(nt(hot_ref[...], wide), hot_ref.shape[0], LANES)
    return table[:LANES], table[LANES : 2 * LANES]


def row_gradient(grad, normal, const, dgain, dbias, valid):
    channels = grad.shape[0]
    factor, part_bias, part_gain = rows_to_cols(
        [const[0:1], dbias / const[1:2], dgain / const[1:2]], channels
    )
    return (factor * (grad - (part_bias + normal * part_gain)) * valid).astype(BF16)


def fourth_kernel(
    grid, counts_ref, buf_ref, norm_ref, grad_ref, const_ref, weight_ref, hot_ref,
    norm_one_ref, slope_ref, halo_slope_ref, halo_cross_ref,
    out_buf_ref, grad_two_ref, table_ref, sums_ref,
):
    channels = norm_ref.shape[0]
    width = out_buf_ref.shape[1]
    valid = valid_lanes(counts_ref)
    both = jnp.sum(buf_ref[...], axis=0)
    sums_ref[...] = both
    grad = row_gradient(grad_ref[...], norm_ref[...], const_ref[...], both[0:1], both[1:2], valid)
    grad_two_ref[...] = grad
    local_slope, local_cross = turn(slope_ref[...]), turn(slope_ref[...] * norm_one_ref[...])
    local, halo = scatter(grad, weight_ref, hot_ref)
    dgain = jnp.sum(local * local_cross + halo * halo_cross_ref[...], axis=0, keepdims=True)
    dbias = jnp.sum(local * local_slope + halo * halo_slope_ref[...], axis=0, keepdims=True)
    table_ref[...] = local.T[: norm_ref.shape[0]]
    base = pack_rows(split3(dgain)[:2] + split3(dbias)[:2], 0.0)
    out_buf_ref[...] = jnp.broadcast_to(base.astype(BF16)[None], out_buf_ref.shape)
    put_blocks(out_buf_ref, halo, grid, -1, width, base)


def packed_weight_grad(taken_ref, grad, put):
    channels = grad.shape[0]
    zero = jnp.zeros((channels, LANES), BF16)

    def taken(k):
        return taken_ref[k * channels : (k + 1) * channels, :]

    for part in range(3):
        upper = jnp.concatenate([grad, zero], axis=1)
        lower = jnp.concatenate([zero[:32], grad[32 * part : 32 * part + 32]], axis=1)
        right = jnp.concatenate([upper, lower], axis=0)
        left = jnp.concatenate(
            [
                jnp.concatenate([taken(3 * e + part) for e in range(6)], axis=0),
                jnp.concatenate([taken(21 + e) for e in range(6)], axis=0),
            ],
            axis=1,
        )
        result = nt(left, right)
        for e in range(6):
            put(3 * e + part, result[e * channels : (e + 1) * channels])
    last = nt(taken_ref[18 * channels : 21 * channels, :], pad_to(grad, LANES, LANES))
    for e in range(3):
        put(18 + e, last[e * channels : (e + 1) * channels])


def store_packed(taken_ref, grad, ref):
    channels = grad.shape[0]
    used = 21 * channels

    def put(block, value):
        ref[block * channels : (block + 1) * channels, :] = value.astype(ref.dtype)

    packed_weight_grad(taken_ref, grad, put)
    if ref.shape[0] > used:
        ref[used:, :] = jnp.zeros((ref.shape[0] - used, LANES), ref.dtype)


def fifth_kernel(
    grid, counts_ref, buf_ref, table_ref, place_ref, norm_ref, slope_ref, const_ref, sums_two_ref,
    taken_zero_ref, taken_act_ref, grad_two_ref,
    grad_one_ref, give_ref, sums_ref,
):
    width = buf_ref.shape[1]
    channels = norm_ref.shape[0]
    valid = valid_lanes(counts_ref)
    dgain, dbias = unpack_rows(
        jnp.sum(buf_ref[...].astype(F32), axis=0, keepdims=True), ((0, 2), (2, 4))
    )
    two = sums_two_ref[...]
    sums_ref[...] = jnp.concatenate([dgain, dbias, two], axis=0)[:, :channels]
    arrived = take_blocks(buf_ref, grid, 1, width).astype(BF16)
    back = table_ref[...] + tn(arrived, place_ref[...])[:channels]
    grad = row_gradient(back * slope_ref[...], norm_ref[...], const_ref[...], dgain, dbias, valid)
    grad_one_ref[...] = grad
    core = lax.axis_index("gy") % 2

    @pl.when(core == 0)
    def _():
        store_packed(taken_act_ref, grad_two_ref[...], give_ref)

    @pl.when(core != 0)
    def _():
        store_packed(taken_zero_ref, grad, give_ref)


def back_kernel(
    grad_ref, weight_ref, hot_ref, taken_zero_ref, taken_act_ref, grad_two_ref, table_ref, halo_ref, keep_ref
):
    core = lax.axis_index("gy") % 2

    @pl.when(core == 0)
    def _():
        store_packed(taken_zero_ref, grad_ref[...], keep_ref)

    @pl.when(core != 0)
    def _():
        store_packed(taken_act_ref, grad_two_ref[...], keep_ref)

    local, halo = scatter(grad_ref[...], weight_ref, hot_ref)
    table_ref[...] = local.T[: grad_ref.shape[0]]
    halo_ref[...] = halo.astype(BF16)


def sixth_kernel(grid, width, halo_ref, keep_ref, got_ref, out_buf_ref):
    devices, rows = out_buf_ref.shape[0], out_buf_ref.shape[1] - width
    put_blocks(out_buf_ref, halo_ref[...], grid, -1, width)
    total = (keep_ref[...] + got_ref[...].astype(F32)).astype(BF16)
    out_buf_ref[:, width:, :] = total.reshape(devices, rows, LANES)


def seventh_kernel(grid, width, buf_ref, out_buf_ref, halo_ref):
    halo_ref[...] = take_blocks(buf_ref, grid, 1, width).astype(BF16)
    devices, rows = buf_ref.shape[0], buf_ref.shape[1] - width
    pieces = []
    for core in range(2):
        total = jnp.zeros((rows, LANES), F32)
        for d in range(core, devices, 2):
            total = total + buf_ref[d, width:, :].astype(F32)
        pieces.append(total.astype(BF16))
    for d in range(devices):
        out_buf_ref[d] = pieces[d % 2]


def unpack(src_ref, out_hbm, block_ref, sems):
    channels = block_ref.shape[1]
    lane = iota((channels, LANES), 1)
    copies = []

    def send(first, count):
        part = pl.ds(first, count)
        copies.append(pltpu.make_async_copy(block_ref.at[part], out_hbm.at[part], sems.at[len(copies)]))
        copies[-1].start()

    for e in range(7):
        extra = jnp.zeros((channels, LANES), F32)
        for part in range(3):
            block = 3 * e + part
            value = src_ref[block * channels : (block + 1) * channels, :].astype(F32)
            block_ref[block] = value[:, :channels]
            if e < 6:
                moved = pltpu.roll(value, 32 * (part + 1), 1)
                extra = jnp.where(lane // 32 == part, moved, extra)
        send(3 * e, 3)
        if e < 6:
            block_ref[21 + e] = extra[:, :channels]
            send(21 + e, 1)
    for copy in copies:
        copy.wait()


def own_kernel(
    counts_ref, own_ref, small_in, sums_in, halo_ref, table_ref, place_ref, grad_ref,
    one_hbm, two_hbm, small_hbm, sums_hbm, more_hbm, more_ref, block_ref, sems, small_sems,
):
    core = lax.axis_index("gy") % 2
    channels = table_ref.shape[0]
    back = table_ref[...] + tn(halo_ref[...], place_ref[...])[:channels]
    more_ref[...] = ((back + grad_ref[...]) * valid_lanes(counts_ref)).astype(BF16)
    pairs = ((small_in, small_hbm), (sums_in, sums_hbm), (more_ref, more_hbm))
    copies = [pltpu.make_async_copy(src, dst, small_sems.at[at]) for at, (src, dst) in enumerate(pairs)]
    for copy in copies:
        copy.start()

    @pl.when(core == 0)
    def _():
        unpack(own_ref, one_hbm, block_ref, sems)

    @pl.when(core != 0)
    def _():
        unpack(own_ref, two_hbm, block_ref, sems)

    for copy in copies:
        copy.wait()


def other_kernel(other_ref, one_in, two_in, one_hbm, two_hbm, block_ref, sems):
    core = lax.axis_index("gy") % 2

    @pl.when(core == 0)
    def _():
        unpack(other_ref, two_hbm, block_ref, sems)

    @pl.when(core != 0)
    def _():
        unpack(other_ref, one_hbm, block_ref, sems)


def call(kernel, outs, *args, smem=0, scratch=(), hbm=(), hbm_outs=(), aliases=None, carry=()):
    n_in, n_out = len(args), len(outs)
    aliases = dict(aliases or {})
    aliases.update({n_in + at: n_out + at for at in range(len(carry))})

    def space(at):
        if at >= n_in:
            return pl.ANY
        if at in hbm:
            return pltpu.HBM
        return pltpu.SMEM if at < smem else pltpu.VMEM

    def out_space(at):
        if at >= n_out:
            return pl.ANY
        return pltpu.HBM if at in hbm_outs else pltpu.VMEM

    def body(*refs):
        first_out = n_in + len(carry)
        kernel(*refs[:n_in], *refs[first_out : first_out + n_out], *refs[first_out + n_out + len(carry) :])

    args = [pltpu.with_memory_space_constraint(x, pltpu.HBM) if at in hbm else x for at, x in enumerate(args)]
    outs = list(outs) + [(x.shape, x.dtype) for x in carry]
    return pl.pallas_call(
        body,
        out_shape=tuple(jax.ShapeDtypeStruct(shape, dtype) for shape, dtype in outs),
        in_specs=[pl.BlockSpec(memory_space=space(at)) for at in range(n_in + len(carry))],
        out_specs=tuple(pl.BlockSpec(memory_space=out_space(at)) for at in range(len(outs))),
        scratch_shapes=list(scratch),
        input_output_aliases=aliases,
        compiler_params=pltpu.CompilerParams(vmem_limit_bytes=40 * 1024 * 1024),
    )(*args, *carry)


def to_all(x):
    return lax.all_to_all(x, AXES, 0, 0)


def swap_core(x):
    size = lax.axis_size("gy")
    return lax.ppermute(x, "gy", [(i, i ^ 1) for i in range(size)])


def on_device(
    features, kernel_map, send_rows, counts, weight_one, weight_two,
    first_norm_scale, first_norm_bias, second_norm_scale, second_norm_bias, cotangent,
):
    channels, rows = features.shape
    offsets = kernel_map.shape[0]
    width = send_rows.shape[1]
    grid = (lax.axis_size("gx"), lax.axis_size("gy"))
    devices = grid[0] * grid[1]
    flat = offsets * channels
    table = rows + 8 * width
    piece = -(-21 * channels // (devices * 16)) * 16
    packed = piece * devices
    full = (channels, rows)
    square = (LANES, LANES)
    one_flat = weight_one.reshape(flat, channels)
    two_flat = weight_two.reshape(flat, channels)
    scale_one, bias_one, scale_two, bias_two = [
        v.reshape(1, channels)
        for v in (first_norm_scale, first_norm_bias, second_norm_scale, second_norm_bias)
    ]

    taken = ((flat, LANES), BF16)
    buf, start, place, hot, one_near = call(
        functools.partial(open_kernel, grid),
        [
            ((devices, width, LANES), BF16), (full, BF16), (square, BF16),
            ((table, offsets * LANES), BF16), (one_flat.shape, BF16),
        ],
        counts, features, send_rows, kernel_map, one_flat, smem=1, hbm=(1, 2, 3, 4),
        scratch=[
            pltpu.VMEM(full, BF16), pltpu.VMEM(send_rows.shape, jnp.int32),
            pltpu.VMEM(kernel_map.shape, jnp.int32), pltpu.SemaphoreType.DMA((4,)),
        ],
    )
    buf = to_all(buf)
    buf, hidden_one, taken_zero, flag = call(
        functools.partial(first_kernel, grid),
        [((devices, width, LANES), BF16), (full, F32), taken, (square, F32)],
        counts, buf, start, hot, one_near, place, smem=1,
    )
    buf = to_all(buf)
    buf, hidden_two, taken_act, norm_one, slope_one, halo_slope, halo_cross, const_one, taken_zero = call(
        functools.partial(second_kernel, grid),
        [
            ((devices, 2, LANES), F32), (full, F32), taken, (full, F32), (full, F32),
            (square, F32), (square, F32), ((8, LANES), F32),
        ],
        counts, buf, hidden_one, flag, scale_one, bias_one, hot, two_flat,
        smem=1, scratch=[pltpu.VMEM((devices, LANES), F32)], carry=[taken_zero],
    )
    buf = to_all(buf)
    buf, output, norm_two, grad_sum, const_two, taken_zero, taken_act = call(
        third_kernel,
        [((devices, 2, LANES), F32), (full, BF16), (full, F32), (full, F32), ((8, LANES), F32)],
        counts, buf, hidden_two, start, cotangent, scale_two, bias_two, smem=1, carry=[taken_zero, taken_act],
    )
    buf = to_all(buf)
    buf, grad_two, table_two, sums_two, taken_zero, taken_act = call(
        functools.partial(fourth_kernel, grid),
        [((devices, width, LANES), BF16), (full, BF16), (full, F32), ((2, LANES), F32)],
        counts, buf, norm_two, grad_sum, const_two, two_flat, hot, norm_one, slope_one, halo_slope, halo_cross,
        smem=1, carry=[taken_zero, taken_act],
    )
    buf = to_all(buf)
    grad_one, give, grad_norms = call(
        functools.partial(fifth_kernel, grid),
        [(full, BF16), ((packed, LANES), BF16), ((4, channels), F32)],
        counts, buf, table_two, place, norm_one, slope_one, const_one, sums_two,
        taken_zero, taken_act, grad_two, smem=1,
    )
    got = swap_core(give)
    table_one, halo_one, keep = call(
        back_kernel,
        [(full, F32), (square, BF16), ((packed, LANES), F32)],
        grad_one, one_flat, hot, taken_zero, taken_act, grad_two,
    )
    (buf,) = call(
        functools.partial(sixth_kernel, grid, width),
        [((devices, width + piece, LANES), BF16)],
        halo_one, keep, got,
    )
    buf = to_all(buf)
    buf, halo = call(
        functools.partial(seventh_kernel, grid, width),
        [((devices, piece, LANES), BF16), (square, BF16)],
        buf,
    )
    own = to_all(buf).reshape(packed, LANES)
    other = swap_core(own)
    weights = [(weight_one.shape, F32), (weight_two.shape, F32)]
    blocks = [pltpu.VMEM(weight_one.shape, F32), pltpu.SemaphoreType.DMA((13,))]
    grad_weight_one, grad_weight_two, output, grad_norms, grad_features = call(
        own_kernel,
        weights + [(full, BF16), ((4, channels), F32), (full, BF16)],
        counts, own, output, grad_norms, halo, table_one, place, grad_sum, smem=1, hbm_outs=(0, 1, 2, 3, 4),
        scratch=[pltpu.VMEM(full, BF16)] + blocks + [pltpu.SemaphoreType.DMA((3,))],
    )
    grad_weight_one, grad_weight_two = call(
        other_kernel, weights, other, grad_weight_one, grad_weight_two,
        hbm=(1, 2), hbm_outs=(0, 1), scratch=blocks, aliases={1: 0, 2: 1},
    )
    return (output, grad_features, grad_weight_one, grad_weight_two, grad_norms)


def solution(mesh):
    return jax.shard_map(
        on_device,
        mesh=mesh,
        in_specs=(
            P(None, ("gx", "gy")),
            P(None, ("gx", "gy")),
            P(None, ("gx", "gy")),
            P(("gx", "gy")),
            P(),
            P(),
            P(),
            P(),
            P(),
            P(),
            P(None, ("gx", "gy")),
        ),
        out_specs=(P(None, ("gx", "gy")), P(None, ("gx", "gy")), P(), P(), P()),
        check_vma=False,
    )
```

```python
import functools

import jax
import jax.numpy as jnp
from jax import lax
from jax.experimental import pallas as pl
from jax.experimental.pallas import tpu as pltpu
from jax.sharding import PartitionSpec as P

EPS = 1e-05
STEP_LIST = ((1, 0), (-1, 0), (0, 1), (0, -1), (1, 1), (1, -1), (-1, 1), (-1, -1))
AXES = ("gx", "gy")
LANES = 128
F32 = jnp.float32
BF16 = jnp.bfloat16


def nn(a, b):
    return lax.dot_general(a, b, (((1,), (0,)), ((), ())), preferred_element_type=F32)


def nt(a, b):
    return lax.dot_general(a, b, (((1,), (1,)), ((), ())), preferred_element_type=F32)


def tn(a, b):
    return lax.dot_general(a, b, (((0,), (0,)), ((), ())), preferred_element_type=F32)


def iota(shape, dim):
    return lax.broadcasted_iota(jnp.int32, shape, dim)


def sigmoid(v):
    return 1.0 / (1.0 + jnp.exp(-v))


def neighbour(place, grid, step):
    i, j = place[0] + step[0], place[1] + step[1]
    inside = (i >= 0) & (i < grid[0]) & (j >= 0) & (j < grid[1])
    return jnp.where(inside, i * grid[1] + j, place[0] * grid[1] + place[1]), inside


def here():
    return lax.axis_index("gx"), lax.axis_index("gy")


def put_blocks(buf_ref, rows, grid, sign, width, base=None):
    place = here()
    for n, (a, b) in enumerate(STEP_LIST):
        dest, _ = neighbour(place, grid, (sign * a, sign * b))
        block = rows[n * width : (n + 1) * width]
        if base is not None:
            block = jnp.where(iota(block.shape, 1) < 96, block, base)
        buf_ref[dest, 0:width, :] = block.astype(BF16)


def take_blocks(buf_ref, grid, sign, width):
    place = here()
    blocks = []
    for a, b in STEP_LIST:
        src, inside = neighbour(place, grid, (sign * a, sign * b))
        block = buf_ref[src, 0:width, :].astype(F32)
        blocks.append(jnp.where(inside, block, 0.0))
    return jnp.concatenate(blocks, axis=0)


def pad_to(x, rows, lanes):
    if x.shape[1] < lanes:
        x = jnp.concatenate([x, jnp.zeros((x.shape[0], lanes - x.shape[1]), x.dtype)], axis=1)
    if x.shape[0] < rows:
        x = jnp.concatenate([x, jnp.zeros((rows - x.shape[0], lanes), x.dtype)], axis=0)
    return x


def halve(x, least):
    while x.shape[0] > least and x.shape[0] % 2 == 0:
        rows = x.shape[0] // 2
        x = x[:rows] + x[rows:]
    return x


def row_sum(x):
    return jnp.sum(halve(x, 8), axis=0, keepdims=True)


def turn(x):
    return pad_to(x, LANES, LANES).T


def lane_sums(x):
    return row_sum(turn(x))


def rows_to_cols(rows, channels):
    return [jnp.broadcast_to(row, (LANES, LANES)).T[:channels] for row in rows]


def centre(hidden, counts_ref):
    count = counts_ref[0].astype(F32)
    mask = (iota((LANES, LANES), 0) < counts_ref[0]).astype(F32)
    turned = turn(hidden)
    sums = row_sum(turned * mask)
    centred = (turned - sums / count) * mask
    return sums, centred, row_sum(centred * centred)


def split3(x):
    high = x.astype(BF16).astype(F32)
    mid = (x - high).astype(BF16).astype(F32)
    low = (x - high - mid).astype(BF16).astype(F32)
    return [high, mid, low]


def pack_rows(pieces, last):
    sub = iota((16, LANES), 0)
    lane = iota((16, LANES), 1)
    total = jnp.zeros((16, LANES), F32)
    for q, piece in enumerate(pieces):
        total = jnp.where(sub // 3 == q, piece, total)
    part = sub % 3
    moved = jnp.where(
        part == 0,
        pltpu.roll(total, 96, 1),
        jnp.where(part == 1, pltpu.roll(total, 64, 1), pltpu.roll(total, 32, 1)),
    )
    moved = jnp.where(sub == 15, last, moved)
    return jnp.where(lane >= 96, moved, 0.0)


def unpack_rows(tiles, groups):
    devices = tiles.shape[0]
    flat = tiles.reshape(devices * 16, LANES)
    sub = iota(tiles.shape, 1)
    lane = iota(tiles.shape, 2)
    part = sub % 3
    moved = [pltpu.roll(flat, 32 * (p + 1), 1).reshape(tiles.shape) for p in range(3)]
    value = jnp.where(part == 0, moved[0], jnp.where(part == 1, moved[1], moved[2]))
    value = jnp.where((lane // 32 == part) & (sub < 15), value, 0.0)
    results = []
    for low, high in groups:
        mask = (sub >= 3 * low) & (sub < 3 * high)
        results.append(jnp.sum(jnp.where(mask, value, 0.0), axis=1))
    return results


def valid_lanes(counts_ref, rows=1):
    return (iota((rows, LANES), 1) < counts_ref[0]).astype(F32)


def open_kernel(
    grid, counts_ref, features_hbm, send_hbm, map_hbm, one_hbm,
    buf_ref, start_ref, place_ref, hot_ref, one_ref, features_ref, send_ref, map_ref, sems,
):
    pairs = ((features_hbm, features_ref), (send_hbm, send_ref), (map_hbm, map_ref), (one_hbm, one_ref))
    copies = [pltpu.make_async_copy(src, dst, sems.at[at]) for at, (src, dst) in enumerate(pairs)]
    for copy in copies:
        copy.start()
    for copy in copies[:3]:
        copy.wait()
    width = send_ref.shape[1]
    send = pad_to(send_ref[...].astype(F32), LANES, LANES).T
    lane = iota((width, LANES), 1).astype(F32)
    place = jnp.concatenate(
        [jnp.where(lane == send[:width, n : n + 1], 1.0, 0.0) for n in range(send_ref.shape[0])], axis=0
    ).astype(BF16)
    place_ref[...] = place
    valid = valid_lanes(counts_ref)
    start = features_ref[...].astype(F32) * valid
    start_ref[...] = start.astype(BF16)
    extra = jnp.where(iota((LANES - 96, LANES), 0) == 0, valid, 0.0)
    rows = nt(place, jnp.concatenate([start, extra], axis=0).astype(BF16))
    put_blocks(buf_ref, rows, grid, 1, width)
    sub = iota((hot_ref.shape[0], LANES), 0).astype(jnp.int16)
    columns = map_ref[...].astype(jnp.int16)
    one, zero = jnp.ones(sub.shape, BF16), jnp.zeros(sub.shape, BF16)
    for k in range(map_ref.shape[0]):
        hot_ref[:, k * LANES : (k + 1) * LANES] = jnp.where(sub == columns[k : k + 1, :], one, zero)
    copies[3].wait()


def gather(tables, hot_ref, taken_refs):
    channels = tables[0].shape[0]
    taken = nn(jnp.concatenate(tables, axis=0), hot_ref[...]).astype(BF16)
    for at, ref in enumerate(taken_refs):
        for k in range(hot_ref.shape[1] // LANES):
            ref[k * channels : (k + 1) * channels, :] = taken[
                at * channels : (at + 1) * channels, k * LANES : (k + 1) * LANES
            ]


def gather_convolve(table, hot_ref, weight_ref, taken_ref):
    gather([table], hot_ref, [taken_ref])
    return tn(weight_ref[...], taken_ref[...])


def first_kernel(
    grid, counts_ref, buf_ref, start_ref, hot_ref, weight_ref, place_ref,
    out_buf_ref, hidden_ref, taken_ref, flag_ref,
):
    width = buf_ref.shape[1]
    channels = start_ref.shape[0]
    halo_rows = take_blocks(buf_ref, grid, -1, width)
    flag_ref[...] = jnp.broadcast_to(halo_rows[:, 96:97], (LANES, LANES))
    halo = halo_rows.T[:channels].astype(BF16)
    table = jnp.concatenate([start_ref[...], halo], axis=1)
    hidden = gather_convolve(table, hot_ref, weight_ref, taken_ref)
    hidden_ref[...] = hidden
    sums, centred, spread = centre(hidden, counts_ref)
    base = pack_rows(split3(sums) + split3(spread)[:2], counts_ref[0].astype(F32))
    out_buf_ref[...] = jnp.broadcast_to(base.astype(BF16)[None], out_buf_ref.shape)
    rows = nn(place_ref[...], centred.astype(BF16))
    put_blocks(out_buf_ref, rows, grid, 1, width, base)


def second_kernel(
    grid, counts_ref, buf_ref, hidden_ref, flag_ref, scale_ref, bias_ref, hot_ref, weight_ref,
    out_buf_ref, hidden_two_ref, taken_ref, norm_ref, slope_ref, halo_slope_ref, halo_cross_ref,
    const_ref, mean_ref,
):
    width = buf_ref.shape[1]
    channels = hidden_ref.shape[0]
    tiles = buf_ref[...].astype(F32)
    sums, spreads = unpack_rows(tiles, ((0, 3), (3, 5)))
    counts = tiles[:, 15, 96:97]
    total = jnp.sum(counts, axis=0, keepdims=True)
    means = sums / counts
    mean_ref[...] = means
    mean = jnp.sum(sums, axis=0, keepdims=True) / total
    apart = means - mean
    var = jnp.sum(spreads + counts * apart * apart, axis=0, keepdims=True) / total
    rstd = lax.rsqrt(var + EPS)
    scale = pad_to(scale_ref[...], 1, LANES)
    bias = pad_to(bias_ref[...], 1, LANES)
    total_row = jnp.broadcast_to(total, (1, LANES))
    mean_c, rstd_c, scale_c, bias_c = rows_to_cols([mean, rstd, scale, bias], channels)
    sub = iota((8, LANES), 0)
    const_ref[...] = jnp.where(sub == 0, scale * rstd, jnp.where(sub == 1, total_row, 0.0))

    valid = valid_lanes(counts_ref)
    normal = (hidden_ref[...] - mean_c) * rstd_c
    norm_ref[...] = normal
    linear = scale_c * normal + bias_c
    sig = sigmoid(linear)
    slope_ref[...] = sig * (1.0 + linear * (1.0 - sig)) * valid
    act = (linear * sig * valid).astype(BF16)

    place = here()
    lifted = []
    for n, (a, b) in enumerate(STEP_LIST):
        src, inside = neighbour(place, grid, (-a, -b))
        block = buf_ref[src, 0:width, :].astype(F32) + mean_ref[pl.ds(src, 1), :]
        lifted.append(jnp.where(inside, block, 0.0))
    lane = iota((LANES, LANES), 1)
    halo = jnp.where(lane < channels, jnp.concatenate(lifted, axis=0), 0.0)
    flag = flag_ref[...]
    halo_normal = (halo - mean) * rstd
    halo_linear = scale * halo_normal + bias
    halo_sig = sigmoid(halo_linear)
    halo_slope = halo_sig * (1.0 + halo_linear * (1.0 - halo_sig)) * flag
    halo_slope_ref[...] = halo_slope
    halo_cross_ref[...] = halo_slope * halo_normal
    halo_act = (halo_linear * halo_sig * flag).T[:channels].astype(BF16)

    table = jnp.concatenate([act, halo_act], axis=1)
    hidden = gather_convolve(table, hot_ref, weight_ref, taken_ref)
    hidden_two_ref[...] = hidden
    sums_two, _, spread_two = centre(hidden, counts_ref)
    stat = jnp.concatenate([sums_two, spread_two], axis=0)
    stat = jnp.where(iota((2, LANES), 1) < 96, stat, counts_ref[0].astype(F32))
    out_buf_ref[...] = jnp.broadcast_to(stat[None], out_buf_ref.shape)


def third_kernel(
    counts_ref, buf_ref, hidden_ref, start_ref, cotangent_ref, scale_ref, bias_ref,
    out_buf_ref, output_ref, norm_ref, grad_ref, const_ref,
):
    channels = hidden_ref.shape[0]
    sums = buf_ref[:, 0, :]
    spreads = buf_ref[:, 1, :]
    counts = sums[:, 96:97]
    total = jnp.sum(counts, axis=0, keepdims=True)
    mean = jnp.sum(sums, axis=0, keepdims=True) / total
    apart = sums / counts - mean
    var = jnp.sum(spreads + counts * apart * apart, axis=0, keepdims=True) / total
    rstd = lax.rsqrt(var + EPS)
    scale = pad_to(scale_ref[...], 1, LANES)
    bias = pad_to(bias_ref[...], 1, LANES)
    total_row = jnp.broadcast_to(total, (1, LANES))
    mean_c, rstd_c, scale_c, bias_c = rows_to_cols([mean, rstd, scale, bias], channels)
    sub = iota((8, LANES), 0)
    const_ref[...] = jnp.where(sub == 0, scale * rstd, jnp.where(sub == 1, total_row, 0.0))
    valid = valid_lanes(counts_ref)
    normal = (hidden_ref[...] - mean_c) * rstd_c
    norm_ref[...] = normal
    summed = scale_c * normal + bias_c + start_ref[...].astype(F32)
    sig = sigmoid(summed)
    output_ref[...] = (summed * sig * valid).astype(BF16)
    grad = cotangent_ref[...].astype(F32) * valid * (sig * (1.0 + summed * (1.0 - sig)))
    grad_ref[...] = grad
    rows = jnp.concatenate([lane_sums(grad * normal * valid), lane_sums(grad)], axis=0)
    out_buf_ref[...] = jnp.broadcast_to(rows[None], out_buf_ref.shape)


def scatter(grad, weight_ref, hot_ref):
    channels = grad.shape[0]
    terms = nn(weight_ref[...], grad).astype(BF16)
    offsets = hot_ref.shape[1] // LANES
    wide = jnp.concatenate([terms[k * channels : (k + 1) * channels] for k in range(offsets)], axis=1)
    halo = pad_to(nt(hot_ref[LANES : 2 * LANES, :], wide), LANES, LANES)
    return pad_to(nt(hot_ref[:LANES, :], wide), LANES, LANES), halo


def row_gradient(grad, normal, const, dgain, dbias, valid):
    channels = grad.shape[0]
    factor, part_bias, part_gain = rows_to_cols(
        [const[0:1], dbias / const[1:2], dgain / const[1:2]], channels
    )
    return (factor * (grad - (part_bias + normal * part_gain)) * valid).astype(BF16)


def fourth_kernel(
    grid, counts_ref, buf_ref, norm_ref, grad_ref, const_ref, weight_ref, hot_ref,
    norm_one_ref, slope_ref, halo_slope_ref, halo_cross_ref,
    out_buf_ref, grad_two_ref, table_ref, sums_ref,
):
    channels = norm_ref.shape[0]
    width = out_buf_ref.shape[1]
    valid = valid_lanes(counts_ref)
    both = halve(buf_ref[...], 1)[0]
    sums_ref[...] = both
    grad = row_gradient(grad_ref[...], norm_ref[...], const_ref[...], both[0:1], both[1:2], valid)
    grad_two_ref[...] = grad
    local_slope, local_cross = turn(slope_ref[...]), turn(slope_ref[...] * norm_one_ref[...])
    local, halo = scatter(grad, weight_ref, hot_ref)
    dgain = row_sum(local * local_cross + halo * halo_cross_ref[...])
    dbias = row_sum(local * local_slope + halo * halo_slope_ref[...])
    table_ref[...] = local.T[: norm_ref.shape[0]]
    base = pack_rows(split3(dgain)[:2] + split3(dbias)[:2], 0.0)
    out_buf_ref[...] = jnp.broadcast_to(base.astype(BF16)[None], out_buf_ref.shape)
    put_blocks(out_buf_ref, halo, grid, -1, width, base)


def packed_weight_grad(taken_ref, grad, put):
    channels = grad.shape[0]
    zero = jnp.zeros((channels, LANES), BF16)

    def taken(k):
        return taken_ref[k * channels : (k + 1) * channels, :]

    for part in range(3):
        upper = jnp.concatenate([grad, zero], axis=1)
        lower = jnp.concatenate([zero[:32], grad[32 * part : 32 * part + 32]], axis=1)
        right = jnp.concatenate([upper, lower], axis=0)
        left = jnp.concatenate(
            [
                jnp.concatenate([taken(3 * e + part) for e in range(6)], axis=0),
                jnp.concatenate([taken(21 + e) for e in range(6)], axis=0),
            ],
            axis=1,
        )
        result = nt(left, right)
        for e in range(6):
            put(3 * e + part, result[e * channels : (e + 1) * channels])
    last = nt(taken_ref[18 * channels : 21 * channels, :], pad_to(grad, LANES, LANES))
    for e in range(3):
        put(18 + e, last[e * channels : (e + 1) * channels])


def store_packed(taken_ref, grad, ref):
    channels = grad.shape[0]
    used = 21 * channels

    def put(block, value):
        ref[block * channels : (block + 1) * channels, :] = value.astype(ref.dtype)

    packed_weight_grad(taken_ref, grad, put)
    if ref.shape[0] > used:
        ref[used:, :] = jnp.zeros((ref.shape[0] - used, LANES), ref.dtype)


def fifth_kernel(
    grid, counts_ref, buf_ref, table_ref, place_ref, norm_ref, slope_ref, const_ref, sums_two_ref,
    taken_zero_ref, taken_act_ref, grad_two_ref,
    grad_one_ref, give_ref, sums_ref,
):
    width = buf_ref.shape[1]
    channels = norm_ref.shape[0]
    valid = valid_lanes(counts_ref)
    dgain, dbias = unpack_rows(
        halve(buf_ref[...].astype(F32), 1), ((0, 2), (2, 4))
    )
    two = sums_two_ref[...]
    sums_ref[...] = jnp.concatenate([dgain, dbias, two], axis=0)[:, :channels]
    arrived = take_blocks(buf_ref, grid, 1, width).astype(BF16)
    back = table_ref[...] + tn(arrived, place_ref[...])[:channels]
    grad = row_gradient(back * slope_ref[...], norm_ref[...], const_ref[...], dgain, dbias, valid)
    grad_one_ref[...] = grad
    core = lax.axis_index("gy") % 2

    @pl.when(core == 0)
    def _():
        store_packed(taken_act_ref, grad_two_ref[...], give_ref)

    @pl.when(core != 0)
    def _():
        store_packed(taken_zero_ref, grad, give_ref)


def back_kernel(
    grad_ref, weight_ref, hot_ref, taken_zero_ref, taken_act_ref, grad_two_ref, table_ref, halo_ref, keep_ref
):
    core = lax.axis_index("gy") % 2

    @pl.when(core == 0)
    def _():
        store_packed(taken_zero_ref, grad_ref[...], keep_ref)

    @pl.when(core != 0)
    def _():
        store_packed(taken_act_ref, grad_two_ref[...], keep_ref)

    local, halo = scatter(grad_ref[...], weight_ref, hot_ref)
    table_ref[...] = local.T[: grad_ref.shape[0]]
    halo_ref[...] = halo.astype(BF16)


def sixth_kernel(grid, width, halo_ref, keep_ref, got_ref, out_buf_ref):
    devices, rows = out_buf_ref.shape[0], out_buf_ref.shape[1] - width
    put_blocks(out_buf_ref, halo_ref[...], grid, -1, width)
    total = (keep_ref[...] + got_ref[...].astype(F32)).astype(BF16)
    out_buf_ref[:, width:, :] = total.reshape(devices, rows, LANES)


def seventh_kernel(grid, width, buf_ref, out_buf_ref, halo_ref):
    halo_ref[...] = take_blocks(buf_ref, grid, 1, width).astype(BF16)
    devices, rows = buf_ref.shape[0], buf_ref.shape[1] - width
    pieces = []
    for core in range(2):
        total = jnp.zeros((rows, LANES), F32)
        for d in range(core, devices, 2):
            total = total + buf_ref[d, width:, :].astype(F32)
        pieces.append(total.astype(BF16))
    for d in range(devices):
        out_buf_ref[d] = pieces[d % 2]


def unpack(src_ref, out_hbm, block_ref, sems):
    channels = block_ref.shape[1]
    lane = iota((channels, LANES), 1)
    copies = []

    def send(first, count):
        part = pl.ds(first, count)
        copies.append(pltpu.make_async_copy(block_ref.at[part], out_hbm.at[part], sems.at[len(copies)]))
        copies[-1].start()

    for e in range(7):
        extra = jnp.zeros((channels, LANES), F32)
        for part in range(3):
            block = 3 * e + part
            value = src_ref[block * channels : (block + 1) * channels, :].astype(F32)
            block_ref[block] = value[:, :channels]
            if e < 6:
                moved = pltpu.roll(value, 32 * (part + 1), 1)
                extra = jnp.where(lane // 32 == part, moved, extra)
        send(3 * e, 3)
        if e < 6:
            block_ref[21 + e] = extra[:, :channels]
            send(21 + e, 1)
    for copy in copies:
        copy.wait()


def own_kernel(
    counts_ref, own_ref, small_in, sums_in, halo_ref, table_ref, place_ref, grad_ref,
    one_hbm, two_hbm, small_hbm, sums_hbm, more_hbm, more_ref, block_ref, sems, small_sems,
):
    core = lax.axis_index("gy") % 2
    channels = table_ref.shape[0]
    back = table_ref[...] + tn(halo_ref[...], place_ref[...])[:channels]
    more_ref[...] = ((back + grad_ref[...]) * valid_lanes(counts_ref)).astype(BF16)
    pairs = ((small_in, small_hbm), (sums_in, sums_hbm), (more_ref, more_hbm))
    copies = [pltpu.make_async_copy(src, dst, small_sems.at[at]) for at, (src, dst) in enumerate(pairs)]
    for copy in copies:
        copy.start()

    @pl.when(core == 0)
    def _():
        unpack(own_ref, one_hbm, block_ref, sems)

    @pl.when(core != 0)
    def _():
        unpack(own_ref, two_hbm, block_ref, sems)

    for copy in copies:
        copy.wait()


def other_kernel(other_ref, one_in, two_in, one_hbm, two_hbm, block_ref, sems):
    core = lax.axis_index("gy") % 2

    @pl.when(core == 0)
    def _():
        unpack(other_ref, two_hbm, block_ref, sems)

    @pl.when(core != 0)
    def _():
        unpack(other_ref, one_hbm, block_ref, sems)


def call(kernel, outs, *args, smem=0, scratch=(), hbm=(), hbm_outs=(), aliases=None, carry=()):
    n_in, n_out = len(args), len(outs)
    aliases = dict(aliases or {})
    aliases.update({n_in + at: n_out + at for at in range(len(carry))})

    def space(at):
        if at >= n_in:
            return pl.ANY
        if at in hbm:
            return pltpu.HBM
        return pltpu.SMEM if at < smem else pltpu.VMEM

    def out_space(at):
        if at >= n_out:
            return pl.ANY
        return pltpu.HBM if at in hbm_outs else pltpu.VMEM

    def body(*refs):
        first_out = n_in + len(carry)
        kernel(*refs[:n_in], *refs[first_out : first_out + n_out], *refs[first_out + n_out + len(carry) :])

    args = [pltpu.with_memory_space_constraint(x, pltpu.HBM) if at in hbm else x for at, x in enumerate(args)]
    outs = list(outs) + [(x.shape, x.dtype) for x in carry]
    return pl.pallas_call(
        body,
        out_shape=tuple(jax.ShapeDtypeStruct(shape, dtype) for shape, dtype in outs),
        in_specs=[pl.BlockSpec(memory_space=space(at)) for at in range(n_in + len(carry))],
        out_specs=tuple(pl.BlockSpec(memory_space=out_space(at)) for at in range(len(outs))),
        scratch_shapes=list(scratch),
        input_output_aliases=aliases,
        compiler_params=pltpu.CompilerParams(vmem_limit_bytes=40 * 1024 * 1024),
    )(*args, *carry)


def to_all(x):
    return lax.all_to_all(x, AXES, 0, 0)


def swap_core(x):
    size = lax.axis_size("gy")
    return lax.ppermute(x, "gy", [(i, i ^ 1) for i in range(size)])


def on_device(
    features, kernel_map, send_rows, counts, weight_one, weight_two,
    first_norm_scale, first_norm_bias, second_norm_scale, second_norm_bias, cotangent,
):
    channels, rows = features.shape
    offsets = kernel_map.shape[0]
    width = send_rows.shape[1]
    grid = (lax.axis_size("gx"), lax.axis_size("gy"))
    devices = grid[0] * grid[1]
    flat = offsets * channels
    table = rows + 8 * width
    piece = -(-21 * channels // (devices * 16)) * 16
    packed = piece * devices
    full = (channels, rows)
    square = (LANES, LANES)
    one_flat = weight_one.reshape(flat, channels)
    two_flat = weight_two.reshape(flat, channels)
    scale_one, bias_one, scale_two, bias_two = [
        v.reshape(1, channels)
        for v in (first_norm_scale, first_norm_bias, second_norm_scale, second_norm_bias)
    ]

    taken = ((flat, LANES), BF16)
    buf, start, place, hot, one_near = call(
        functools.partial(open_kernel, grid),
        [
            ((devices, width, LANES), BF16), (full, BF16), (square, BF16),
            ((table, offsets * LANES), BF16), (one_flat.shape, BF16),
        ],
        counts, features, send_rows, kernel_map, one_flat, smem=1, hbm=(1, 2, 3, 4),
        scratch=[
            pltpu.VMEM(full, BF16), pltpu.VMEM(send_rows.shape, jnp.int32),
            pltpu.VMEM(kernel_map.shape, jnp.int32), pltpu.SemaphoreType.DMA((4,)),
        ],
    )
    buf = to_all(buf)
    buf, hidden_one, taken_zero, flag = call(
        functools.partial(first_kernel, grid),
        [((devices, width, LANES), BF16), (full, F32), taken, (square, F32)],
        counts, buf, start, hot, one_near, place, smem=1,
    )
    buf = to_all(buf)
    buf, hidden_two, taken_act, norm_one, slope_one, halo_slope, halo_cross, const_one, taken_zero = call(
        functools.partial(second_kernel, grid),
        [
            ((devices, 2, LANES), F32), (full, F32), taken, (full, F32), (full, F32),
            (square, F32), (square, F32), ((8, LANES), F32),
        ],
        counts, buf, hidden_one, flag, scale_one, bias_one, hot, two_flat,
        smem=1, scratch=[pltpu.VMEM((devices, LANES), F32)], carry=[taken_zero],
    )
    buf = to_all(buf)
    buf, output, norm_two, grad_sum, const_two, taken_zero, taken_act = call(
        third_kernel,
        [((devices, 2, LANES), F32), (full, BF16), (full, F32), (full, F32), ((8, LANES), F32)],
        counts, buf, hidden_two, start, cotangent, scale_two, bias_two, smem=1, carry=[taken_zero, taken_act],
    )
    buf = to_all(buf)
    buf, grad_two, table_two, sums_two, taken_zero, taken_act = call(
        functools.partial(fourth_kernel, grid),
        [((devices, width, LANES), BF16), (full, BF16), (full, F32), ((2, LANES), F32)],
        counts, buf, norm_two, grad_sum, const_two, two_flat, hot, norm_one, slope_one, halo_slope, halo_cross,
        smem=1, carry=[taken_zero, taken_act],
    )
    buf = to_all(buf)
    grad_one, give, grad_norms = call(
        functools.partial(fifth_kernel, grid),
        [(full, BF16), ((packed, LANES), BF16), ((4, channels), F32)],
        counts, buf, table_two, place, norm_one, slope_one, const_one, sums_two,
        taken_zero, taken_act, grad_two, smem=1,
    )
    got = swap_core(give)
    table_one, halo_one, keep = call(
        back_kernel,
        [(full, F32), (square, BF16), ((packed, LANES), F32)],
        grad_one, one_flat, hot, taken_zero, taken_act, grad_two,
    )
    (buf,) = call(
        functools.partial(sixth_kernel, grid, width),
        [((devices, width + piece, LANES), BF16)],
        halo_one, keep, got,
    )
    buf = to_all(buf)
    buf, halo = call(
        functools.partial(seventh_kernel, grid, width),
        [((devices, piece, LANES), BF16), (square, BF16)],
        buf,
    )
    own = to_all(buf).reshape(packed, LANES)
    other = swap_core(own)
    weights = [(weight_one.shape, F32), (weight_two.shape, F32)]
    blocks = [pltpu.VMEM(weight_one.shape, F32), pltpu.SemaphoreType.DMA((13,))]
    grad_weight_one, grad_weight_two, output, grad_norms, grad_features = call(
        own_kernel,
        weights + [(full, BF16), ((4, channels), F32), (full, BF16)],
        counts, own, output, grad_norms, halo, table_one, place, grad_sum, smem=1, hbm_outs=(0, 1, 2, 3, 4),
        scratch=[pltpu.VMEM(full, BF16)] + blocks + [pltpu.SemaphoreType.DMA((3,))],
    )
    grad_weight_one, grad_weight_two = call(
        other_kernel, weights, other, grad_weight_one, grad_weight_two,
        hbm=(1, 2), hbm_outs=(0, 1), scratch=blocks, aliases={1: 0, 2: 1},
    )
    return (output, grad_features, grad_weight_one, grad_weight_two, grad_norms)


def solution(mesh):
    return jax.shard_map(
        on_device,
        mesh=mesh,
        in_specs=(
            P(None, ("gx", "gy")),
            P(None, ("gx", "gy")),
            P(None, ("gx", "gy")),
            P(("gx", "gy")),
            P(),
            P(),
            P(),
            P(),
            P(),
            P(),
            P(None, ("gx", "gy")),
        ),
        out_specs=(P(None, ("gx", "gy")), P(None, ("gx", "gy")), P(), P(), P()),
        check_vma=False,
    )
```

```python
import functools

import jax
import jax.numpy as jnp
from jax import lax
from jax.experimental import pallas as pl
from jax.experimental.pallas import tpu as pltpu
from jax.sharding import PartitionSpec as P

EPS = 1e-05
STEP_LIST = ((1, 0), (-1, 0), (0, 1), (0, -1), (1, 1), (1, -1), (-1, 1), (-1, -1))
AXES = ("gx", "gy")
LANES = 128
F32 = jnp.float32
BF16 = jnp.bfloat16


def nn(a, b):
    return lax.dot_general(a, b, (((1,), (0,)), ((), ())), preferred_element_type=F32)


def nt(a, b):
    return lax.dot_general(a, b, (((1,), (1,)), ((), ())), preferred_element_type=F32)


def tn(a, b):
    return lax.dot_general(a, b, (((0,), (0,)), ((), ())), preferred_element_type=F32)


def iota(shape, dim):
    return lax.broadcasted_iota(jnp.int32, shape, dim)


def sigmoid(v):
    return 1.0 / (1.0 + jnp.exp(-v))


def neighbour(place, grid, step):
    i, j = place[0] + step[0], place[1] + step[1]
    inside = (i >= 0) & (i < grid[0]) & (j >= 0) & (j < grid[1])
    return jnp.where(inside, i * grid[1] + j, place[0] * grid[1] + place[1]), inside


def here():
    return lax.axis_index("gx"), lax.axis_index("gy")


def put_blocks(buf_ref, rows, grid, sign, width, base=None):
    place = here()
    for n, (a, b) in enumerate(STEP_LIST):
        dest, _ = neighbour(place, grid, (sign * a, sign * b))
        block = rows[n * width : (n + 1) * width]
        if base is not None:
            block = jnp.where(iota(block.shape, 1) < 96, block, base)
        buf_ref[dest, 0:width, :] = block.astype(BF16)


def take_blocks(buf_ref, grid, sign, width):
    place = here()
    blocks = []
    for a, b in STEP_LIST:
        src, inside = neighbour(place, grid, (sign * a, sign * b))
        block = buf_ref[src, 0:width, :].astype(F32)
        blocks.append(jnp.where(inside, block, 0.0))
    return jnp.concatenate(blocks, axis=0)


def pad_to(x, rows, lanes):
    if x.shape[1] < lanes:
        x = jnp.concatenate([x, jnp.zeros((x.shape[0], lanes - x.shape[1]), x.dtype)], axis=1)
    if x.shape[0] < rows:
        x = jnp.concatenate([x, jnp.zeros((rows - x.shape[0], lanes), x.dtype)], axis=0)
    return x


def halve(x, least):
    while x.shape[0] > least and x.shape[0] % 2 == 0:
        rows = x.shape[0] // 2
        x = x[:rows] + x[rows:]
    return x


def row_sum(x):
    return jnp.sum(halve(x, 8), axis=0, keepdims=True)


def turn(x):
    return pad_to(x, LANES, LANES).T


def lane_sums(x):
    return row_sum(turn(x))


def rows_to_cols(rows, channels):
    return [jnp.broadcast_to(row, (LANES, LANES)).T[:channels] for row in rows]


def centre(hidden, counts_ref):
    count = counts_ref[0].astype(F32)
    mask = (iota((LANES, LANES), 0) < counts_ref[0]).astype(F32)
    turned = turn(hidden)
    sums = row_sum(turned * mask)
    centred = (turned - sums / count) * mask
    return sums, centred, row_sum(centred * centred)


def split3(x):
    high = x.astype(BF16).astype(F32)
    mid = (x - high).astype(BF16).astype(F32)
    low = (x - high - mid).astype(BF16).astype(F32)
    return [high, mid, low]


def pack_rows(pieces, last):
    sub = iota((16, LANES), 0)
    lane = iota((16, LANES), 1)
    total = jnp.zeros((16, LANES), F32)
    for q, piece in enumerate(pieces):
        total = jnp.where(sub // 3 == q, piece, total)
    part = sub % 3
    moved = jnp.where(
        part == 0,
        pltpu.roll(total, 96, 1),
        jnp.where(part == 1, pltpu.roll(total, 64, 1), pltpu.roll(total, 32, 1)),
    )
    moved = jnp.where(sub == 15, last, moved)
    return jnp.where(lane >= 96, moved, 0.0)


def unpack_rows(tiles, groups):
    devices = tiles.shape[0]
    flat = tiles.reshape(devices * 16, LANES)
    sub = iota(tiles.shape, 1)
    lane = iota(tiles.shape, 2)
    part = sub % 3
    moved = [pltpu.roll(flat, 32 * (p + 1), 1).reshape(tiles.shape) for p in range(3)]
    value = jnp.where(part == 0, moved[0], jnp.where(part == 1, moved[1], moved[2]))
    value = jnp.where((lane // 32 == part) & (sub < 15), value, 0.0)
    results = []
    for low, high in groups:
        mask = (sub >= 3 * low) & (sub < 3 * high)
        results.append(jnp.sum(jnp.where(mask, value, 0.0), axis=1))
    return results


def valid_lanes(counts_ref, rows=1):
    return (iota((rows, LANES), 1) < counts_ref[0]).astype(F32)


def open_kernel(
    grid, counts_ref, features_hbm, send_hbm, map_hbm, one_hbm,
    buf_ref, start_ref, place_ref, hot_ref, one_ref, features_ref, send_ref, map_ref, sems,
):
    pairs = ((features_hbm, features_ref), (send_hbm, send_ref), (map_hbm, map_ref), (one_hbm, one_ref))
    copies = [pltpu.make_async_copy(src, dst, sems.at[at]) for at, (src, dst) in enumerate(pairs)]
    for copy in copies:
        copy.start()
    for copy in copies[:3]:
        copy.wait()
    width = send_ref.shape[1]
    send = pad_to(send_ref[...].astype(F32), LANES, LANES).T
    lane = iota((width, LANES), 1).astype(F32)
    place = jnp.concatenate(
        [jnp.where(lane == send[:width, n : n + 1], 1.0, 0.0) for n in range(send_ref.shape[0])], axis=0
    ).astype(BF16)
    place_ref[...] = place
    valid = valid_lanes(counts_ref)
    start = features_ref[...].astype(F32) * valid
    start_ref[...] = start.astype(BF16)
    extra = jnp.where(iota((LANES - 96, LANES), 0) == 0, valid, 0.0)
    rows = nt(place, jnp.concatenate([start, extra], axis=0).astype(BF16))
    put_blocks(buf_ref, rows, grid, 1, width)
    sub = iota((hot_ref.shape[0], LANES), 0).astype(jnp.int16)
    columns = map_ref[...].astype(jnp.int16)
    one, zero = jnp.ones(sub.shape, BF16), jnp.zeros(sub.shape, BF16)
    for k in range(map_ref.shape[0]):
        hot_ref[:, k * LANES : (k + 1) * LANES] = jnp.where(sub == columns[k : k + 1, :], one, zero)
    copies[3].wait()


def gather(tables, hot_ref, taken_refs):
    channels = tables[0].shape[0]
    table = jnp.concatenate(tables, axis=0)
    offsets = hot_ref.shape[1] // LANES
    for first, last in ((0, offsets // 2), (offsets // 2, offsets)):
        taken = nn(table, hot_ref[:, first * LANES : last * LANES]).astype(BF16)
        for at, ref in enumerate(taken_refs):
            for k in range(first, last):
                ref[k * channels : (k + 1) * channels, :] = taken[
                    at * channels : (at + 1) * channels, (k - first) * LANES : (k - first + 1) * LANES
                ]


def gather_convolve(table, hot_ref, weight_ref, taken_ref):
    gather([table], hot_ref, [taken_ref])
    return tn(weight_ref[...], taken_ref[...])


def first_kernel(
    grid, counts_ref, buf_ref, start_ref, hot_ref, weight_ref, place_ref,
    out_buf_ref, hidden_ref, taken_ref, flag_ref,
):
    width = buf_ref.shape[1]
    channels = start_ref.shape[0]
    halo_rows = take_blocks(buf_ref, grid, -1, width)
    flag_ref[...] = jnp.broadcast_to(halo_rows[:, 96:97], (LANES, LANES))
    halo = halo_rows.T[:channels].astype(BF16)
    table = jnp.concatenate([start_ref[...], halo], axis=1)
    hidden = gather_convolve(table, hot_ref, weight_ref, taken_ref)
    hidden_ref[...] = hidden
    sums, centred, spread = centre(hidden, counts_ref)
    base = pack_rows(split3(sums) + split3(spread)[:2], counts_ref[0].astype(F32))
    out_buf_ref[...] = jnp.broadcast_to(base.astype(BF16)[None], out_buf_ref.shape)
    rows = nn(place_ref[...], centred.astype(BF16))
    put_blocks(out_buf_ref, rows, grid, 1, width, base)


def second_kernel(
    grid, counts_ref, buf_ref, hidden_ref, flag_ref, scale_ref, bias_ref, hot_ref, weight_ref,
    out_buf_ref, hidden_two_ref, taken_ref, norm_ref, slope_ref, halo_slope_ref, halo_cross_ref,
    const_ref, mean_ref,
):
    width = buf_ref.shape[1]
    channels = hidden_ref.shape[0]
    tiles = buf_ref[...].astype(F32)
    sums, spreads = unpack_rows(tiles, ((0, 3), (3, 5)))
    counts = tiles[:, 15, 96:97]
    total = jnp.sum(counts, axis=0, keepdims=True)
    means = sums / counts
    mean_ref[...] = means
    mean = jnp.sum(sums, axis=0, keepdims=True) / total
    apart = means - mean
    var = jnp.sum(spreads + counts * apart * apart, axis=0, keepdims=True) / total
    rstd = lax.rsqrt(var + EPS)
    scale = pad_to(scale_ref[...], 1, LANES)
    bias = pad_to(bias_ref[...], 1, LANES)
    total_row = jnp.broadcast_to(total, (1, LANES))
    mean_c, rstd_c, scale_c, bias_c = rows_to_cols([mean, rstd, scale, bias], channels)
    sub = iota((8, LANES), 0)
    const_ref[...] = jnp.where(sub == 0, scale * rstd, jnp.where(sub == 1, total_row, 0.0))

    valid = valid_lanes(counts_ref)
    normal = (hidden_ref[...] - mean_c) * rstd_c
    norm_ref[...] = normal
    linear = scale_c * normal + bias_c
    sig = sigmoid(linear)
    slope_ref[...] = sig * (1.0 + linear * (1.0 - sig)) * valid
    act = (linear * sig * valid).astype(BF16)

    place = here()
    lifted = []
    for n, (a, b) in enumerate(STEP_LIST):
        src, inside = neighbour(place, grid, (-a, -b))
        block = buf_ref[src, 0:width, :].astype(F32) + mean_ref[pl.ds(src, 1), :]
        lifted.append(jnp.where(inside, block, 0.0))
    lane = iota((LANES, LANES), 1)
    halo = jnp.where(lane < channels, jnp.concatenate(lifted, axis=0), 0.0)
    flag = flag_ref[...]
    halo_normal = (halo - mean) * rstd
    halo_linear = scale * halo_normal + bias
    halo_sig = sigmoid(halo_linear)
    halo_slope = halo_sig * (1.0 + halo_linear * (1.0 - halo_sig)) * flag
    halo_slope_ref[...] = halo_slope
    halo_cross_ref[...] = halo_slope * halo_normal
    halo_act = (halo_linear * halo_sig * flag).T[:channels].astype(BF16)

    table = jnp.concatenate([act, halo_act], axis=1)
    hidden = gather_convolve(table, hot_ref, weight_ref, taken_ref)
    hidden_two_ref[...] = hidden
    sums_two, _, spread_two = centre(hidden, counts_ref)
    stat = jnp.concatenate([sums_two, spread_two], axis=0)
    stat = jnp.where(iota((2, LANES), 1) < 96, stat, counts_ref[0].astype(F32))
    out_buf_ref[...] = jnp.broadcast_to(stat[None], out_buf_ref.shape)


def third_kernel(
    counts_ref, buf_ref, hidden_ref, start_ref, cotangent_ref, scale_ref, bias_ref,
    out_buf_ref, output_ref, norm_ref, grad_ref, const_ref,
):
    channels = hidden_ref.shape[0]
    sums = buf_ref[:, 0, :]
    spreads = buf_ref[:, 1, :]
    counts = sums[:, 96:97]
    total = jnp.sum(counts, axis=0, keepdims=True)
    mean = jnp.sum(sums, axis=0, keepdims=True) / total
    apart = sums / counts - mean
    var = jnp.sum(spreads + counts * apart * apart, axis=0, keepdims=True) / total
    rstd = lax.rsqrt(var + EPS)
    scale = pad_to(scale_ref[...], 1, LANES)
    bias = pad_to(bias_ref[...], 1, LANES)
    total_row = jnp.broadcast_to(total, (1, LANES))
    mean_c, rstd_c, scale_c, bias_c = rows_to_cols([mean, rstd, scale, bias], channels)
    sub = iota((8, LANES), 0)
    const_ref[...] = jnp.where(sub == 0, scale * rstd, jnp.where(sub == 1, total_row, 0.0))
    valid = valid_lanes(counts_ref)
    normal = (hidden_ref[...] - mean_c) * rstd_c
    norm_ref[...] = normal
    summed = scale_c * normal + bias_c + start_ref[...].astype(F32)
    sig = sigmoid(summed)
    output_ref[...] = (summed * sig * valid).astype(BF16)
    grad = cotangent_ref[...].astype(F32) * valid * (sig * (1.0 + summed * (1.0 - sig)))
    grad_ref[...] = grad
    rows = jnp.concatenate([lane_sums(grad * normal * valid), lane_sums(grad)], axis=0)
    out_buf_ref[...] = jnp.broadcast_to(rows[None], out_buf_ref.shape)


def scatter(grad, weight_ref, hot_ref):
    channels = grad.shape[0]
    terms = nn(weight_ref[...], grad).astype(BF16)
    offsets = hot_ref.shape[1] // LANES
    wide = jnp.concatenate([terms[k * channels : (k + 1) * channels] for k in range(offsets)], axis=1)
    halo = pad_to(nt(hot_ref[LANES : 2 * LANES, :], wide), LANES, LANES)
    return pad_to(nt(hot_ref[:LANES, :], wide), LANES, LANES), halo


def row_gradient(grad, normal, const, dgain, dbias, valid):
    channels = grad.shape[0]
    factor, part_bias, part_gain = rows_to_cols(
        [const[0:1], dbias / const[1:2], dgain / const[1:2]], channels
    )
    return (factor * (grad - (part_bias + normal * part_gain)) * valid).astype(BF16)


def fourth_kernel(
    grid, counts_ref, buf_ref, norm_ref, grad_ref, const_ref, weight_ref, hot_ref,
    norm_one_ref, slope_ref, halo_slope_ref, halo_cross_ref,
    out_buf_ref, grad_two_ref, table_ref, sums_ref,
):
    channels = norm_ref.shape[0]
    width = out_buf_ref.shape[1]
    valid = valid_lanes(counts_ref)
    both = halve(buf_ref[...], 1)[0]
    sums_ref[...] = both
    grad = row_gradient(grad_ref[...], norm_ref[...], const_ref[...], both[0:1], both[1:2], valid)
    grad_two_ref[...] = grad
    local_slope, local_cross = turn(slope_ref[...]), turn(slope_ref[...] * norm_one_ref[...])
    local, halo = scatter(grad, weight_ref, hot_ref)
    dgain = row_sum(local * local_cross + halo * halo_cross_ref[...])
    dbias = row_sum(local * local_slope + halo * halo_slope_ref[...])
    table_ref[...] = local.T[: norm_ref.shape[0]]
    base = pack_rows(split3(dgain)[:2] + split3(dbias)[:2], 0.0)
    out_buf_ref[...] = jnp.broadcast_to(base.astype(BF16)[None], out_buf_ref.shape)
    put_blocks(out_buf_ref, halo, grid, -1, width, base)


def packed_weight_grad(taken_ref, grad, put):
    channels = grad.shape[0]
    zero = jnp.zeros((channels, LANES), BF16)

    def taken(k):
        return taken_ref[k * channels : (k + 1) * channels, :]

    for part in range(3):
        upper = jnp.concatenate([grad, zero], axis=1)
        lower = jnp.concatenate([zero[:32], grad[32 * part : 32 * part + 32]], axis=1)
        right = jnp.concatenate([upper, lower], axis=0)
        left = jnp.concatenate(
            [
                jnp.concatenate([taken(3 * e + part) for e in range(6)], axis=0),
                jnp.concatenate([taken(21 + e) for e in range(6)], axis=0),
            ],
            axis=1,
        )
        result = nt(left, right)
        for e in range(6):
            put(3 * e + part, result[e * channels : (e + 1) * channels])
    last = nt(taken_ref[18 * channels : 21 * channels, :], pad_to(grad, LANES, LANES))
    for e in range(3):
        put(18 + e, last[e * channels : (e + 1) * channels])


def store_packed(taken_ref, grad, ref):
    channels = grad.shape[0]
    used = 21 * channels

    def put(block, value):
        ref[block * channels : (block + 1) * channels, :] = value.astype(ref.dtype)

    packed_weight_grad(taken_ref, grad, put)
    if ref.shape[0] > used:
        ref[used:, :] = jnp.zeros((ref.shape[0] - used, LANES), ref.dtype)


def fifth_kernel(
    grid, counts_ref, buf_ref, table_ref, place_ref, norm_ref, slope_ref, const_ref, sums_two_ref,
    taken_zero_ref, taken_act_ref, grad_two_ref,
    grad_one_ref, give_ref, sums_ref,
):
    width = buf_ref.shape[1]
    channels = norm_ref.shape[0]
    valid = valid_lanes(counts_ref)
    dgain, dbias = unpack_rows(
        halve(buf_ref[...].astype(F32), 1), ((0, 2), (2, 4))
    )
    two = sums_two_ref[...]
    sums_ref[...] = jnp.concatenate([dgain, dbias, two], axis=0)[:, :channels]
    arrived = take_blocks(buf_ref, grid, 1, width).astype(BF16)
    back = table_ref[...] + tn(arrived, place_ref[...])[:channels]
    grad = row_gradient(back * slope_ref[...], norm_ref[...], const_ref[...], dgain, dbias, valid)
    grad_one_ref[...] = grad
    core = lax.axis_index("gy") % 2

    @pl.when(core == 0)
    def _():
        store_packed(taken_act_ref, grad_two_ref[...], give_ref)

    @pl.when(core != 0)
    def _():
        store_packed(taken_zero_ref, grad, give_ref)


def back_kernel(
    grad_ref, weight_ref, hot_ref, taken_zero_ref, taken_act_ref, grad_two_ref, table_ref, halo_ref, keep_ref
):
    core = lax.axis_index("gy") % 2

    @pl.when(core == 0)
    def _():
        store_packed(taken_zero_ref, grad_ref[...], keep_ref)

    @pl.when(core != 0)
    def _():
        store_packed(taken_act_ref, grad_two_ref[...], keep_ref)

    local, halo = scatter(grad_ref[...], weight_ref, hot_ref)
    table_ref[...] = local.T[: grad_ref.shape[0]]
    halo_ref[...] = halo.astype(BF16)


def sixth_kernel(grid, width, halo_ref, keep_ref, got_ref, out_buf_ref):
    devices, rows = out_buf_ref.shape[0], out_buf_ref.shape[1] - width
    put_blocks(out_buf_ref, halo_ref[...], grid, -1, width)
    total = (keep_ref[...] + got_ref[...].astype(F32)).astype(BF16)
    out_buf_ref[:, width:, :] = total.reshape(devices, rows, LANES)


def seventh_kernel(grid, width, buf_ref, out_buf_ref, halo_ref):
    halo_ref[...] = take_blocks(buf_ref, grid, 1, width).astype(BF16)
    devices, rows = buf_ref.shape[0], buf_ref.shape[1] - width
    pieces = []
    for core in range(2):
        total = jnp.zeros((rows, LANES), F32)
        for d in range(core, devices, 2):
            total = total + buf_ref[d, width:, :].astype(F32)
        pieces.append(total.astype(BF16))
    for d in range(devices):
        out_buf_ref[d] = pieces[d % 2]


def unpack(src_ref, out_hbm, block_ref, sems):
    channels = block_ref.shape[1]
    lane = iota((channels, LANES), 1)
    copies = []

    def send(first, count):
        part = pl.ds(first, count)
        copies.append(pltpu.make_async_copy(block_ref.at[part], out_hbm.at[part], sems.at[len(copies)]))
        copies[-1].start()

    for e in range(7):
        extra = jnp.zeros((channels, LANES), F32)
        for part in range(3):
            block = 3 * e + part
            value = src_ref[block * channels : (block + 1) * channels, :].astype(F32)
            block_ref[block] = value[:, :channels]
            if e < 6:
                moved = pltpu.roll(value, 32 * (part + 1), 1)
                extra = jnp.where(lane // 32 == part, moved, extra)
        send(3 * e, 3)
        if e < 6:
            block_ref[21 + e] = extra[:, :channels]
            send(21 + e, 1)
    for copy in copies:
        copy.wait()


def own_kernel(
    counts_ref, own_ref, small_in, sums_in, halo_ref, table_ref, place_ref, grad_ref,
    one_hbm, two_hbm, small_hbm, sums_hbm, more_hbm, more_ref, block_ref, sems, small_sems,
):
    core = lax.axis_index("gy") % 2
    channels = table_ref.shape[0]
    back = table_ref[...] + tn(halo_ref[...], place_ref[...])[:channels]
    more_ref[...] = ((back + grad_ref[...]) * valid_lanes(counts_ref)).astype(BF16)
    pairs = ((small_in, small_hbm), (sums_in, sums_hbm), (more_ref, more_hbm))
    copies = [pltpu.make_async_copy(src, dst, small_sems.at[at]) for at, (src, dst) in enumerate(pairs)]
    for copy in copies:
        copy.start()

    @pl.when(core == 0)
    def _():
        unpack(own_ref, one_hbm, block_ref, sems)

    @pl.when(core != 0)
    def _():
        unpack(own_ref, two_hbm, block_ref, sems)

    for copy in copies:
        copy.wait()


def other_kernel(other_ref, one_in, two_in, one_hbm, two_hbm, block_ref, sems):
    core = lax.axis_index("gy") % 2

    @pl.when(core == 0)
    def _():
        unpack(other_ref, two_hbm, block_ref, sems)

    @pl.when(core != 0)
    def _():
        unpack(other_ref, one_hbm, block_ref, sems)


def call(kernel, outs, *args, smem=0, scratch=(), hbm=(), hbm_outs=(), aliases=None, carry=()):
    n_in, n_out = len(args), len(outs)
    aliases = dict(aliases or {})
    aliases.update({n_in + at: n_out + at for at in range(len(carry))})

    def space(at):
        if at >= n_in:
            return pl.ANY
        if at in hbm:
            return pltpu.HBM
        return pltpu.SMEM if at < smem else pltpu.VMEM

    def out_space(at):
        if at >= n_out:
            return pl.ANY
        return pltpu.HBM if at in hbm_outs else pltpu.VMEM

    def body(*refs):
        first_out = n_in + len(carry)
        kernel(*refs[:n_in], *refs[first_out : first_out + n_out], *refs[first_out + n_out + len(carry) :])

    args = [pltpu.with_memory_space_constraint(x, pltpu.HBM) if at in hbm else x for at, x in enumerate(args)]
    outs = list(outs) + [(x.shape, x.dtype) for x in carry]
    return pl.pallas_call(
        body,
        out_shape=tuple(jax.ShapeDtypeStruct(shape, dtype) for shape, dtype in outs),
        in_specs=[pl.BlockSpec(memory_space=space(at)) for at in range(n_in + len(carry))],
        out_specs=tuple(pl.BlockSpec(memory_space=out_space(at)) for at in range(len(outs))),
        scratch_shapes=list(scratch),
        input_output_aliases=aliases,
        compiler_params=pltpu.CompilerParams(vmem_limit_bytes=40 * 1024 * 1024),
    )(*args, *carry)


def to_all(x):
    return lax.all_to_all(x, AXES, 0, 0)


def swap_core(x):
    size = lax.axis_size("gy")
    return lax.ppermute(x, "gy", [(i, i ^ 1) for i in range(size)])


def on_device(
    features, kernel_map, send_rows, counts, weight_one, weight_two,
    first_norm_scale, first_norm_bias, second_norm_scale, second_norm_bias, cotangent,
):
    channels, rows = features.shape
    offsets = kernel_map.shape[0]
    width = send_rows.shape[1]
    grid = (lax.axis_size("gx"), lax.axis_size("gy"))
    devices = grid[0] * grid[1]
    flat = offsets * channels
    table = rows + 8 * width
    piece = -(-21 * channels // (devices * 16)) * 16
    packed = piece * devices
    full = (channels, rows)
    square = (LANES, LANES)
    one_flat = weight_one.reshape(flat, channels)
    two_flat = weight_two.reshape(flat, channels)
    scale_one, bias_one, scale_two, bias_two = [
        v.reshape(1, channels)
        for v in (first_norm_scale, first_norm_bias, second_norm_scale, second_norm_bias)
    ]

    taken = ((flat, LANES), BF16)
    buf, start, place, hot, one_near = call(
        functools.partial(open_kernel, grid),
        [
            ((devices, width, LANES), BF16), (full, BF16), (square, BF16),
            ((table, offsets * LANES), BF16), (one_flat.shape, BF16),
        ],
        counts, features, send_rows, kernel_map, one_flat, smem=1, hbm=(1, 2, 3, 4),
        scratch=[
            pltpu.VMEM(full, BF16), pltpu.VMEM(send_rows.shape, jnp.int32),
            pltpu.VMEM(kernel_map.shape, jnp.int32), pltpu.SemaphoreType.DMA((4,)),
        ],
    )
    buf = to_all(buf)
    buf, hidden_one, taken_zero, flag = call(
        functools.partial(first_kernel, grid),
        [((devices, width, LANES), BF16), (full, F32), taken, (square, F32)],
        counts, buf, start, hot, one_near, place, smem=1,
    )
    buf = to_all(buf)
    buf, hidden_two, taken_act, norm_one, slope_one, halo_slope, halo_cross, const_one, taken_zero = call(
        functools.partial(second_kernel, grid),
        [
            ((devices, 2, LANES), F32), (full, F32), taken, (full, F32), (full, F32),
            (square, F32), (square, F32), ((8, LANES), F32),
        ],
        counts, buf, hidden_one, flag, scale_one, bias_one, hot, two_flat,
        smem=1, scratch=[pltpu.VMEM((devices, LANES), F32)], carry=[taken_zero],
    )
    buf = to_all(buf)
    buf, output, norm_two, grad_sum, const_two, taken_zero, taken_act = call(
        third_kernel,
        [((devices, 2, LANES), F32), (full, BF16), (full, F32), (full, F32), ((8, LANES), F32)],
        counts, buf, hidden_two, start, cotangent, scale_two, bias_two, smem=1, carry=[taken_zero, taken_act],
    )
    buf = to_all(buf)
    buf, grad_two, table_two, sums_two, taken_zero, taken_act = call(
        functools.partial(fourth_kernel, grid),
        [((devices, width, LANES), BF16), (full, BF16), (full, F32), ((2, LANES), F32)],
        counts, buf, norm_two, grad_sum, const_two, two_flat, hot, norm_one, slope_one, halo_slope, halo_cross,
        smem=1, carry=[taken_zero, taken_act],
    )
    buf = to_all(buf)
    grad_one, give, grad_norms = call(
        functools.partial(fifth_kernel, grid),
        [(full, BF16), ((packed, LANES), BF16), ((4, channels), F32)],
        counts, buf, table_two, place, norm_one, slope_one, const_one, sums_two,
        taken_zero, taken_act, grad_two, smem=1,
    )
    got = swap_core(give)
    table_one, halo_one, keep = call(
        back_kernel,
        [(full, F32), (square, BF16), ((packed, LANES), F32)],
        grad_one, one_flat, hot, taken_zero, taken_act, grad_two,
    )
    (buf,) = call(
        functools.partial(sixth_kernel, grid, width),
        [((devices, width + piece, LANES), BF16)],
        halo_one, keep, got,
    )
    buf = to_all(buf)
    buf, halo = call(
        functools.partial(seventh_kernel, grid, width),
        [((devices, piece, LANES), BF16), (square, BF16)],
        buf,
    )
    own = to_all(buf).reshape(packed, LANES)
    other = swap_core(own)
    weights = [(weight_one.shape, F32), (weight_two.shape, F32)]
    blocks = [pltpu.VMEM(weight_one.shape, F32), pltpu.SemaphoreType.DMA((13,))]
    grad_weight_one, grad_weight_two, output, grad_norms, grad_features = call(
        own_kernel,
        weights + [(full, BF16), ((4, channels), F32), (full, BF16)],
        counts, own, output, grad_norms, halo, table_one, place, grad_sum, smem=1, hbm_outs=(0, 1, 2, 3, 4),
        scratch=[pltpu.VMEM(full, BF16)] + blocks + [pltpu.SemaphoreType.DMA((3,))],
    )
    grad_weight_one, grad_weight_two = call(
        other_kernel, weights, other, grad_weight_one, grad_weight_two,
        hbm=(1, 2), hbm_outs=(0, 1), scratch=blocks, aliases={1: 0, 2: 1},
    )
    return (output, grad_features, grad_weight_one, grad_weight_two, grad_norms)


def solution(mesh):
    return jax.shard_map(
        on_device,
        mesh=mesh,
        in_specs=(
            P(None, ("gx", "gy")),
            P(None, ("gx", "gy")),
            P(None, ("gx", "gy")),
            P(("gx", "gy")),
            P(),
            P(),
            P(),
            P(),
            P(),
            P(),
            P(None, ("gx", "gy")),
        ),
        out_specs=(P(None, ("gx", "gy")), P(None, ("gx", "gy")), P(), P(), P()),
        check_vma=False,
    )
```

```python
import functools

import jax
import jax.numpy as jnp
from jax import lax
from jax.experimental import pallas as pl
from jax.experimental.pallas import tpu as pltpu
from jax.sharding import PartitionSpec as P

EPS = 1e-05
STEP_LIST = ((1, 0), (-1, 0), (0, 1), (0, -1), (1, 1), (1, -1), (-1, 1), (-1, -1))
AXES = ("gx", "gy")
LANES = 128
F32 = jnp.float32
BF16 = jnp.bfloat16


def nn(a, b):
    return lax.dot_general(a, b, (((1,), (0,)), ((), ())), preferred_element_type=F32)


def nt(a, b):
    return lax.dot_general(a, b, (((1,), (1,)), ((), ())), preferred_element_type=F32)


def tn(a, b):
    return lax.dot_general(a, b, (((0,), (0,)), ((), ())), preferred_element_type=F32)


def iota(shape, dim):
    return lax.broadcasted_iota(jnp.int32, shape, dim)


def sigmoid(v):
    return 1.0 / (1.0 + jnp.exp(-v))


def neighbour(place, grid, step):
    i, j = place[0] + step[0], place[1] + step[1]
    inside = (i >= 0) & (i < grid[0]) & (j >= 0) & (j < grid[1])
    return jnp.where(inside, i * grid[1] + j, place[0] * grid[1] + place[1]), inside


def here():
    return lax.axis_index("gx"), lax.axis_index("gy")


def put_blocks(buf_ref, rows, grid, sign, width, base=None):
    place = here()
    for n, (a, b) in enumerate(STEP_LIST):
        dest, _ = neighbour(place, grid, (sign * a, sign * b))
        block = rows[n * width : (n + 1) * width]
        if base is not None:
            block = jnp.where(iota(block.shape, 1) < 96, block, base)
        buf_ref[dest, 0:width, :] = block.astype(BF16)


def take_blocks(buf_ref, grid, sign, width):
    place = here()
    blocks = []
    for a, b in STEP_LIST:
        src, inside = neighbour(place, grid, (sign * a, sign * b))
        block = buf_ref[src, 0:width, :].astype(F32)
        blocks.append(jnp.where(inside, block, 0.0))
    return jnp.concatenate(blocks, axis=0)


def pad_to(x, rows, lanes):
    if x.shape[1] < lanes:
        x = jnp.concatenate([x, jnp.zeros((x.shape[0], lanes - x.shape[1]), x.dtype)], axis=1)
    if x.shape[0] < rows:
        x = jnp.concatenate([x, jnp.zeros((rows - x.shape[0], lanes), x.dtype)], axis=0)
    return x


def turn(x):
    return pad_to(x, LANES, LANES).T


def lane_sums(x):
    return jnp.sum(turn(x), axis=0, keepdims=True)


def rows_to_cols(rows, channels):
    return [jnp.broadcast_to(row, (LANES, LANES)).T[:channels] for row in rows]


def centre(hidden, counts_ref):
    count = counts_ref[0].astype(F32)
    mask = (iota((LANES, LANES), 0) < counts_ref[0]).astype(F32)
    turned = turn(hidden)
    sums = jnp.sum(turned * mask, axis=0, keepdims=True)
    centred = (turned - sums / count) * mask
    return sums, centred, jnp.sum(centred * centred, axis=0, keepdims=True)


def split3(x):
    high = x.astype(BF16).astype(F32)
    mid = (x - high).astype(BF16).astype(F32)
    low = (x - high - mid).astype(BF16).astype(F32)
    return [high, mid, low]


def pack_rows(pieces, last):
    sub = iota((16, LANES), 0)
    lane = iota((16, LANES), 1)
    total = jnp.zeros((16, LANES), F32)
    for q, piece in enumerate(pieces):
        total = jnp.where(sub // 3 == q, piece, total)
    part = sub % 3
    moved = jnp.where(
        part == 0,
        pltpu.roll(total, 96, 1),
        jnp.where(part == 1, pltpu.roll(total, 64, 1), pltpu.roll(total, 32, 1)),
    )
    moved = jnp.where(sub == 15, last, moved)
    return jnp.where(lane >= 96, moved, 0.0)


def unpack_rows(tiles, groups):
    devices = tiles.shape[0]
    flat = tiles.reshape(devices * 16, LANES)
    sub = iota(tiles.shape, 1)
    lane = iota(tiles.shape, 2)
    part = sub % 3
    moved = [pltpu.roll(flat, 32 * (p + 1), 1).reshape(tiles.shape) for p in range(3)]
    value = jnp.where(part == 0, moved[0], jnp.where(part == 1, moved[1], moved[2]))
    value = jnp.where((lane // 32 == part) & (sub < 15), value, 0.0)
    results = []
    for low, high in groups:
        mask = (sub >= 3 * low) & (sub < 3 * high)
        results.append(jnp.sum(jnp.where(mask, value, 0.0), axis=1))
    return results


def valid_lanes(counts_ref, rows=1):
    return (iota((rows, LANES), 1) < counts_ref[0]).astype(F32)


def open_kernel(
    grid, counts_ref, features_hbm, send_hbm, map_hbm, one_hbm,
    buf_ref, start_ref, place_ref, hot_ref, one_ref, features_ref, send_ref, map_ref, sems,
):
    pairs = ((features_hbm, features_ref), (send_hbm, send_ref), (map_hbm, map_ref), (one_hbm, one_ref))
    copies = [pltpu.make_async_copy(src, dst, sems.at[at]) for at, (src, dst) in enumerate(pairs)]
    for copy in copies:
        copy.start()
    for copy in copies[:3]:
        copy.wait()
    width = send_ref.shape[1]
    send = pad_to(send_ref[...].astype(F32), LANES, LANES).T
    lane = iota((width, LANES), 1).astype(F32)
    place = jnp.concatenate(
        [jnp.where(lane == send[:width, n : n + 1], 1.0, 0.0) for n in range(send_ref.shape[0])], axis=0
    ).astype(BF16)
    place_ref[...] = place
    valid = valid_lanes(counts_ref)
    start = features_ref[...].astype(F32) * valid
    start_ref[...] = start.astype(BF16)
    extra = jnp.where(iota((LANES - 96, LANES), 0) == 0, valid, 0.0)
    rows = nt(place, jnp.concatenate([start, extra], axis=0).astype(BF16))
    put_blocks(buf_ref, rows, grid, 1, width)
    sub = iota((hot_ref.shape[0], LANES), 0).astype(jnp.int16)
    columns = map_ref[...].astype(jnp.int16)
    one, zero = jnp.ones(sub.shape, BF16), jnp.zeros(sub.shape, BF16)
    for k in range(map_ref.shape[0]):
        hot_ref[:, k * LANES : (k + 1) * LANES] = jnp.where(sub == columns[k : k + 1, :], one, zero)
    copies[3].wait()


def gather(tables, hot_ref, taken_refs):
    channels = tables[0].shape[0]
    taken = nn(jnp.concatenate(tables, axis=0), hot_ref[...]).astype(BF16)
    for at, ref in enumerate(taken_refs):
        for k in range(hot_ref.shape[1] // LANES):
            ref[k * channels : (k + 1) * channels, :] = taken[
                at * channels : (at + 1) * channels, k * LANES : (k + 1) * LANES
            ]


def gather_convolve(table, hot_ref, weight_ref, taken_ref):
    gather([table], hot_ref, [taken_ref])
    return tn(weight_ref[...], taken_ref[...])


def first_kernel(
    grid, counts_ref, buf_ref, start_ref, hot_ref, weight_ref, place_ref,
    out_buf_ref, hidden_ref, taken_ref, flag_ref,
):
    width = buf_ref.shape[1]
    channels = start_ref.shape[0]
    halo_rows = take_blocks(buf_ref, grid, -1, width)
    flag_ref[...] = jnp.broadcast_to(halo_rows[:, 96:97], (LANES, LANES))
    halo = halo_rows.T[:channels].astype(BF16)
    table = jnp.concatenate([start_ref[...], halo], axis=1)
    hidden = gather_convolve(table, hot_ref, weight_ref, taken_ref)
    hidden_ref[...] = hidden
    sums, centred, spread = centre(hidden, counts_ref)
    base = pack_rows(split3(sums) + split3(spread)[:2], counts_ref[0].astype(F32))
    out_buf_ref[...] = jnp.broadcast_to(base.astype(BF16)[None], out_buf_ref.shape)
    rows = nn(place_ref[...], centred.astype(BF16))
    put_blocks(out_buf_ref, rows, grid, 1, width, base)


def second_kernel(
    grid, counts_ref, buf_ref, hidden_ref, flag_ref, scale_ref, bias_ref, hot_ref, weight_ref,
    out_buf_ref, hidden_two_ref, taken_ref, norm_ref, slope_ref, halo_slope_ref, halo_cross_ref,
    const_ref, mean_ref,
):
    width = buf_ref.shape[1]
    channels = hidden_ref.shape[0]
    tiles = buf_ref[...].astype(F32)
    sums, spreads = unpack_rows(tiles, ((0, 3), (3, 5)))
    counts = tiles[:, 15, 96:97]
    total = jnp.sum(counts, axis=0, keepdims=True)
    means = sums / counts
    mean_ref[...] = means
    mean = jnp.sum(sums, axis=0, keepdims=True) / total
    apart = means - mean
    var = jnp.sum(spreads + counts * apart * apart, axis=0, keepdims=True) / total
    rstd = lax.rsqrt(var + EPS)
    scale = pad_to(scale_ref[...], 1, LANES)
    bias = pad_to(bias_ref[...], 1, LANES)
    total_row = jnp.broadcast_to(total, (1, LANES))
    mean_c, rstd_c, scale_c, bias_c = rows_to_cols([mean, rstd, scale, bias], channels)
    sub = iota((8, LANES), 0)
    const_ref[...] = jnp.where(sub == 0, scale * rstd, jnp.where(sub == 1, total_row, 0.0))

    valid = valid_lanes(counts_ref)
    normal = (hidden_ref[...] - mean_c) * rstd_c
    norm_ref[...] = normal
    linear = scale_c * normal + bias_c
    sig = sigmoid(linear)
    slope_ref[...] = sig * (1.0 + linear * (1.0 - sig)) * valid
    act = (linear * sig * valid).astype(BF16)

    place = here()
    lifted = []
    for n, (a, b) in enumerate(STEP_LIST):
        src, inside = neighbour(place, grid, (-a, -b))
        block = buf_ref[src, 0:width, :].astype(F32) + mean_ref[pl.ds(src, 1), :]
        lifted.append(jnp.where(inside, block, 0.0))
    lane = iota((LANES, LANES), 1)
    halo = jnp.where(lane < channels, jnp.concatenate(lifted, axis=0), 0.0)
    flag = flag_ref[...]
    halo_normal = (halo - mean) * rstd
    halo_linear = scale * halo_normal + bias
    halo_sig = sigmoid(halo_linear)
    halo_slope = halo_sig * (1.0 + halo_linear * (1.0 - halo_sig)) * flag
    halo_slope_ref[...] = halo_slope
    halo_cross_ref[...] = halo_slope * halo_normal
    halo_act = (halo_linear * halo_sig * flag).T[:channels].astype(BF16)

    table = jnp.concatenate([act, halo_act], axis=1)
    hidden = gather_convolve(table, hot_ref, weight_ref, taken_ref)
    hidden_two_ref[...] = hidden
    sums_two, _, spread_two = centre(hidden, counts_ref)
    stat = jnp.concatenate([sums_two, spread_two], axis=0)
    stat = jnp.where(iota((2, LANES), 1) < 96, stat, counts_ref[0].astype(F32))
    out_buf_ref[...] = jnp.broadcast_to(stat[None], out_buf_ref.shape)


def third_kernel(
    counts_ref, buf_ref, hidden_ref, start_ref, cotangent_ref, scale_ref, bias_ref,
    out_buf_ref, output_ref, norm_ref, grad_ref, const_ref,
):
    channels = hidden_ref.shape[0]
    sums = buf_ref[:, 0, :]
    spreads = buf_ref[:, 1, :]
    counts = sums[:, 96:97]
    total = jnp.sum(counts, axis=0, keepdims=True)
    mean = jnp.sum(sums, axis=0, keepdims=True) / total
    apart = sums / counts - mean
    var = jnp.sum(spreads + counts * apart * apart, axis=0, keepdims=True) / total
    rstd = lax.rsqrt(var + EPS)
    scale = pad_to(scale_ref[...], 1, LANES)
    bias = pad_to(bias_ref[...], 1, LANES)
    total_row = jnp.broadcast_to(total, (1, LANES))
    mean_c, rstd_c, scale_c, bias_c = rows_to_cols([mean, rstd, scale, bias], channels)
    sub = iota((8, LANES), 0)
    const_ref[...] = jnp.where(sub == 0, scale * rstd, jnp.where(sub == 1, total_row, 0.0))
    valid = valid_lanes(counts_ref)
    normal = (hidden_ref[...] - mean_c) * rstd_c
    norm_ref[...] = normal
    summed = scale_c * normal + bias_c + start_ref[...].astype(F32)
    sig = sigmoid(summed)
    output_ref[...] = (summed * sig * valid).astype(BF16)
    grad = cotangent_ref[...].astype(F32) * valid * (sig * (1.0 + summed * (1.0 - sig)))
    grad_ref[...] = grad
    rows = jnp.concatenate([lane_sums(grad * normal * valid), lane_sums(grad)], axis=0)
    out_buf_ref[...] = jnp.broadcast_to(rows[None], out_buf_ref.shape)


def scatter(grad, weight_ref, hot_ref):
    channels = grad.shape[0]
    terms = nn(weight_ref[...], grad).astype(BF16)
    offsets = hot_ref.shape[1] // LANES
    wide = jnp.concatenate([terms[k * channels : (k + 1) * channels] for k in range(offsets)], axis=1)
    halo = pad_to(nt(hot_ref[LANES : 2 * LANES, :], wide), LANES, LANES)
    return pad_to(nt(hot_ref[:LANES, :], wide), LANES, LANES), halo


def row_gradient(grad, normal, const, dgain, dbias, valid):
    channels = grad.shape[0]
    factor, part_bias, part_gain = rows_to_cols(
        [const[0:1], dbias / const[1:2], dgain / const[1:2]], channels
    )
    return (factor * (grad - (part_bias + normal * part_gain)) * valid).astype(BF16)


def fourth_kernel(
    grid, counts_ref, buf_ref, norm_ref, grad_ref, const_ref, weight_ref, hot_ref,
    norm_one_ref, slope_ref, halo_slope_ref, halo_cross_ref,
    out_buf_ref, grad_two_ref, table_ref, sums_ref,
):
    channels = norm_ref.shape[0]
    width = out_buf_ref.shape[1]
    valid = valid_lanes(counts_ref)
    both = jnp.sum(buf_ref[...], axis=0)
    sums_ref[...] = both
    grad = row_gradient(grad_ref[...], norm_ref[...], const_ref[...], both[0:1], both[1:2], valid)
    grad_two_ref[...] = grad
    local_slope, local_cross = turn(slope_ref[...]), turn(slope_ref[...] * norm_one_ref[...])
    local, halo = scatter(grad, weight_ref, hot_ref)
    dgain = jnp.sum(local * local_cross + halo * halo_cross_ref[...], axis=0, keepdims=True)
    dbias = jnp.sum(local * local_slope + halo * halo_slope_ref[...], axis=0, keepdims=True)
    table_ref[...] = local.T[: norm_ref.shape[0]]
    base = pack_rows(split3(dgain)[:2] + split3(dbias)[:2], 0.0)
    out_buf_ref[...] = jnp.broadcast_to(base.astype(BF16)[None], out_buf_ref.shape)
    put_blocks(out_buf_ref, halo, grid, -1, width, base)


def packed_weight_grad(taken_ref, grad, put):
    channels = grad.shape[0]
    zero = jnp.zeros((channels, LANES), BF16)

    def taken(k):
        return taken_ref[k * channels : (k + 1) * channels, :]

    for part in range(3):
        upper = jnp.concatenate([grad, zero], axis=1)
        lower = jnp.concatenate([zero[:32], grad[32 * part : 32 * part + 32]], axis=1)
        right = jnp.concatenate([upper, lower], axis=0)
        left = jnp.concatenate(
            [
                jnp.concatenate([taken(3 * e + part) for e in range(6)], axis=0),
                jnp.concatenate([taken(21 + e) for e in range(6)], axis=0),
            ],
            axis=1,
        )
        result = nt(left, right)
        for e in range(6):
            put(3 * e + part, result[e * channels : (e + 1) * channels])
    last = nt(taken_ref[18 * channels : 21 * channels, :], pad_to(grad, LANES, LANES))
    for e in range(3):
        put(18 + e, last[e * channels : (e + 1) * channels])


def store_packed(taken_ref, grad, ref):
    channels = grad.shape[0]
    used = 21 * channels

    def put(block, value):
        ref[block * channels : (block + 1) * channels, :] = value.astype(ref.dtype)

    packed_weight_grad(taken_ref, grad, put)
    if ref.shape[0] > used:
        ref[used:, :] = jnp.zeros((ref.shape[0] - used, LANES), ref.dtype)


def fifth_kernel(
    grid, counts_ref, buf_ref, table_ref, place_ref, norm_ref, slope_ref, const_ref, sums_two_ref,
    taken_zero_ref, taken_act_ref, grad_two_ref,
    grad_one_ref, give_ref, sums_ref,
):
    width = buf_ref.shape[1]
    channels = norm_ref.shape[0]
    valid = valid_lanes(counts_ref)
    dgain, dbias = unpack_rows(
        jnp.sum(buf_ref[...].astype(F32), axis=0, keepdims=True), ((0, 2), (2, 4))
    )
    two = sums_two_ref[...]
    sums_ref[...] = jnp.concatenate([dgain, dbias, two], axis=0)[:, :channels]
    arrived = take_blocks(buf_ref, grid, 1, width).astype(BF16)
    back = table_ref[...] + tn(arrived, place_ref[...])[:channels]
    grad = row_gradient(back * slope_ref[...], norm_ref[...], const_ref[...], dgain, dbias, valid)
    grad_one_ref[...] = grad
    core = lax.axis_index("gy") % 2

    @pl.when(core == 0)
    def _():
        store_packed(taken_act_ref, grad_two_ref[...], give_ref)

    @pl.when(core != 0)
    def _():
        store_packed(taken_zero_ref, grad, give_ref)


def back_kernel(
    grad_ref, weight_ref, hot_ref, taken_zero_ref, taken_act_ref, grad_two_ref, table_ref, halo_ref, keep_ref
):
    core = lax.axis_index("gy") % 2

    @pl.when(core == 0)
    def _():
        store_packed(taken_zero_ref, grad_ref[...], keep_ref)

    @pl.when(core != 0)
    def _():
        store_packed(taken_act_ref, grad_two_ref[...], keep_ref)

    local, halo = scatter(grad_ref[...], weight_ref, hot_ref)
    table_ref[...] = local.T[: grad_ref.shape[0]]
    halo_ref[...] = halo.astype(BF16)


def sixth_kernel(grid, width, halo_ref, keep_ref, got_ref, out_buf_ref):
    devices, rows = out_buf_ref.shape[0], out_buf_ref.shape[1] - width
    put_blocks(out_buf_ref, halo_ref[...], grid, -1, width)
    total = (keep_ref[...] + got_ref[...].astype(F32)).astype(BF16)
    out_buf_ref[:, width:, :] = total.reshape(devices, rows, LANES)


def seventh_kernel(grid, width, buf_ref, out_buf_ref, halo_ref):
    halo_ref[...] = take_blocks(buf_ref, grid, 1, width).astype(BF16)
    devices, rows = buf_ref.shape[0], buf_ref.shape[1] - width
    pieces = []
    for core in range(2):
        total = jnp.zeros((rows, LANES), F32)
        for d in range(core, devices, 2):
            total = total + buf_ref[d, width:, :].astype(F32)
        pieces.append(total.astype(BF16))
    for d in range(devices):
        out_buf_ref[d] = pieces[d % 2]


def unpack(src_ref, out_hbm, block_ref, sems):
    channels = block_ref.shape[1]
    lane = iota((channels, LANES), 1)
    copies = []

    def send(first, count):
        part = pl.ds(first, count)
        copies.append(pltpu.make_async_copy(block_ref.at[part], out_hbm.at[part], sems.at[len(copies)]))
        copies[-1].start()

    for e in range(7):
        extra = jnp.zeros((channels, LANES), F32)
        for part in range(3):
            block = 3 * e + part
            value = src_ref[block * channels : (block + 1) * channels, :].astype(F32)
            block_ref[block] = value[:, :channels]
            if e < 6:
                moved = pltpu.roll(value, 32 * (part + 1), 1)
                extra = jnp.where(lane // 32 == part, moved, extra)
        send(3 * e, 3)
        if e < 6:
            block_ref[21 + e] = extra[:, :channels]
            send(21 + e, 1)
    for copy in copies:
        copy.wait()


def own_kernel(
    counts_ref, own_ref, small_in, sums_in, halo_ref, table_ref, place_ref, grad_ref,
    one_hbm, two_hbm, small_hbm, sums_hbm, more_hbm, more_ref, block_ref, sems, small_sems,
):
    core = lax.axis_index("gy") % 2
    channels = table_ref.shape[0]
    back = table_ref[...] + tn(halo_ref[...], place_ref[...])[:channels]
    more_ref[...] = ((back + grad_ref[...]) * valid_lanes(counts_ref)).astype(BF16)
    pairs = ((small_in, small_hbm), (sums_in, sums_hbm), (more_ref, more_hbm))
    copies = [pltpu.make_async_copy(src, dst, small_sems.at[at]) for at, (src, dst) in enumerate(pairs)]
    for copy in copies:
        copy.start()

    @pl.when(core == 0)
    def _():
        unpack(own_ref, one_hbm, block_ref, sems)

    @pl.when(core != 0)
    def _():
        unpack(own_ref, two_hbm, block_ref, sems)

    for copy in copies:
        copy.wait()


def other_kernel(other_ref, one_in, two_in, one_hbm, two_hbm, block_ref, sems):
    core = lax.axis_index("gy") % 2

    @pl.when(core == 0)
    def _():
        unpack(other_ref, two_hbm, block_ref, sems)

    @pl.when(core != 0)
    def _():
        unpack(other_ref, one_hbm, block_ref, sems)


def call(kernel, outs, *args, smem=0, scratch=(), hbm=(), hbm_outs=(), aliases=None, carry=()):
    n_in, n_out = len(args), len(outs)
    aliases = dict(aliases or {})
    aliases.update({n_in + at: n_out + at for at in range(len(carry))})

    def space(at):
        if at >= n_in:
            return pl.ANY
        if at in hbm:
            return pltpu.HBM
        return pltpu.SMEM if at < smem else pltpu.VMEM

    def out_space(at):
        if at >= n_out:
            return pl.ANY
        return pltpu.HBM if at in hbm_outs else pltpu.VMEM

    def body(*refs):
        first_out = n_in + len(carry)
        kernel(*refs[:n_in], *refs[first_out : first_out + n_out], *refs[first_out + n_out + len(carry) :])

    args = [pltpu.with_memory_space_constraint(x, pltpu.HBM) if at in hbm else x for at, x in enumerate(args)]
    outs = list(outs) + [(x.shape, x.dtype) for x in carry]
    return pl.pallas_call(
        body,
        out_shape=tuple(jax.ShapeDtypeStruct(shape, dtype) for shape, dtype in outs),
        in_specs=[pl.BlockSpec(memory_space=space(at)) for at in range(n_in + len(carry))],
        out_specs=tuple(pl.BlockSpec(memory_space=out_space(at)) for at in range(len(outs))),
        scratch_shapes=list(scratch),
        input_output_aliases=aliases,
        compiler_params=pltpu.CompilerParams(vmem_limit_bytes=40 * 1024 * 1024),
    )(*args, *carry)


def to_all(x):
    return lax.all_to_all(x, AXES, 0, 0)


def swap_core(x):
    size = lax.axis_size("gy")
    return lax.ppermute(x, "gy", [(i, i ^ 1) for i in range(size)])


def on_device(
    features, kernel_map, send_rows, counts, weight_one, weight_two,
    first_norm_scale, first_norm_bias, second_norm_scale, second_norm_bias, cotangent,
):
    channels, rows = features.shape
    offsets = kernel_map.shape[0]
    width = send_rows.shape[1]
    grid = (lax.axis_size("gx"), lax.axis_size("gy"))
    devices = grid[0] * grid[1]
    flat = offsets * channels
    table = rows + 8 * width
    piece = -(-21 * channels // (devices * 16)) * 16
    packed = piece * devices
    full = (channels, rows)
    square = (LANES, LANES)
    one_flat = weight_one.reshape(flat, channels)
    two_flat = weight_two.reshape(flat, channels)
    scale_one, bias_one, scale_two, bias_two = [
        v.reshape(1, channels)
        for v in (first_norm_scale, first_norm_bias, second_norm_scale, second_norm_bias)
    ]

    taken = ((flat, LANES), BF16)
    buf, start, place, hot, one_near = call(
        functools.partial(open_kernel, grid),
        [
            ((devices, width, LANES), BF16), (full, BF16), (square, BF16),
            ((table, offsets * LANES), BF16), (one_flat.shape, BF16),
        ],
        counts, features, send_rows, kernel_map, one_flat, smem=1, hbm=(1, 2, 3, 4),
        scratch=[
            pltpu.VMEM(full, BF16), pltpu.VMEM(send_rows.shape, jnp.int32),
            pltpu.VMEM(kernel_map.shape, jnp.int32), pltpu.SemaphoreType.DMA((4,)),
        ],
    )
    buf = to_all(buf)
    buf, hidden_one, taken_zero, flag = call(
        functools.partial(first_kernel, grid),
        [((devices, width, LANES), BF16), (full, F32), taken, (square, F32)],
        counts, buf, start, hot, one_near, place, smem=1,
    )
    buf = to_all(buf)
    buf, hidden_two, taken_act, norm_one, slope_one, halo_slope, halo_cross, const_one, taken_zero = call(
        functools.partial(second_kernel, grid),
        [
            ((devices, 2, LANES), F32), (full, F32), taken, (full, F32), (full, F32),
            (square, F32), (square, F32), ((8, LANES), F32),
        ],
        counts, buf, hidden_one, flag, scale_one, bias_one, hot, two_flat,
        smem=1, scratch=[pltpu.VMEM((devices, LANES), F32)], carry=[taken_zero],
    )
    buf = to_all(buf)
    buf, output, norm_two, grad_sum, const_two, taken_zero, taken_act = call(
        third_kernel,
        [((devices, 2, LANES), F32), (full, BF16), (full, F32), (full, F32), ((8, LANES), F32)],
        counts, buf, hidden_two, start, cotangent, scale_two, bias_two, smem=1, carry=[taken_zero, taken_act],
    )
    buf = to_all(buf)
    buf, grad_two, table_two, sums_two, taken_zero, taken_act = call(
        functools.partial(fourth_kernel, grid),
        [((devices, width, LANES), BF16), (full, BF16), (full, F32), ((2, LANES), F32)],
        counts, buf, norm_two, grad_sum, const_two, two_flat, hot, norm_one, slope_one, halo_slope, halo_cross,
        smem=1, carry=[taken_zero, taken_act],
    )
    buf = to_all(buf)
    grad_one, give, grad_norms = call(
        functools.partial(fifth_kernel, grid),
        [(full, BF16), ((packed, LANES), BF16), ((4, channels), F32)],
        counts, buf, table_two, place, norm_one, slope_one, const_one, sums_two,
        taken_zero, taken_act, grad_two, smem=1,
    )
    got = swap_core(give)
    table_one, halo_one, keep = call(
        back_kernel,
        [(full, F32), (square, BF16), ((packed, LANES), F32)],
        grad_one, one_flat, hot, taken_zero, taken_act, grad_two,
    )
    (buf,) = call(
        functools.partial(sixth_kernel, grid, width),
        [((devices, width + piece, LANES), BF16)],
        halo_one, keep, got,
    )
    buf = to_all(buf)
    buf, halo = call(
        functools.partial(seventh_kernel, grid, width),
        [((devices, piece, LANES), BF16), (square, BF16)],
        buf,
    )
    own = to_all(buf).reshape(packed, LANES)
    other = swap_core(own)
    weights = [(weight_one.shape, F32), (weight_two.shape, F32)]
    blocks = [pltpu.VMEM(weight_one.shape, F32), pltpu.SemaphoreType.DMA((13,))]
    grad_weight_one, grad_weight_two, output, grad_norms, grad_features = call(
        own_kernel,
        weights + [(full, BF16), ((4, channels), F32), (full, BF16)],
        counts, own, output, grad_norms, halo, table_one, place, grad_sum, smem=1, hbm_outs=(0, 1, 2, 3, 4),
        scratch=[pltpu.VMEM(full, BF16)] + blocks + [pltpu.SemaphoreType.DMA((3,))],
    )
    grad_weight_one, grad_weight_two = call(
        other_kernel, weights, other, grad_weight_one, grad_weight_two,
        hbm=(1, 2), hbm_outs=(0, 1), scratch=blocks, aliases={1: 0, 2: 1},
    )
    return (output, grad_features, grad_weight_one, grad_weight_two, grad_norms)


def solution(mesh):
    return jax.shard_map(
        on_device,
        mesh=mesh,
        in_specs=(
            P(None, ("gx", "gy")),
            P(None, ("gx", "gy")),
            P(None, ("gx", "gy")),
            P(("gx", "gy")),
            P(),
            P(),
            P(),
            P(),
            P(),
            P(),
            P(None, ("gx", "gy")),
        ),
        out_specs=(P(None, ("gx", "gy")), P(None, ("gx", "gy")), P(), P(), P()),
        check_vma=False,
    )
```
